32 devices in a mesh: dp: 16 (over z, y, x), mp: 2 (over core).
Axes of the slice: x: 2, y: 2, z: 4, core: 2. Of those that a mesh axis runs over, the one named last changes fastest.
Arguments:
- tokens_in: bfloat16 [2048, 8192], P('dp', 'mp'), may hold values from -6 to 6
- gate_pre: bfloat16 [2048, 28672], P('dp', 'mp'), may hold values from -8 to 8
- up_pre: bfloat16 [2048, 28672], P('dp', 'mp'), may hold values from -6 to 6
- hidden_grad: bfloat16 [2048, 28672], P('dp', 'mp'), may hold values from -160 to 160
- out_grad: bfloat16 [2048, 8192], P('dp', 'mp'), may hold values from -160 to 160
- proj_model: bfloat16 [8192, 128], P('mp'), may hold values from -0.0625 to 0.0625
- proj_hidden: bfloat16 [28672, 128], P('mp'), may hold values from -0.03125 to 0.03125
Outputs:
- whitened: float32 [16, 128, 64], P('dp', 'mp')
The draws below stay inside these ranges and needn't reach their ends.
All inputs are finite; a program needn't handle non-finite values.
Results may differ from the reference program's by a relative error of at most 0.003.
Values sent between devices are 32-bit elements; how exact they have to be, the bound alone decides.
No kernel may reach another device: no remote copies, remote signals or barrier semaphores. Data moves between devices by JAX's collectives and lax.ppermute only.
A program may use at most 64 MiB of HBM per device.

```python
import math
import jax
import jax.numpy as jnp
from jax import lax

D = 8192
FF = 28672
RANK = 64
LEN = 128
EXAMPLES = 16
TOKENS = 2048


def example_scale(key, rising):
    scale_key = jax.random.fold_in(key, 11)
    position = jnp.arange(EXAMPLES, dtype=jnp.float32) / max(EXAMPLES - 1, 1)
    spread = jnp.exp(jax.random.uniform(scale_key, (EXAMPLES,), jnp.float32, 0.0, math.log(10.0)))
    return rising ** position * spread


def scaled_rows(key, columns_all):
    base_key = jax.random.fold_in(key, 3)
    base = jnp.clip(jax.random.normal(base_key, (TOKENS, columns_all), jnp.float32), -4.0, 4.0)
    rising = 3.0
    factors = jnp.repeat(example_scale(key, rising), LEN)
    return (base * factors[:, None]).astype(jnp.bfloat16)


def draw_hidden_grad(key, part):
    return scaled_rows(jax.random.fold_in(key, 101), FF)


def draw_out_grad(key, part):
    return scaled_rows(jax.random.fold_in(key, 202), D)


def block_levels(key, shape, split, smallest, high):
    def one(dim, parts):
        heights = jax.random.uniform(jax.random.fold_in(jax.random.fold_in(key, 6), dim), (parts,), jnp.float32, smallest / len(split), high / len(split))
        return jnp.repeat(jnp.exp(heights), shape[dim] // parts).reshape((-1,) + (1,) * (len(shape) - dim - 1))

    loudness = one(*split[0])
    for cut in split[1:]:
        loudness = loudness * one(*cut)
    return loudness


def centred(stream_key, shape, scale, most, split=(), kind=jnp.bfloat16):
    gain = block_levels(stream_key, shape, split, -0.22, 0.18) if split else 1.0
    values = jax.random.normal(stream_key, shape, jnp.float32) * scale * gain
    return jnp.minimum(jnp.maximum(values, -most), most).astype(kind)


def setup_inputs(seed: int = 0) -> dict:
    keys = jax.random.split(jax.random.key(seed), 8)
    return {
        "tokens_in": centred(keys[0], (TOKENS, D), 1.0, 6.0, ((0, 16), (1, 2))),
        "gate_pre": centred(keys[1], (TOKENS, FF), 1.5, 8.0, ((0, 16), (1, 2))),
        "up_pre": centred(keys[2], (TOKENS, FF), 1.0, 6.0, ((0, 16), (1, 2))),
        "hidden_grad": draw_hidden_grad(jax.random.fold_in(keys[7], 71), 0),
        "out_grad": draw_out_grad(jax.random.fold_in(keys[7], 71), 0),
        "proj_model": centred(keys[5], (D, 2 * RANK), D ** -0.5, 0.0625, ((0, 2),)),
        "proj_hidden": centred(keys[6], (FF, 2 * RANK), FF ** -0.5, 0.03125, ((0, 2),)),
    }


highest = lax.Precision.HIGHEST

def gradient_blocks(projected):
    columns_each = projected.shape[-1] // 4
    input_side = projected[..., :columns_each]
    output_side = projected[..., columns_each:2 * columns_each]
    upward = projected[..., 2 * columns_each:3 * columns_each]
    hidden_side = projected[..., 3 * columns_each:]
    up_block = jnp.einsum('elr,els->ers', input_side, upward, precision=highest)
    down_block = jnp.einsum('elr,els->ers', hidden_side, output_side, precision=highest)
    return jnp.concatenate([up_block, down_block], axis=1)

def reference(tokens_in, gate_pre, up_pre, hidden_grad, out_grad, proj_model, proj_hidden):

    def project(pieces):
        token_rows, gate_rows, up_rows, grad_rows, outer_rows = pieces
        gate_act = jax.nn.silu(gate_rows.astype(jnp.float32))
        up_grad = (grad_rows.astype(jnp.float32) * gate_act).astype(jnp.bfloat16)
        hidden = (gate_act * up_rows.astype(jnp.float32)).astype(jnp.bfloat16)
        projected = jnp.concatenate([jnp.dot(token_rows.astype(jnp.float32), proj_model[:, :RANK].astype(jnp.float32), preferred_element_type=jnp.float32), jnp.dot(outer_rows.astype(jnp.float32), proj_model[:, RANK:].astype(jnp.float32), preferred_element_type=jnp.float32), jnp.dot(up_grad.astype(jnp.float32), proj_hidden[:, :RANK].astype(jnp.float32), preferred_element_type=jnp.float32), jnp.dot(hidden.astype(jnp.float32), proj_hidden[:, RANK:].astype(jnp.float32), preferred_element_type=jnp.float32)], axis=1)
        return gradient_blocks(projected[None])[0]
    blocks = lax.map(project, (tokens_in.reshape(EXAMPLES, LEN, D), gate_pre.reshape(EXAMPLES, LEN, FF), up_pre.reshape(EXAMPLES, LEN, FF), hidden_grad.reshape(EXAMPLES, LEN, FF), out_grad.reshape(EXAMPLES, LEN, D)))
    flat_rows = blocks.reshape(EXAMPLES * 2 * RANK, RANK)
    gram = jnp.dot(flat_rows.T.astype(jnp.float32), flat_rows.astype(jnp.float32), precision=highest, preferred_element_type=jnp.float32)
    lower = jnp.linalg.cholesky(gram)
    solved = jax.scipy.linalg.solve_triangular(lower, flat_rows.T, lower=True)
    factor = math.sqrt(EXAMPLES * 2 * RANK)
    return (solved.T * factor).reshape(EXAMPLES, 2 * RANK, RANK)
```

```python
import functools
import math

import jax
import jax.numpy as jnp
from jax import lax
from jax.experimental import pallas as pl
from jax.experimental.pallas import tpu as pltpu
from jax.sharding import PartitionSpec as P

RANK = 64
LEN = 128
WIDE = 2 * RANK

highest = lax.Precision.HIGHEST
whole_vmem = pl.BlockSpec(memory_space=pltpu.VMEM)
left_in_hbm = pl.BlockSpec(memory_space=pl.ANY)


def pieces_of(width, most):
    count = most
    while width % (count * 128):
        count //= 2
    return count, width // count


def lanes_of(shape):
    return lax.broadcasted_iota(jnp.int32, shape, len(shape) - 1)


def project_kernel(
    shards, place, gate, up, grad, proj_hidden, tokens, outer, proj_model, *rest
):
    outs = rest[:shards]
    gate_v, up_v, grad_v, hidden_w, tokens_v, outer_v, model_w, sems, model_sems = rest[shards:]
    rows, hidden_width = gate.shape
    model_width = tokens.shape[1]
    hidden_count, hidden_each = pieces_of(hidden_width, 8)
    model_count, model_each = pieces_of(model_width, 4)

    hidden_copies = []
    for piece in range(hidden_count):
        cut = pl.ds(piece * hidden_each, hidden_each)
        hidden_copies.append(
            [
                pltpu.make_async_copy(gate.at[:, cut], gate_v.at[:, cut], sems.at[piece, 0]),
                pltpu.make_async_copy(grad.at[:, cut], grad_v.at[:, cut], sems.at[piece, 1]),
                pltpu.make_async_copy(up.at[:, cut], up_v.at[:, cut], sems.at[piece, 2]),
                pltpu.make_async_copy(
                    proj_hidden.at[cut, :], hidden_w.at[cut, :], sems.at[piece, 3]
                ),
            ]
        )
    model_copies = []
    for piece in range(model_count):
        cut = pl.ds(piece * model_each, model_each)
        model_copies.append(
            [
                pltpu.make_async_copy(
                    tokens.at[:, cut], tokens_v.at[:, cut], model_sems.at[piece, 0]
                ),
                pltpu.make_async_copy(
                    outer.at[:, cut], outer_v.at[:, cut], model_sems.at[piece, 1]
                ),
                pltpu.make_async_copy(
                    proj_model.at[cut, :], model_w.at[cut, :], model_sems.at[piece, 2]
                ),
            ]
        )
    for group in hidden_copies + model_copies:
        for copy in group:
            copy.start()

    step = 256 if hidden_each % 256 == 0 else 128
    hidden_sum = jnp.zeros((2 * rows, WIDE), jnp.float32)
    for piece in range(hidden_count):
        for copy in hidden_copies[piece]:
            copy.wait()
        for first in range(piece * hidden_each, (piece + 1) * hidden_each, step):
            cut = slice(first, first + step)
            half = gate_v[:, cut].astype(jnp.float32) * 0.5
            act = half + half * jnp.tanh(half)
            up_grad = (grad_v[:, cut].astype(jnp.float32) * act).astype(jnp.bfloat16)
            hidden = (act * up_v[:, cut].astype(jnp.float32)).astype(jnp.bfloat16)
            both = jnp.concatenate([up_grad, hidden], axis=0)
            hidden_sum += jnp.dot(both, hidden_w[cut, :], preferred_element_type=jnp.float32)
    model_sum = jnp.zeros((2 * rows, WIDE), jnp.float32)
    for piece in range(model_count):
        for copy in model_copies[piece]:
            copy.wait()
        cut = slice(piece * model_each, (piece + 1) * model_each)
        both = jnp.concatenate([tokens_v[:, cut], outer_v[:, cut]], axis=0)
        model_sum += jnp.dot(both, model_w[cut, :], preferred_element_type=jnp.float32)

    upward = hidden_sum[:rows]
    hidden_side = hidden_sum[rows:]
    input_side = model_sum[:rows]
    output_side = model_sum[rows:]
    lane = lanes_of((rows, WIDE))
    rows_each = WIDE // shards
    me = place[0]
    for shard in range(shards):
        at = shard * rows_each
        if at < RANK:
            left = input_side if at == 0 else pltpu.roll(input_side, WIDE - at, 1)
            right = pltpu.roll(upward, RANK, 1)
        else:
            left = pltpu.roll(hidden_side, WIDE - at, 1)
            right = output_side
        if rows_each < RANK:
            left = jnp.where(lane < rows_each, left, 0.0)
        block = jnp.where(lane < RANK, left, right)
        for away in range(shards):

            @pl.when(me == (shard - away) % shards)
            def _(block=block, away=away):
                outs[away][...] = block


def project(place, gate_pre, up_pre, hidden_grad, proj_hidden, tokens_in, out_grad, proj_model):
    shards = lax.axis_size("mp")
    rows, hidden_width = gate_pre.shape
    model_width = tokens_in.shape[1]
    hidden_count, _ = pieces_of(hidden_width, 8)
    model_count, _ = pieces_of(model_width, 4)
    held = jnp.bfloat16
    return pl.pallas_call(
        functools.partial(project_kernel, shards),
        out_shape=[jax.ShapeDtypeStruct((rows, WIDE), jnp.float32)] * shards,
        in_specs=[pl.BlockSpec(memory_space=pltpu.SMEM)] + [left_in_hbm] * 7,
        out_specs=[whole_vmem] * shards,
        scratch_shapes=[
            pltpu.VMEM((rows, hidden_width), held),
            pltpu.VMEM((rows, hidden_width), held),
            pltpu.VMEM((rows, hidden_width), held),
            pltpu.VMEM((hidden_width, WIDE), held),
            pltpu.VMEM((rows, model_width), held),
            pltpu.VMEM((rows, model_width), held),
            pltpu.VMEM((model_width, WIDE), held),
            pltpu.SemaphoreType.DMA((hidden_count, 4)),
            pltpu.SemaphoreType.DMA((model_count, 3)),
        ],
        compiler_params=pltpu.CompilerParams(vmem_limit_bytes=40 * 2**20),
        name="project",
    )(place, gate_pre, up_pre, hidden_grad, proj_hidden, tokens_in, out_grad, proj_model)


def gram_kernel(count, *refs):
    parts, (rows_ref, gram_ref) = refs[:count], refs[count:]
    total = parts[0][...]
    for part in parts[1:]:
        total += part[...]
    row = lax.broadcasted_iota(jnp.int32, (WIDE, WIDE), 0)
    lane = lanes_of((WIDE, WIDE))
    gram = jnp.zeros((RANK, WIDE), jnp.float32)
    for example in range(total.shape[0] // LEN):
        sides = total[example * LEN : (example + 1) * LEN]
        crossed = jnp.dot(
            sides.T, sides, precision=highest, preferred_element_type=jnp.float32
        )
        mixed = jnp.where((row < RANK) != (lane < RANK), crossed, 0.0)
        mine = mixed[RANK:]
        rows_ref[example] = mine
        gram += jnp.dot(mine, mixed, precision=highest, preferred_element_type=jnp.float32)
    top, bottom = gram[: RANK // 2], gram[RANK // 2 :]
    gram_ref[...] = jnp.where(
        lanes_of(top.shape) < RANK, pltpu.roll(top, RANK, 1), bottom
    )


def gram_of(parts):
    examples = parts[0].shape[0] // LEN
    return pl.pallas_call(
        functools.partial(gram_kernel, len(parts)),
        out_shape=[
            jax.ShapeDtypeStruct((examples, RANK, WIDE), jnp.float32),
            jax.ShapeDtypeStruct((RANK // 2, WIDE), jnp.float32),
        ],
        in_specs=[whole_vmem] * len(parts),
        out_specs=[whole_vmem] * 2,
        name="gram",
    )(*parts)


def whiten_kernel(factor, rows_each, rows_ref, gram_ref, out_ref):
    packed = gram_ref[...]
    gram = jnp.concatenate([pltpu.roll(packed, RANK, 1), packed], axis=0)
    height = 8
    lane = lanes_of((height, WIDE))
    sub = lax.broadcasted_iota(jnp.int32, (height, WIDE), 0)
    for example in range(rows_ref.shape[0]):
        joined = jnp.where(lanes_of((RANK, WIDE)) < RANK, rows_ref[example], gram)
        state = [joined[at : at + height] for at in range(0, RANK, height)]
        for pivot in range(RANK):
            held, inner = divmod(pivot, height)
            spot = RANK + pivot
            row = state[held][inner : inner + 1, :]
            scaled = row * (1.0 / row[:, spot : spot + 1])
            for other in range(held, RANK // height):
                column = state[other][:, spot : spot + 1]
                taken = column * scaled
                if other == held:
                    taken = jnp.where(sub > inner, taken, 0.0)
                state[other] = state[other] - taken
        done = []
        for held, block in enumerate(state):
            diagonal = jnp.sum(
                jnp.where(lane == RANK + held * height + sub, block, 0.0), axis=1, keepdims=True
            )
            done.append(block * (lax.rsqrt(diagonal) * factor))
        solved = jnp.concatenate(done, axis=0).T
        out_ref[example] = solved[:rows_each, :]


def whiten(rows, gram, rows_each, factor):
    return pl.pallas_call(
        functools.partial(whiten_kernel, factor, rows_each),
        out_shape=jax.ShapeDtypeStruct((rows.shape[0], rows_each, RANK), jnp.float32),
        in_specs=[whole_vmem] * 2,
        out_specs=whole_vmem,
        name="whiten",
    )(rows, gram)


def summed_everywhere(value):
    axes = ("dp", "mp")
    devices = lax.axis_size("dp") * lax.axis_size("mp")
    pieces = value.reshape(devices, -1)
    received = lax.all_to_all(pieces, axes, 0, 0, tiled=True)
    total = jnp.sum(received, axis=0, keepdims=True)
    gathered = lax.all_to_all(jnp.broadcast_to(total, pieces.shape), axes, 0, 0, tiled=True)
    return gathered.reshape(value.shape)


def shards(tokens_in, gate_pre, up_pre, hidden_grad, out_grad, proj_model, proj_hidden):
    model_shards = lax.axis_size("mp")
    rows_each = WIDE // model_shards
    local_examples = tokens_in.shape[0] // LEN
    place = lax.axis_index("mp").astype(jnp.int32).reshape(1)
    parts = project(
        place, gate_pre, up_pre, hidden_grad, proj_hidden, tokens_in, out_grad, proj_model
    )
    received = [parts[0]]
    for away in range(1, model_shards):
        pairs = [(source, (source + away) % model_shards) for source in range(model_shards)]
        received.append(lax.ppermute(parts[away], "mp", pairs))
    rows, gram = gram_of(received)
    gram = summed_everywhere(gram)
    factor = math.sqrt(local_examples * lax.axis_size("dp") * 2 * RANK)
    return whiten(rows, gram, rows_each, factor)


def solution(mesh):
    in_specs = (
        P("dp", "mp"),
        P("dp", "mp"),
        P("dp", "mp"),
        P("dp", "mp"),
        P("dp", "mp"),
        P("mp", None),
        P("mp", None),
    )
    out_specs = P("dp", "mp", None)
    return jax.shard_map(shards, mesh=mesh, in_specs=in_specs, out_specs=out_specs, check_vma=False)
```

```python
import functools
import math

import jax
import jax.numpy as jnp
from jax import lax
from jax.experimental import pallas as pl
from jax.experimental.pallas import tpu as pltpu
from jax.sharding import PartitionSpec as P

RANK = 64
LEN = 128
WIDE = 2 * RANK

highest = lax.Precision.HIGHEST
whole_vmem = pl.BlockSpec(memory_space=pltpu.VMEM)
left_in_hbm = pl.BlockSpec(memory_space=pl.ANY)
small = pltpu.CompilerParams(vmem_limit_bytes=8 * 2**20)


def pieces_of(width, most):
    count = most
    while width % (count * 128):
        count //= 2
    return count, width // count


def lanes_of(shape):
    return lax.broadcasted_iota(jnp.int32, shape, len(shape) - 1)


def project_kernel(gate, up, grad, proj_hidden, tokens, outer, proj_model, out, *rest):
    gate_v, up_v, grad_v, hidden_w, tokens_v, outer_v, model_w, sems, model_sems = rest
    rows, hidden_width = gate.shape
    model_width = tokens.shape[1]
    hidden_count, hidden_each = pieces_of(hidden_width, 8)
    model_count, model_each = pieces_of(model_width, 4)

    hidden_copies = []
    for piece in range(hidden_count):
        cut = pl.ds(piece * hidden_each, hidden_each)
        hidden_copies.append(
            [
                pltpu.make_async_copy(gate.at[:, cut], gate_v.at[:, cut], sems.at[piece, 0]),
                pltpu.make_async_copy(grad.at[:, cut], grad_v.at[:, cut], sems.at[piece, 1]),
                pltpu.make_async_copy(up.at[:, cut], up_v.at[:, cut], sems.at[piece, 2]),
                pltpu.make_async_copy(
                    proj_hidden.at[cut, :], hidden_w.at[cut, :], sems.at[piece, 3]
                ),
            ]
        )
    model_copies = []
    for piece in range(model_count):
        cut = pl.ds(piece * model_each, model_each)
        model_copies.append(
            [
                pltpu.make_async_copy(
                    tokens.at[:, cut], tokens_v.at[:, cut], model_sems.at[piece, 0]
                ),
                pltpu.make_async_copy(
                    outer.at[:, cut], outer_v.at[:, cut], model_sems.at[piece, 1]
                ),
                pltpu.make_async_copy(
                    proj_model.at[cut, :], model_w.at[cut, :], model_sems.at[piece, 2]
                ),
            ]
        )
    for group in hidden_copies + model_copies:
        for copy in group:
            copy.start()

    step = 256 if hidden_each % 256 == 0 else 128
    hidden_sum = jnp.zeros((2 * rows, WIDE), jnp.float32)
    for piece in range(hidden_count):
        for copy in hidden_copies[piece]:
            copy.wait()
        for first in range(piece * hidden_each, (piece + 1) * hidden_each, step):
            cut = slice(first, first + step)
            half = gate_v[:, cut].astype(jnp.float32) * 0.5
            act = half + half * jnp.tanh(half)
            up_grad = (grad_v[:, cut].astype(jnp.float32) * act).astype(jnp.bfloat16)
            hidden = (act * up_v[:, cut].astype(jnp.float32)).astype(jnp.bfloat16)
            both = jnp.concatenate([up_grad, hidden], axis=0)
            hidden_sum += jnp.dot(both, hidden_w[cut, :], preferred_element_type=jnp.float32)
    model_sum = jnp.zeros((2 * rows, WIDE), jnp.float32)
    for piece in range(model_count):
        for copy in model_copies[piece]:
            copy.wait()
        cut = slice(piece * model_each, (piece + 1) * model_each)
        both = jnp.concatenate([tokens_v[:, cut], outer_v[:, cut]], axis=0)
        model_sum += jnp.dot(both, model_w[cut, :], preferred_element_type=jnp.float32)

    low = lanes_of((rows, WIDE)) < RANK
    upward = pltpu.roll(hidden_sum[:rows], RANK, 1)
    hidden_side = pltpu.roll(hidden_sum[rows:], RANK, 1)
    out[:, :WIDE] = jnp.where(low, model_sum[:rows], upward)
    out[:, WIDE:] = jnp.where(low, hidden_side, model_sum[rows:])


def project(gate_pre, up_pre, hidden_grad, proj_hidden, tokens_in, out_grad, proj_model):
    rows, hidden_width = gate_pre.shape
    model_width = tokens_in.shape[1]
    hidden_count, _ = pieces_of(hidden_width, 8)
    model_count, _ = pieces_of(model_width, 4)
    held = jnp.bfloat16
    return pl.pallas_call(
        project_kernel,
        out_shape=jax.ShapeDtypeStruct((rows, 2 * WIDE), jnp.float32),
        in_specs=[left_in_hbm] * 7,
        out_specs=whole_vmem,
        scratch_shapes=[
            pltpu.VMEM((rows, hidden_width), held),
            pltpu.VMEM((rows, hidden_width), held),
            pltpu.VMEM((rows, hidden_width), held),
            pltpu.VMEM((hidden_width, WIDE), held),
            pltpu.VMEM((rows, model_width), held),
            pltpu.VMEM((rows, model_width), held),
            pltpu.VMEM((model_width, WIDE), held),
            pltpu.SemaphoreType.DMA((hidden_count, 4)),
            pltpu.SemaphoreType.DMA((model_count, 3)),
        ],
        compiler_params=pltpu.CompilerParams(vmem_limit_bytes=60 * 2**20),
        name="project",
    )(gate_pre, up_pre, hidden_grad, proj_hidden, tokens_in, out_grad, proj_model)


def gram_kernel(rows_each, count, *refs):
    place, parts, (rows_ref, gram_ref) = refs[0], refs[1 : 1 + count], refs[1 + count :]
    total = parts[0][...]
    for part in parts[1:]:
        total += part[...]
    row = lax.broadcasted_iota(jnp.int32, (WIDE, WIDE), 0)
    lane = lanes_of((WIDE, WIDE))
    low = lanes_of((RANK, WIDE)) < RANK
    gram = jnp.zeros((RANK, WIDE), jnp.float32)
    shift = lax.rem(WIDE - place[0] * rows_each, WIDE)
    for example in range(total.shape[0] // LEN):
        mixed = []
        for at in (0, WIDE):
            sides = total[example * LEN : (example + 1) * LEN, at : at + WIDE]
            crossed = jnp.dot(
                sides.T, sides, precision=highest, preferred_element_type=jnp.float32
            )
            mixed.append(jnp.where((row < RANK) != (lane < RANK), crossed, 0.0))
        up_block, down_block = mixed[0][RANK:], mixed[1][RANK:]
        across = jnp.where(low, up_block, pltpu.roll(down_block, RANK, 1))
        rows_ref[example] = jnp.where(low, pltpu.roll(across, shift, 1), 0.0)
        gram += jnp.dot(
            jnp.concatenate([up_block, down_block], axis=1),
            jnp.concatenate(mixed, axis=0),
            precision=highest,
            preferred_element_type=jnp.float32,
        )
    top, bottom = gram[: RANK // 2], gram[RANK // 2 :]
    gram_ref[...] = jnp.where(
        lanes_of(top.shape) < RANK, pltpu.roll(top, RANK, 1), bottom
    )


def gram_of(place, parts, rows_each):
    examples = parts[0].shape[0] // LEN
    return pl.pallas_call(
        functools.partial(gram_kernel, rows_each, len(parts)),
        out_shape=[
            jax.ShapeDtypeStruct((examples, RANK, WIDE), jnp.float32),
            jax.ShapeDtypeStruct((RANK // 2, WIDE), jnp.float32),
        ],
        in_specs=[pl.BlockSpec(memory_space=pltpu.SMEM)] + [whole_vmem] * len(parts),
        out_specs=[whole_vmem] * 2,
        compiler_params=small,
        name="gram",
    )(place, *parts)


def eliminated(state):
    height = 8
    blocks = len(state)
    state = list(state)
    sub = lax.broadcasted_iota(jnp.int32, state[0].shape, 0)

    def across(block, at):
        return jnp.broadcast_to(block[:, at : at + 1], block.shape)

    def down(block, at):
        return jnp.broadcast_to(block[at : at + 1, :], block.shape)

    done = []
    for held in range(blocks):
        base = RANK + held * height
        own = state[held]
        columns = [across(own, base + k) for k in range(height)]
        corner = {
            (k, m): down(columns[m], k) for k in range(height) for m in range(k, height)
        }
        rows = [down(own, k) for k in range(height)]
        ahead = None
        if held + 1 < blocks:
            ahead = [across(state[held + 1], base + k) for k in range(height)]
        factors = {}
        inverses = []
        for k in range(height):
            inverse = 1.0 / corner[k, k]
            inverses.append(inverse)
            for m in range(k + 1, height):
                factor = corner[k, m] * inverse
                factors[k, m] = factor
                for n in range(m, height):
                    corner[m, n] = corner[m, n] - factor * corner[k, n]
                rows[m] = rows[m] - factor * rows[k]
                if ahead is not None:
                    ahead[m] = ahead[m] - factor * ahead[k]
        if ahead is not None:
            taken = [ahead[k] * (inverses[k] * rows[k]) for k in range(height)]
            while len(taken) > 1:
                taken = [left + right for left, right in zip(taken[::2], taken[1::2])]
            state[held + 1] = state[held + 1] - taken[0]
        if held + 2 < blocks:
            back = [inverses[k] * rows[k] for k in range(height)]
            for k in reversed(range(height)):
                for m in range(k):
                    back[m] = back[m] - factors[m, k] * back[k]
            for other in range(held + 2, blocks):
                for k in range(height):
                    state[other] = state[other] - across(state[other], base + k) * back[k]
        block = rows[0] * lax.rsqrt(corner[0, 0])
        for k in range(1, height):
            block = jnp.where(sub == k, rows[k] * lax.rsqrt(corner[k, k]), block)
        done.append(block)
    return done


def whiten_kernel(factor, rows_each, rows_ref, gram_ref, out_ref):
    packed = gram_ref[...]
    gram = jnp.concatenate([pltpu.roll(packed, RANK, 1), packed], axis=0)
    low = lanes_of((RANK, WIDE)) < RANK
    for example in range(rows_ref.shape[0]):
        joined = jnp.where(low, rows_ref[example], gram)
        done = eliminated([joined[at : at + 8] for at in range(0, RANK, 8)])
        solved = (jnp.concatenate(done, axis=0) * factor).T
        out_ref[example] = solved[:rows_each, :]


def whiten(rows, gram, rows_each, factor):
    return pl.pallas_call(
        functools.partial(whiten_kernel, factor, rows_each),
        out_shape=jax.ShapeDtypeStruct((rows.shape[0], rows_each, RANK), jnp.float32),
        in_specs=[whole_vmem] * 2,
        out_specs=whole_vmem,
        compiler_params=small,
        name="whiten",
    )(rows, gram)


def summed_over_groups(value):
    groups = lax.axis_size("dp")
    for level in range(groups.bit_length() - 1):
        pairs = [(source, source ^ 2**level) for source in range(groups)]
        value = value + lax.ppermute(value, "dp", pairs)
    return value


def shards(tokens_in, gate_pre, up_pre, hidden_grad, out_grad, proj_model, proj_hidden):
    model_shards = lax.axis_size("mp")
    rows_each = WIDE // model_shards
    local_examples = tokens_in.shape[0] // LEN
    place = lax.axis_index("mp").astype(jnp.int32).reshape(1)
    part = project(
        gate_pre, up_pre, hidden_grad, proj_hidden, tokens_in, out_grad, proj_model
    )
    parts = [part]
    for away in range(1, model_shards):
        pairs = [(source, (source + away) % model_shards) for source in range(model_shards)]
        parts.append(lax.ppermute(part, "mp", pairs))
    rows, gram = gram_of(place, parts, rows_each)
    gram = summed_over_groups(gram)
    factor = math.sqrt(local_examples * lax.axis_size("dp") * 2 * RANK)
    return whiten(rows, gram, rows_each, factor)


def solution(mesh):
    in_specs = (
        P("dp", "mp"),
        P("dp", "mp"),
        P("dp", "mp"),
        P("dp", "mp"),
        P("dp", "mp"),
        P("mp", None),
        P("mp", None),
    )
    out_specs = P("dp", "mp", None)
    return jax.shard_map(shards, mesh=mesh, in_specs=in_specs, out_specs=out_specs, check_vma=False)
```

```python
import functools
import math

import jax
import jax.numpy as jnp
from jax import lax
from jax.experimental import pallas as pl
from jax.experimental.pallas import tpu as pltpu
from jax.sharding import PartitionSpec as P

RANK = 64
LEN = 128
WIDE = 2 * RANK
HIDDEN_PIECES = 16
MODEL_PIECES = 4
AHEAD = 4
STRIP = 32

highest = lax.Precision.HIGHEST
whole_vmem = pl.BlockSpec(memory_space=pltpu.VMEM)
left_in_hbm = pl.BlockSpec(memory_space=pl.ANY)
small = pltpu.CompilerParams(vmem_limit_bytes=8 * 2**20)


def pieces_of(width, most):
    count = most
    while width % (count * 128):
        count //= 2
    return count, width // count


def lanes_of(shape):
    return lax.broadcasted_iota(jnp.int32, shape, len(shape) - 1)


def project_kernel(gate, up, grad, proj_hidden, tokens, outer, proj_model, out, *rest):
    gate_v, up_v, grad_v, hidden_w, tokens_v, outer_v, model_w, acts, sems, model_sems = rest
    rows, hidden_width = gate.shape
    model_width = tokens.shape[1]
    hidden_count, hidden_each = pieces_of(hidden_width, HIDDEN_PIECES)
    model_count, model_each = pieces_of(model_width, MODEL_PIECES)

    hidden_copies = []
    for piece in range(hidden_count):
        cut = pl.ds(piece * hidden_each, hidden_each)
        hidden_copies.append(
            [
                pltpu.make_async_copy(gate.at[:, cut], gate_v.at[:, cut], sems.at[piece, 0]),
                pltpu.make_async_copy(grad.at[:, cut], grad_v.at[:, cut], sems.at[piece, 1]),
                pltpu.make_async_copy(up.at[:, cut], up_v.at[:, cut], sems.at[piece, 2]),
                pltpu.make_async_copy(
                    proj_hidden.at[cut, :], hidden_w.at[cut, :], sems.at[piece, 3]
                ),
            ]
        )
    model_copies = []
    for piece in range(model_count):
        cut = pl.ds(piece * model_each, model_each)
        model_copies.append(
            [
                pltpu.make_async_copy(
                    tokens.at[:, cut], tokens_v.at[:, cut], model_sems.at[piece, 0]
                ),
                pltpu.make_async_copy(
                    outer.at[:, cut], outer_v.at[:, cut], model_sems.at[piece, 1]
                ),
                pltpu.make_async_copy(
                    proj_model.at[cut, :], model_w.at[cut, :], model_sems.at[piece, 2]
                ),
            ]
        )
    waiting = hidden_copies + model_copies

    def start(which):
        if which < len(waiting):
            for copy in waiting[which]:
                copy.start()

    for which in range(AHEAD):
        start(which)
    hidden_sum = jnp.zeros((2 * rows, WIDE), jnp.float32)
    for piece in range(hidden_count):
        for copy in hidden_copies[piece]:
            copy.wait()
        start(piece + AHEAD)
        slot = piece % 2
        for strip in range(0, rows, STRIP):
            for first in range(0, hidden_each, 128):
                at = (slice(strip, strip + STRIP), pl.ds(piece * hidden_each + first, 128))
                half = gate_v[at].astype(jnp.float32) * 0.5
                act = half + half * jnp.tanh(half)
                to = pl.ds(first, 128)
                acts[slot, pl.ds(strip, STRIP), to] = (
                    grad_v[at].astype(jnp.float32) * act
                ).astype(jnp.bfloat16)
                acts[slot, pl.ds(rows + strip, STRIP), to] = (
                    act * up_v[at].astype(jnp.float32)
                ).astype(jnp.bfloat16)
        cut = slice(piece * hidden_each, (piece + 1) * hidden_each)
        hidden_sum += jnp.dot(acts[slot], hidden_w[cut, :], preferred_element_type=jnp.float32)
    model_sum = jnp.zeros((2 * rows, WIDE), jnp.float32)
    for piece in range(model_count):
        for copy in model_copies[piece]:
            copy.wait()
        start(hidden_count + piece + AHEAD)
        cut = slice(piece * model_each, (piece + 1) * model_each)
        both = jnp.concatenate([tokens_v[:, cut], outer_v[:, cut]], axis=0)
        model_sum += jnp.dot(both, model_w[cut, :], preferred_element_type=jnp.float32)

    low = lanes_of((rows, WIDE)) < RANK
    upward = pltpu.roll(hidden_sum[:rows], RANK, 1)
    hidden_side = pltpu.roll(hidden_sum[rows:], RANK, 1)
    out[:, :WIDE] = jnp.where(low, model_sum[:rows], upward)
    out[:, WIDE:] = jnp.where(low, hidden_side, model_sum[rows:])


def project(gate_pre, up_pre, hidden_grad, proj_hidden, tokens_in, out_grad, proj_model):
    rows, hidden_width = gate_pre.shape
    model_width = tokens_in.shape[1]
    hidden_count, _ = pieces_of(hidden_width, HIDDEN_PIECES)
    model_count, _ = pieces_of(model_width, MODEL_PIECES)
    held = jnp.bfloat16
    return pl.pallas_call(
        project_kernel,
        out_shape=jax.ShapeDtypeStruct((rows, 2 * WIDE), jnp.float32),
        in_specs=[left_in_hbm] * 7,
        out_specs=whole_vmem,
        scratch_shapes=[
            pltpu.VMEM((rows, hidden_width), held),
            pltpu.VMEM((rows, hidden_width), held),
            pltpu.VMEM((rows, hidden_width), held),
            pltpu.VMEM((hidden_width, WIDE), held),
            pltpu.VMEM((rows, model_width), held),
            pltpu.VMEM((rows, model_width), held),
            pltpu.VMEM((model_width, WIDE), held),
            pltpu.VMEM((2, 2 * rows, hidden_width // hidden_count), held),
            pltpu.SemaphoreType.DMA((hidden_count, 4)),
            pltpu.SemaphoreType.DMA((model_count, 3)),
        ],
        compiler_params=pltpu.CompilerParams(vmem_limit_bytes=56 * 10**6),
        name="project",
    )(gate_pre, up_pre, hidden_grad, proj_hidden, tokens_in, out_grad, proj_model)


def gram_kernel(rows_each, count, *refs):
    place, parts, (rows_ref, gram_ref) = refs[0], refs[1 : 1 + count], refs[1 + count :]
    total = parts[0][...]
    for part in parts[1:]:
        total += part[...]
    row = lax.broadcasted_iota(jnp.int32, (WIDE, WIDE), 0)
    lane = lanes_of((WIDE, WIDE))
    low = lanes_of((RANK, WIDE)) < RANK
    gram = jnp.zeros((RANK, WIDE), jnp.float32)
    shift = lax.rem(WIDE - place[0] * rows_each, WIDE)
    for example in range(total.shape[0] // LEN):
        mixed = []
        for at in (0, WIDE):
            sides = total[example * LEN : (example + 1) * LEN, at : at + WIDE]
            crossed = jnp.dot(
                sides.T, sides, precision=highest, preferred_element_type=jnp.float32
            )
            mixed.append(jnp.where((row < RANK) != (lane < RANK), crossed, 0.0))
        up_block, down_block = mixed[0][RANK:], mixed[1][RANK:]
        across = jnp.where(low, up_block, pltpu.roll(down_block, RANK, 1))
        rows_ref[example] = jnp.where(low, pltpu.roll(across, shift, 1), 0.0)
        gram += jnp.dot(
            jnp.concatenate([up_block, down_block], axis=1),
            jnp.concatenate(mixed, axis=0),
            precision=highest,
            preferred_element_type=jnp.float32,
        )
    top, bottom = gram[: RANK // 2], gram[RANK // 2 :]
    gram_ref[...] = jnp.where(
        lanes_of(top.shape) < RANK, pltpu.roll(top, RANK, 1), bottom
    )


def gram_of(place, parts, rows_each):
    examples = parts[0].shape[0] // LEN
    return pl.pallas_call(
        functools.partial(gram_kernel, rows_each, len(parts)),
        out_shape=[
            jax.ShapeDtypeStruct((examples, RANK, WIDE), jnp.float32),
            jax.ShapeDtypeStruct((RANK // 2, WIDE), jnp.float32),
        ],
        in_specs=[pl.BlockSpec(memory_space=pltpu.SMEM)] + [whole_vmem] * len(parts),
        out_specs=[whole_vmem] * 2,
        compiler_params=small,
        name="gram",
    )(place, *parts)


def eliminated(state):
    height = 8
    blocks = len(state)
    state = list(state)
    sub = lax.broadcasted_iota(jnp.int32, state[0].shape, 0)

    def across(block, at):
        return jnp.broadcast_to(block[:, at : at + 1], block.shape)

    def down(block, at):
        return jnp.broadcast_to(block[at : at + 1, :], block.shape)

    done = []
    for held in range(blocks):
        base = RANK + held * height
        own = state[held]
        columns = [across(own, base + k) for k in range(height)]
        corner = {
            (k, m): down(columns[m], k) for k in range(height) for m in range(k, height)
        }
        rows = [down(own, k) for k in range(height)]
        ahead = None
        if held + 1 < blocks:
            ahead = [across(state[held + 1], base + k) for k in range(height)]
        factors = {}
        inverses = []
        for k in range(height):
            inverse = 1.0 / corner[k, k]
            inverses.append(inverse)
            for m in range(k + 1, height):
                factor = corner[k, m] * inverse
                factors[k, m] = factor
                for n in range(m, height):
                    corner[m, n] = corner[m, n] - factor * corner[k, n]
                rows[m] = rows[m] - factor * rows[k]
                if ahead is not None:
                    ahead[m] = ahead[m] - factor * ahead[k]
        if ahead is not None:
            taken = [ahead[k] * (inverses[k] * rows[k]) for k in range(height)]
            while len(taken) > 1:
                taken = [left + right for left, right in zip(taken[::2], taken[1::2])]
            state[held + 1] = state[held + 1] - taken[0]
        if held + 2 < blocks:
            back = [inverses[k] * rows[k] for k in range(height)]
            for k in reversed(range(height)):
                for m in range(k):
                    back[m] = back[m] - factors[m, k] * back[k]
            for other in range(held + 2, blocks):
                for k in range(height):
                    state[other] = state[other] - across(state[other], base + k) * back[k]
        block = rows[0] * lax.rsqrt(corner[0, 0])
        for k in range(1, height):
            block = jnp.where(sub == k, rows[k] * lax.rsqrt(corner[k, k]), block)
        done.append(block)
    return done


def whiten_kernel(factor, rows_each, rows_ref, gram_ref, out_ref):
    packed = gram_ref[...]
    gram = jnp.concatenate([pltpu.roll(packed, RANK, 1), packed], axis=0)
    low = lanes_of((RANK, WIDE)) < RANK
    for example in range(rows_ref.shape[0]):
        joined = jnp.where(low, rows_ref[example], gram)
        done = eliminated([joined[at : at + 8] for at in range(0, RANK, 8)])
        solved = (jnp.concatenate(done, axis=0) * factor).T
        out_ref[example] = solved[:rows_each, :]


def whiten(rows, gram, rows_each, factor):
    return pl.pallas_call(
        functools.partial(whiten_kernel, factor, rows_each),
        out_shape=jax.ShapeDtypeStruct((rows.shape[0], rows_each, RANK), jnp.float32),
        in_specs=[whole_vmem] * 2,
        out_specs=whole_vmem,
        compiler_params=small,
        name="whiten",
    )(rows, gram)


def summed_over_groups(value):
    groups, model_shards = lax.axis_size("dp"), lax.axis_size("mp")
    last = model_shards - 1
    for level in range(groups.bit_length() - 1):
        pairs = [
            (group * model_shards + last, (group ^ 2**level) * model_shards + last)
            for group in range(groups)
        ]
        value = value + lax.ppermute(value, ("dp", "mp"), pairs)
    result = value
    for other in range(last):
        received = lax.ppermute(value, "mp", [(last, other)])
        result = jnp.where(lax.axis_index("mp") == other, received, result)
    return result


def shards(tokens_in, gate_pre, up_pre, hidden_grad, out_grad, proj_model, proj_hidden):
    model_shards = lax.axis_size("mp")
    rows_each = WIDE // model_shards
    local_examples = tokens_in.shape[0] // LEN
    place = lax.axis_index("mp").astype(jnp.int32).reshape(1)
    part = project(
        gate_pre, up_pre, hidden_grad, proj_hidden, tokens_in, out_grad, proj_model
    )
    parts = [part]
    for away in range(1, model_shards):
        pairs = [(source, (source + away) % model_shards) for source in range(model_shards)]
        parts.append(lax.ppermute(part, "mp", pairs))
    rows, gram = gram_of(place, parts, rows_each)
    gram = summed_over_groups(gram)
    factor = math.sqrt(local_examples * lax.axis_size("dp") * 2 * RANK)
    return whiten(rows, gram, rows_each, factor)


def solution(mesh):
    in_specs = (
        P("dp", "mp"),
        P("dp", "mp"),
        P("dp", "mp"),
        P("dp", "mp"),
        P("dp", "mp"),
        P("mp", None),
        P("mp", None),
    )
    out_specs = P("dp", "mp", None)
    return jax.shard_map(shards, mesh=mesh, in_specs=in_specs, out_specs=out_specs, check_vma=False)
```

```python
import functools
import math

import jax
import jax.numpy as jnp
from jax import lax
from jax.experimental import pallas as pl
from jax.experimental.pallas import tpu as pltpu
from jax.sharding import PartitionSpec as P

RANK = 64
LEN = 128
WIDE = 2 * RANK
EACH = 1024
STEP = 256
AHEAD = 4

highest = lax.Precision.HIGHEST
whole_vmem = pl.BlockSpec(memory_space=pltpu.VMEM)
left_in_hbm = pl.BlockSpec(memory_space=pl.ANY)
small = pltpu.CompilerParams(vmem_limit_bytes=8 * 2**20)


def cuts_of(width, each):
    return [(first, min(each, width - first)) for first in range(0, width, each)]


def lanes_of(shape):
    return lax.broadcasted_iota(jnp.int32, shape, len(shape) - 1)


def project_kernel(gate, up, grad, proj_hidden, tokens, outer, proj_model, out, *rest):
    gate_v, up_v, grad_v, hidden_w, tokens_v, outer_v, model_w, sems, model_sems = rest
    rows, hidden_width = gate.shape
    model_width = tokens.shape[1]
    hidden_cuts, model_cuts = cuts_of(hidden_width, EACH), cuts_of(model_width, EACH)

    copies = []
    for piece, (first, size) in enumerate(hidden_cuts):
        cut = pl.ds(first, size)
        pairs = [
            (gate.at[:, cut], gate_v.at[:, cut]),
            (grad.at[:, cut], grad_v.at[:, cut]),
            (up.at[:, cut], up_v.at[:, cut]),
            (proj_hidden.at[cut, :], hidden_w.at[cut, :]),
        ]
        copies.append(
            [
                pltpu.make_async_copy(source, target, sems.at[piece, which])
                for which, (source, target) in enumerate(pairs)
            ]
        )
    for piece, (first, size) in enumerate(model_cuts):
        cut = pl.ds(first, size)
        pairs = [
            (tokens.at[:, cut], tokens_v.at[:, cut]),
            (outer.at[:, cut], outer_v.at[:, cut]),
            (proj_model.at[cut, :], model_w.at[cut, :]),
        ]
        copies.append(
            [
                pltpu.make_async_copy(source, target, model_sems.at[piece, which])
                for which, (source, target) in enumerate(pairs)
            ]
        )

    def arrive(which):
        for copy in copies[which]:
            copy.wait()
        if which + AHEAD < len(copies):
            for copy in copies[which + AHEAD]:
                copy.start()

    for group in copies[:AHEAD]:
        for copy in group:
            copy.start()
    hidden_sum = jnp.zeros((2 * rows, WIDE), jnp.float32)
    for piece, (begin, size) in enumerate(hidden_cuts):
        arrive(piece)
        for first, step in cuts_of(size, STEP):
            cut = slice(begin + first, begin + first + step)
            half = gate_v[:, cut].astype(jnp.float32) * 0.5
            act = half + half * jnp.tanh(half)
            up_grad = (grad_v[:, cut].astype(jnp.float32) * act).astype(jnp.bfloat16)
            hidden = (act * up_v[:, cut].astype(jnp.float32)).astype(jnp.bfloat16)
            both = jnp.concatenate([up_grad, hidden], axis=0)
            hidden_sum += jnp.dot(both, hidden_w[cut, :], preferred_element_type=jnp.float32)
    model_sum = jnp.zeros((2 * rows, WIDE), jnp.float32)
    for piece, (begin, size) in enumerate(model_cuts):
        arrive(len(hidden_cuts) + piece)
        cut = slice(begin, begin + size)
        both = jnp.concatenate([tokens_v[:, cut], outer_v[:, cut]], axis=0)
        model_sum += jnp.dot(both, model_w[cut, :], preferred_element_type=jnp.float32)

    low = lanes_of((rows, WIDE)) < RANK
    upward = pltpu.roll(hidden_sum[:rows], RANK, 1)
    hidden_side = pltpu.roll(hidden_sum[rows:], RANK, 1)
    out[:, :WIDE] = jnp.where(low, model_sum[:rows], upward)
    out[:, WIDE:] = jnp.where(low, hidden_side, model_sum[rows:])


def project(gate_pre, up_pre, hidden_grad, proj_hidden, tokens_in, out_grad, proj_model):
    rows, hidden_width = gate_pre.shape
    model_width = tokens_in.shape[1]
    held = jnp.bfloat16
    return pl.pallas_call(
        project_kernel,
        out_shape=jax.ShapeDtypeStruct((rows, 2 * WIDE), jnp.float32),
        in_specs=[left_in_hbm] * 7,
        out_specs=whole_vmem,
        scratch_shapes=[
            pltpu.VMEM((rows, hidden_width), held),
            pltpu.VMEM((rows, hidden_width), held),
            pltpu.VMEM((rows, hidden_width), held),
            pltpu.VMEM((hidden_width, WIDE), held),
            pltpu.VMEM((rows, model_width), held),
            pltpu.VMEM((rows, model_width), held),
            pltpu.VMEM((model_width, WIDE), held),
            pltpu.SemaphoreType.DMA((len(cuts_of(hidden_width, EACH)), 4)),
            pltpu.SemaphoreType.DMA((len(cuts_of(model_width, EACH)), 3)),
        ],
        compiler_params=pltpu.CompilerParams(vmem_limit_bytes=56 * 10**6),
        name="project",
    )(gate_pre, up_pre, hidden_grad, proj_hidden, tokens_in, out_grad, proj_model)


def gram_kernel(rows_each, count, *refs):
    place, parts, (rows_ref, gram_ref) = refs[0], refs[1 : 1 + count], refs[1 + count :]
    total = parts[0][...]
    for part in parts[1:]:
        total += part[...]
    row = lax.broadcasted_iota(jnp.int32, (WIDE, WIDE), 0)
    lane = lanes_of((WIDE, WIDE))
    low = lanes_of((RANK, WIDE)) < RANK
    gram = jnp.zeros((RANK, WIDE), jnp.float32)
    shift = lax.rem(WIDE - place[0] * rows_each, WIDE)
    for example in range(total.shape[0] // LEN):
        mixed = []
        for at in (0, WIDE):
            sides = total[example * LEN : (example + 1) * LEN, at : at + WIDE]
            crossed = jnp.dot(
                sides.T, sides, precision=highest, preferred_element_type=jnp.float32
            )
            mixed.append(jnp.where((row < RANK) != (lane < RANK), crossed, 0.0))
        up_block, down_block = mixed[0][RANK:], mixed[1][RANK:]
        across = jnp.where(low, up_block, pltpu.roll(down_block, RANK, 1))
        rows_ref[example] = jnp.where(low, pltpu.roll(across, shift, 1), 0.0)
        gram += jnp.dot(
            jnp.concatenate([up_block, down_block], axis=1),
            jnp.concatenate(mixed, axis=0),
            precision=highest,
            preferred_element_type=jnp.float32,
        )
    top, bottom = gram[: RANK // 2], gram[RANK // 2 :]
    gram_ref[...] = jnp.where(
        lanes_of(top.shape) < RANK, pltpu.roll(top, RANK, 1), bottom
    )


def gram_of(place, parts, rows_each):
    examples = parts[0].shape[0] // LEN
    return pl.pallas_call(
        functools.partial(gram_kernel, rows_each, len(parts)),
        out_shape=[
            jax.ShapeDtypeStruct((examples, RANK, WIDE), jnp.float32),
            jax.ShapeDtypeStruct((RANK // 2, WIDE), jnp.float32),
        ],
        in_specs=[pl.BlockSpec(memory_space=pltpu.SMEM)] + [whole_vmem] * len(parts),
        out_specs=[whole_vmem] * 2,
        compiler_params=small,
        name="gram",
    )(place, *parts)


def eliminated(state):
    height = 8
    blocks = len(state)
    state = list(state)
    sub = lax.broadcasted_iota(jnp.int32, state[0].shape, 0)

    def across(block, at):
        return jnp.broadcast_to(block[:, at : at + 1], block.shape)

    def down(block, at):
        return jnp.broadcast_to(block[at : at + 1, :], block.shape)

    done = []
    for held in range(blocks):
        base = RANK + held * height
        own = state[held]
        columns = [across(own, base + k) for k in range(height)]
        corner = {
            (k, m): down(columns[m], k) for k in range(height) for m in range(k, height)
        }
        rows = [down(own, k) for k in range(height)]
        ahead = None
        if held + 1 < blocks:
            ahead = [across(state[held + 1], base + k) for k in range(height)]
        factors = {}
        inverses = []
        for k in range(height):
            inverse = pl.reciprocal(corner[k, k], approx=True)
            inverses.append(inverse)
            for m in range(k + 1, height):
                factor = corner[k, m] * inverse
                factors[k, m] = factor
                for n in range(m, height):
                    corner[m, n] = corner[m, n] - factor * corner[k, n]
                rows[m] = rows[m] - factor * rows[k]
                if ahead is not None:
                    ahead[m] = ahead[m] - factor * ahead[k]
        if ahead is not None:
            taken = [ahead[k] * (inverses[k] * rows[k]) for k in range(height)]
            while len(taken) > 1:
                taken = [left + right for left, right in zip(taken[::2], taken[1::2])]
            state[held + 1] = state[held + 1] - taken[0]
        if held + 2 < blocks:
            back = [inverses[k] * rows[k] for k in range(height)]
            for k in reversed(range(height)):
                for m in range(k):
                    back[m] = back[m] - factors[m, k] * back[k]
            for other in range(held + 2, blocks):
                for k in range(height):
                    state[other] = state[other] - across(state[other], base + k) * back[k]
        block = rows[0] * lax.rsqrt(corner[0, 0])
        for k in range(1, height):
            block = jnp.where(sub == k, rows[k] * lax.rsqrt(corner[k, k]), block)
        done.append(block)
    return done


def whiten_kernel(factor, rows_each, rows_ref, gram_ref, out_ref):
    packed = gram_ref[...]
    gram = jnp.concatenate([pltpu.roll(packed, RANK, 1), packed], axis=0)
    low = lanes_of((RANK, WIDE)) < RANK
    for example in range(rows_ref.shape[0]):
        joined = jnp.where(low, rows_ref[example], gram)
        done = eliminated([joined[at : at + 8] for at in range(0, RANK, 8)])
        solved = (jnp.concatenate(done, axis=0) * factor).T
        out_ref[example] = solved[:rows_each, :]


def whiten(rows, gram, rows_each, factor):
    return pl.pallas_call(
        functools.partial(whiten_kernel, factor, rows_each),
        out_shape=jax.ShapeDtypeStruct((rows.shape[0], rows_each, RANK), jnp.float32),
        in_specs=[whole_vmem] * 2,
        out_specs=whole_vmem,
        compiler_params=small,
        name="whiten",
    )(rows, gram)


def summed_over_groups(value):
    groups, model_shards = lax.axis_size("dp"), lax.axis_size("mp")
    last = model_shards - 1
    for level in range(groups.bit_length() - 1):
        pairs = [
            (
                group * model_shards + shard,
                (group ^ 2**level if shard == last else group) * model_shards + shard,
            )
            for group in range(groups)
            for shard in range(model_shards)
        ]
        value = value + lax.ppermute(value, ("dp", "mp"), pairs)
    result = value
    for away in range(1, model_shards):
        pairs = [(source, (source + away) % model_shards) for source in range(model_shards)]
        received = lax.ppermute(value, "mp", pairs)
        result = jnp.where(lax.axis_index("mp") == away - 1, received, result)
    return result


def shards(tokens_in, gate_pre, up_pre, hidden_grad, out_grad, proj_model, proj_hidden):
    model_shards = lax.axis_size("mp")
    rows_each = WIDE // model_shards
    local_examples = tokens_in.shape[0] // LEN
    place = lax.axis_index("mp").astype(jnp.int32).reshape(1)
    part = project(
        gate_pre, up_pre, hidden_grad, proj_hidden, tokens_in, out_grad, proj_model
    )
    parts = [part]
    for away in range(1, model_shards):
        pairs = [(source, (source + away) % model_shards) for source in range(model_shards)]
        parts.append(lax.ppermute(part, "mp", pairs))
    rows, gram = gram_of(place, parts, rows_each)
    gram = summed_over_groups(gram)
    factor = math.sqrt(local_examples * lax.axis_size("dp") * 2 * RANK)
    return whiten(rows, gram, rows_each, factor)


def solution(mesh):
    in_specs = (
        P("dp", "mp"),
        P("dp", "mp"),
        P("dp", "mp"),
        P("dp", "mp"),
        P("dp", "mp"),
        P("mp", None),
        P("mp", None),
    )
    out_specs = P("dp", "mp", None)
    return jax.shard_map(shards, mesh=mesh, in_specs=in_specs, out_specs=out_specs, check_vma=False)
```

```python
import functools
import math

import jax
import jax.numpy as jnp
from jax import lax
from jax.experimental import pallas as pl
from jax.experimental.pallas import tpu as pltpu
from jax.sharding import PartitionSpec as P

RANK = 64
LEN = 128
WIDE = 2 * RANK
EACH = 1024
STEP = 256
AHEAD = 4

highest = lax.Precision.HIGHEST
whole_vmem = pl.BlockSpec(memory_space=pltpu.VMEM)
left_in_hbm = pl.BlockSpec(memory_space=pl.ANY)
small = pltpu.CompilerParams(vmem_limit_bytes=8 * 2**20)


def cuts_of(width, each):
    return [(first, min(each, width - first)) for first in range(0, width, each)]


def lanes_of(shape):
    return lax.broadcasted_iota(jnp.int32, shape, len(shape) - 1)


def project_kernel(gate, up, grad, proj_hidden, tokens, outer, proj_model, out, *rest):
    gate_v, up_v, grad_v, hidden_w, tokens_v, outer_v, model_w, sems, model_sems = rest
    rows, hidden_width = gate.shape
    model_width = tokens.shape[1]
    hidden_cuts, model_cuts = cuts_of(hidden_width, EACH), cuts_of(model_width, EACH)

    copies = []
    for piece, (first, size) in enumerate(hidden_cuts):
        cut = pl.ds(first, size)
        pairs = [
            (gate.at[:, cut], gate_v.at[:, cut]),
            (grad.at[:, cut], grad_v.at[:, cut]),
            (up.at[:, cut], up_v.at[:, cut]),
            (proj_hidden.at[cut, :], hidden_w.at[cut, :]),
        ]
        copies.append(
            [
                pltpu.make_async_copy(source, target, sems.at[piece, which])
                for which, (source, target) in enumerate(pairs)
            ]
        )
    for piece, (first, size) in enumerate(model_cuts):
        cut = pl.ds(first, size)
        pairs = [
            (tokens.at[:, cut], tokens_v.at[:, cut]),
            (outer.at[:, cut], outer_v.at[:, cut]),
            (proj_model.at[cut, :], model_w.at[cut, :]),
        ]
        copies.append(
            [
                pltpu.make_async_copy(source, target, model_sems.at[piece, which])
                for which, (source, target) in enumerate(pairs)
            ]
        )

    def arrive(which):
        for copy in copies[which]:
            copy.wait()
        if which + AHEAD < len(copies):
            for copy in copies[which + AHEAD]:
                copy.start()

    for group in copies[:AHEAD]:
        for copy in group:
            copy.start()
    def gated(begin, size):
        parts = []
        for first, step in cuts_of(size, STEP):
            cut = slice(begin + first, begin + first + step)
            half = gate_v[:, cut].astype(jnp.float32) * 0.5
            act = half + half * jnp.tanh(half)
            up_grad = (grad_v[:, cut].astype(jnp.float32) * act).astype(jnp.bfloat16)
            hidden = (act * up_v[:, cut].astype(jnp.float32)).astype(jnp.bfloat16)
            parts.append(jnp.concatenate([up_grad, hidden], axis=0))
        return jnp.concatenate(parts, axis=1)

    hidden_sum = jnp.zeros((2 * rows, WIDE), jnp.float32)
    both = None
    for piece, (begin, size) in enumerate(hidden_cuts):
        arrive(piece)
        if piece:
            before, width = hidden_cuts[piece - 1]
            hidden_sum += jnp.dot(
                both,
                hidden_w[before : before + width, :],
                preferred_element_type=jnp.float32,
            )
        both = gated(begin, size)
    before, width = hidden_cuts[-1]
    hidden_sum += jnp.dot(
        both, hidden_w[before : before + width, :], preferred_element_type=jnp.float32
    )
    model_sum = jnp.zeros((2 * rows, WIDE), jnp.float32)
    for piece, (begin, size) in enumerate(model_cuts):
        arrive(len(hidden_cuts) + piece)
        cut = slice(begin, begin + size)
        both = jnp.concatenate([tokens_v[:, cut], outer_v[:, cut]], axis=0)
        model_sum += jnp.dot(both, model_w[cut, :], preferred_element_type=jnp.float32)

    low = lanes_of((rows, WIDE)) < RANK
    upward = pltpu.roll(hidden_sum[:rows], RANK, 1)
    hidden_side = pltpu.roll(hidden_sum[rows:], RANK, 1)
    out[:, :WIDE] = jnp.where(low, model_sum[:rows], upward)
    out[:, WIDE:] = jnp.where(low, hidden_side, model_sum[rows:])


def project(gate_pre, up_pre, hidden_grad, proj_hidden, tokens_in, out_grad, proj_model):
    rows, hidden_width = gate_pre.shape
    model_width = tokens_in.shape[1]
    held = jnp.bfloat16
    return pl.pallas_call(
        project_kernel,
        out_shape=jax.ShapeDtypeStruct((rows, 2 * WIDE), jnp.float32),
        in_specs=[left_in_hbm] * 7,
        out_specs=whole_vmem,
        scratch_shapes=[
            pltpu.VMEM((rows, hidden_width), held),
            pltpu.VMEM((rows, hidden_width), held),
            pltpu.VMEM((rows, hidden_width), held),
            pltpu.VMEM((hidden_width, WIDE), held),
            pltpu.VMEM((rows, model_width), held),
            pltpu.VMEM((rows, model_width), held),
            pltpu.VMEM((model_width, WIDE), held),
            pltpu.SemaphoreType.DMA((len(cuts_of(hidden_width, EACH)), 4)),
            pltpu.SemaphoreType.DMA((len(cuts_of(model_width, EACH)), 3)),
        ],
        compiler_params=pltpu.CompilerParams(vmem_limit_bytes=56 * 10**6),
        name="project",
    )(gate_pre, up_pre, hidden_grad, proj_hidden, tokens_in, out_grad, proj_model)


def gram_kernel(rows_each, count, *refs):
    place, parts, (rows_ref, gram_ref) = refs[0], refs[1 : 1 + count], refs[1 + count :]
    total = parts[0][...]
    for part in parts[1:]:
        total += part[...]
    row = lax.broadcasted_iota(jnp.int32, (WIDE, WIDE), 0)
    lane = lanes_of((WIDE, WIDE))
    low = lanes_of((RANK, WIDE)) < RANK
    gram = jnp.zeros((RANK, WIDE), jnp.float32)
    shift = lax.rem(WIDE - place[0] * rows_each, WIDE)
    for example in range(total.shape[0] // LEN):
        mixed = []
        for at in (0, WIDE):
            sides = total[example * LEN : (example + 1) * LEN, at : at + WIDE]
            crossed = jnp.dot(
                sides.T, sides, precision=highest, preferred_element_type=jnp.float32
            )
            mixed.append(jnp.where((row < RANK) != (lane < RANK), crossed, 0.0))
        up_block, down_block = mixed[0][RANK:], mixed[1][RANK:]
        across = jnp.where(low, up_block, pltpu.roll(down_block, RANK, 1))
        rows_ref[example] = jnp.where(low, pltpu.roll(across, shift, 1), 0.0)
        gram += jnp.dot(
            jnp.concatenate([up_block, down_block], axis=1),
            jnp.concatenate(mixed, axis=0),
            precision=highest,
            preferred_element_type=jnp.float32,
        )
    top, bottom = gram[: RANK // 2], gram[RANK // 2 :]
    gram_ref[...] = jnp.where(
        lanes_of(top.shape) < RANK, pltpu.roll(top, RANK, 1), bottom
    )


def gram_of(place, parts, rows_each):
    examples = parts[0].shape[0] // LEN
    return pl.pallas_call(
        functools.partial(gram_kernel, rows_each, len(parts)),
        out_shape=[
            jax.ShapeDtypeStruct((examples, RANK, WIDE), jnp.float32),
            jax.ShapeDtypeStruct((RANK // 2, WIDE), jnp.float32),
        ],
        in_specs=[pl.BlockSpec(memory_space=pltpu.SMEM)] + [whole_vmem] * len(parts),
        out_specs=[whole_vmem] * 2,
        compiler_params=small,
        name="gram",
    )(place, *parts)


def eliminated(state):
    height = 8
    blocks = len(state)
    state = list(state)
    sub = lax.broadcasted_iota(jnp.int32, state[0].shape, 0)

    def across(block, at):
        return jnp.broadcast_to(block[:, at : at + 1], block.shape)

    def down(block, at):
        return jnp.broadcast_to(block[at : at + 1, :], block.shape)

    done = []
    for held in range(blocks):
        base = RANK + held * height
        own = state[held]
        columns = [across(own, base + k) for k in range(height)]
        corner = {
            (k, m): down(columns[m], k) for k in range(height) for m in range(k, height)
        }
        rows = [down(own, k) for k in range(height)]
        ahead = None
        if held + 1 < blocks:
            ahead = [across(state[held + 1], base + k) for k in range(height)]
        factors = {}
        solved = [None] * height
        for k in range(0, height, 2):
            first, cross, second = corner[k, k], corner[k, k + 1], corner[k + 1, k + 1]
            determinant = first * second - cross * cross
            inverse = pl.reciprocal(determinant, approx=True)
            solved[k] = (second * rows[k] - cross * rows[k + 1]) * inverse
            solved[k + 1] = (first * rows[k + 1] - cross * rows[k]) * inverse
            for m in range(k + 2, height):
                left, right = corner[k, m], corner[k + 1, m]
                upper = second * left - cross * right
                lower = first * right - cross * left
                for n in range(m, height):
                    taken = upper * corner[k, n] + lower * corner[k + 1, n]
                    corner[m, n] = corner[m, n] - taken * inverse
                factors[k, m], factors[k + 1, m] = upper * inverse, lower * inverse
                for several in (rows, ahead):
                    if several is not None:
                        several[m] = several[m] - (
                            factors[k, m] * several[k] + factors[k + 1, m] * several[k + 1]
                        )
        if ahead is not None:
            taken = [ahead[k] * solved[k] for k in range(height)]
            while len(taken) > 1:
                taken = [left + right for left, right in zip(taken[::2], taken[1::2])]
            state[held + 1] = state[held + 1] - taken[0]
        if held + 2 < blocks:
            back = list(solved)
            for m in reversed(range(2, height)):
                for k in range(m - m % 2):
                    back[k] = back[k] - factors[k, m] * back[m]
            for other in range(held + 2, blocks):
                for k in range(height):
                    state[other] = state[other] - across(state[other], base + k) * back[k]
        block = jnp.zeros_like(own)
        for k in range(0, height, 2):
            first, cross, second = corner[k, k], corner[k, k + 1], corner[k + 1, k + 1]
            ratio = cross * pl.reciprocal(first, approx=True)
            final = second - cross * ratio
            block = jnp.where(sub == k, rows[k] * lax.rsqrt(first), block)
            block = jnp.where(
                sub == k + 1, (rows[k + 1] - ratio * rows[k]) * lax.rsqrt(final), block
            )
        done.append(block)
    return done


def whiten_kernel(factor, rows_each, rows_ref, gram_ref, out_ref):
    packed = gram_ref[...]
    gram = jnp.concatenate([pltpu.roll(packed, RANK, 1), packed], axis=0)
    low = lanes_of((RANK, WIDE)) < RANK
    for example in range(rows_ref.shape[0]):
        joined = jnp.where(low, rows_ref[example], gram)
        done = eliminated([joined[at : at + 8] for at in range(0, RANK, 8)])
        solved = (jnp.concatenate(done, axis=0) * factor).T
        out_ref[example] = solved[:rows_each, :]


def whiten(rows, gram, rows_each, factor):
    return pl.pallas_call(
        functools.partial(whiten_kernel, factor, rows_each),
        out_shape=jax.ShapeDtypeStruct((rows.shape[0], rows_each, RANK), jnp.float32),
        in_specs=[whole_vmem] * 2,
        out_specs=whole_vmem,
        compiler_params=small,
        name="whiten",
    )(rows, gram)


def summed_over_groups(value):
    groups, model_shards = lax.axis_size("dp"), lax.axis_size("mp")
    other = 1 if model_shards % 2 == 0 else 0
    for level in range(groups.bit_length() - 1):
        pairs = [
            (group * model_shards + shard, (group ^ 2**level) * model_shards + (shard ^ other))
            for group in range(groups)
            for shard in range(model_shards)
        ]
        value = value + lax.ppermute(value, ("dp", "mp"), pairs)
    return value


def shards(tokens_in, gate_pre, up_pre, hidden_grad, out_grad, proj_model, proj_hidden):
    model_shards = lax.axis_size("mp")
    rows_each = WIDE // model_shards
    local_examples = tokens_in.shape[0] // LEN
    place = lax.axis_index("mp").astype(jnp.int32).reshape(1)
    part = project(
        gate_pre, up_pre, hidden_grad, proj_hidden, tokens_in, out_grad, proj_model
    )
    parts = [part]
    for away in range(1, model_shards):
        pairs = [(source, (source + away) % model_shards) for source in range(model_shards)]
        parts.append(lax.ppermute(part, "mp", pairs))
    rows, gram = gram_of(place, parts, rows_each)
    gram = summed_over_groups(gram)
    factor = math.sqrt(local_examples * lax.axis_size("dp") * 2 * RANK)
    return whiten(rows, gram, rows_each, factor)


def solution(mesh):
    in_specs = (
        P("dp", "mp"),
        P("dp", "mp"),
        P("dp", "mp"),
        P("dp", "mp"),
        P("dp", "mp"),
        P("mp", None),
        P("mp", None),
    )
    out_specs = P("dp", "mp", None)
    return jax.shard_map(shards, mesh=mesh, in_specs=in_specs, out_specs=out_specs, check_vma=False)
```

```python
import functools
import math

import jax
import jax.numpy as jnp
from jax import lax
from jax.experimental import pallas as pl
from jax.experimental.pallas import tpu as pltpu
from jax.sharding import PartitionSpec as P

RANK = 64
LEN = 128
WIDE = 2 * RANK
EACH = 1024
STEP = 256
AHEAD = 4

highest = lax.Precision.HIGHEST
whole_vmem = pl.BlockSpec(memory_space=pltpu.VMEM)
left_in_hbm = pl.BlockSpec(memory_space=pl.ANY)
small = pltpu.CompilerParams(vmem_limit_bytes=8 * 2**20)


def lanes_of(shape):
    return lax.broadcasted_iota(jnp.int32, shape, len(shape) - 1)


def project_kernel(gate, up, grad, proj_hidden, tokens, outer, proj_model, out, *rest):
    gate_v, up_v, grad_v, hidden_w, tokens_v, outer_v, model_w = rest[:7]
    hidden_sum, model_sum, sems, model_sems = rest[7:]
    rows = gate.shape[0]
    hidden_each, model_each = math.gcd(gate.shape[1], EACH), math.gcd(tokens.shape[1], EACH)
    hidden_count = gate.shape[1] // hidden_each
    model_count = tokens.shape[1] // model_each

    def hidden_copies(piece):
        cut = pl.ds(pl.multiple_of(piece * hidden_each, hidden_each), hidden_each)
        pairs = [
            (gate.at[:, cut], gate_v.at[:, cut]),
            (grad.at[:, cut], grad_v.at[:, cut]),
            (up.at[:, cut], up_v.at[:, cut]),
            (proj_hidden.at[cut, :], hidden_w.at[cut, :]),
        ]
        return [
            pltpu.make_async_copy(source, target, sems.at[piece, which])
            for which, (source, target) in enumerate(pairs)
        ]

    def model_copies(piece):
        cut = pl.ds(pl.multiple_of(piece * model_each, model_each), model_each)
        pairs = [
            (tokens.at[:, cut], tokens_v.at[:, cut]),
            (outer.at[:, cut], outer_v.at[:, cut]),
            (proj_model.at[cut, :], model_w.at[cut, :]),
        ]
        return [
            pltpu.make_async_copy(source, target, model_sems.at[piece, which])
            for which, (source, target) in enumerate(pairs)
        ]

    def start(copies):
        for copy in copies:
            copy.start()

    def arrive(copies):
        for copy in copies:
            copy.wait()

    ahead = min(AHEAD, hidden_count)
    for piece in range(ahead):
        start(hidden_copies(piece))
    hidden_sum[...] = jnp.zeros_like(hidden_sum)
    model_sum[...] = jnp.zeros_like(model_sum)

    @pl.loop(0, hidden_count)
    def _(piece):
        arrive(hidden_copies(piece))

        @pl.when(piece + ahead < hidden_count)
        def _():
            start(hidden_copies(piece + ahead))

        @pl.when(piece + ahead == hidden_count)
        def _():
            for other in range(model_count):
                start(model_copies(other))

        base = piece * hidden_each
        total = None
        for first in range(0, hidden_each, STEP):
            step = min(STEP, hidden_each - first)
            cut = pl.ds(pl.multiple_of(base + first, 128), step)
            half = gate_v[:, cut].astype(jnp.float32) * 0.5
            act = half + half * jnp.tanh(half)
            up_grad = (grad_v[:, cut].astype(jnp.float32) * act).astype(jnp.bfloat16)
            hidden = (act * up_v[:, cut].astype(jnp.float32)).astype(jnp.bfloat16)
            both = jnp.concatenate([up_grad, hidden], axis=0)
            part = jnp.dot(both, hidden_w[cut, :], preferred_element_type=jnp.float32)
            total = part if total is None else total + part
        hidden_sum[...] += total

    @pl.loop(0, model_count)
    def _(piece):
        arrive(model_copies(piece))
        cut = pl.ds(pl.multiple_of(piece * model_each, model_each), model_each)
        both = jnp.concatenate([tokens_v[:, cut], outer_v[:, cut]], axis=0)
        model_sum[...] += jnp.dot(both, model_w[cut, :], preferred_element_type=jnp.float32)

    low = lanes_of((rows, WIDE)) < RANK
    upward = pltpu.roll(hidden_sum[:rows, :], RANK, 1)
    hidden_side = pltpu.roll(hidden_sum[rows:, :], RANK, 1)
    out[:, :WIDE] = jnp.where(low, model_sum[:rows, :], upward)
    out[:, WIDE:] = jnp.where(low, hidden_side, model_sum[rows:, :])


def project(gate_pre, up_pre, hidden_grad, proj_hidden, tokens_in, out_grad, proj_model):
    rows, hidden_width = gate_pre.shape
    model_width = tokens_in.shape[1]
    held = jnp.bfloat16
    return pl.pallas_call(
        project_kernel,
        out_shape=jax.ShapeDtypeStruct((rows, 2 * WIDE), jnp.float32),
        in_specs=[left_in_hbm] * 7,
        out_specs=whole_vmem,
        scratch_shapes=[
            pltpu.VMEM((rows, hidden_width), held),
            pltpu.VMEM((rows, hidden_width), held),
            pltpu.VMEM((rows, hidden_width), held),
            pltpu.VMEM((hidden_width, WIDE), held),
            pltpu.VMEM((rows, model_width), held),
            pltpu.VMEM((rows, model_width), held),
            pltpu.VMEM((model_width, WIDE), held),
            pltpu.VMEM((2 * rows, WIDE), jnp.float32),
            pltpu.VMEM((2 * rows, WIDE), jnp.float32),
            pltpu.SemaphoreType.DMA((hidden_width // math.gcd(hidden_width, EACH), 4)),
            pltpu.SemaphoreType.DMA((model_width // math.gcd(model_width, EACH), 3)),
        ],
        compiler_params=pltpu.CompilerParams(vmem_limit_bytes=56 * 10**6),
        name="project",
    )(gate_pre, up_pre, hidden_grad, proj_hidden, tokens_in, out_grad, proj_model)


def gram_kernel(rows_each, count, *refs):
    place, parts, (rows_ref, gram_ref) = refs[0], refs[1 : 1 + count], refs[1 + count :]
    total = parts[0][...]
    for part in parts[1:]:
        total += part[...]
    row = lax.broadcasted_iota(jnp.int32, (WIDE, WIDE), 0)
    lane = lanes_of((WIDE, WIDE))
    low = lanes_of((RANK, WIDE)) < RANK
    gram = jnp.zeros((RANK, WIDE), jnp.float32)
    shift = lax.rem(WIDE - place[0] * rows_each, WIDE)
    for example in range(total.shape[0] // LEN):
        mixed = []
        for at in (0, WIDE):
            sides = total[example * LEN : (example + 1) * LEN, at : at + WIDE]
            crossed = jnp.dot(
                sides.T, sides, precision=highest, preferred_element_type=jnp.float32
            )
            mixed.append(jnp.where((row < RANK) != (lane < RANK), crossed, 0.0))
        up_block, down_block = mixed[0][RANK:], mixed[1][RANK:]
        across = jnp.where(low, up_block, pltpu.roll(down_block, RANK, 1))
        rows_ref[example] = jnp.where(low, pltpu.roll(across, shift, 1), 0.0)
        gram += jnp.dot(
            jnp.concatenate([up_block, down_block], axis=1),
            jnp.concatenate(mixed, axis=0),
            precision=highest,
            preferred_element_type=jnp.float32,
        )
    top, bottom = gram[: RANK // 2], gram[RANK // 2 :]
    gram_ref[...] = jnp.where(
        lanes_of(top.shape) < RANK, pltpu.roll(top, RANK, 1), bottom
    )


def gram_of(place, parts, rows_each):
    examples = parts[0].shape[0] // LEN
    return pl.pallas_call(
        functools.partial(gram_kernel, rows_each, len(parts)),
        out_shape=[
            jax.ShapeDtypeStruct((examples, RANK, WIDE), jnp.float32),
            jax.ShapeDtypeStruct((RANK // 2, WIDE), jnp.float32),
        ],
        in_specs=[pl.BlockSpec(memory_space=pltpu.SMEM)] + [whole_vmem] * len(parts),
        out_specs=[whole_vmem] * 2,
        compiler_params=small,
        name="gram",
    )(place, *parts)


def eliminated(state):
    height = 8
    blocks = len(state)
    state = list(state)
    sub = lax.broadcasted_iota(jnp.int32, state[0].shape, 0)

    def across(block, at):
        return jnp.broadcast_to(block[:, at : at + 1], block.shape)

    def down(block, at):
        return jnp.broadcast_to(block[at : at + 1, :], block.shape)

    done = []
    for held in range(blocks):
        base = RANK + held * height
        own = state[held]
        columns = [across(own, base + k) for k in range(height)]
        corner = {
            (k, m): down(columns[m], k) for k in range(height) for m in range(k, height)
        }
        rows = [down(own, k) for k in range(height)]
        ahead = None
        if held + 1 < blocks:
            ahead = [across(state[held + 1], base + k) for k in range(height)]
        factors = {}
        solved = [None] * height
        for k in range(0, height, 2):
            first, cross, second = corner[k, k], corner[k, k + 1], corner[k + 1, k + 1]
            determinant = first * second - cross * cross
            inverse = pl.reciprocal(determinant, approx=True)
            solved[k] = (second * rows[k] - cross * rows[k + 1]) * inverse
            solved[k + 1] = (first * rows[k + 1] - cross * rows[k]) * inverse
            for m in range(k + 2, height):
                left, right = corner[k, m], corner[k + 1, m]
                upper = second * left - cross * right
                lower = first * right - cross * left
                for n in range(m, height):
                    taken = upper * corner[k, n] + lower * corner[k + 1, n]
                    corner[m, n] = corner[m, n] - taken * inverse
                factors[k, m], factors[k + 1, m] = upper * inverse, lower * inverse
                for several in (rows, ahead):
                    if several is not None:
                        several[m] = several[m] - (
                            factors[k, m] * several[k] + factors[k + 1, m] * several[k + 1]
                        )
        if ahead is not None:
            taken = [ahead[k] * solved[k] for k in range(height)]
            while len(taken) > 1:
                taken = [left + right for left, right in zip(taken[::2], taken[1::2])]
            state[held + 1] = state[held + 1] - taken[0]
        if held + 2 < blocks:
            back = list(solved)
            for m in reversed(range(2, height)):
                for k in range(m - m % 2):
                    back[k] = back[k] - factors[k, m] * back[m]
            for other in range(held + 2, blocks):
                for k in range(height):
                    state[other] = state[other] - across(state[other], base + k) * back[k]
        block = jnp.zeros_like(own)
        for k in range(0, height, 2):
            first, cross, second = corner[k, k], corner[k, k + 1], corner[k + 1, k + 1]
            ratio = cross * pl.reciprocal(first, approx=True)
            final = second - cross * ratio
            block = jnp.where(sub == k, rows[k] * lax.rsqrt(first), block)
            block = jnp.where(
                sub == k + 1, (rows[k + 1] - ratio * rows[k]) * lax.rsqrt(final), block
            )
        done.append(block)
    return done


def whiten_kernel(factor, rows_each, rows_ref, gram_ref, out_ref):
    packed = gram_ref[...]
    gram = jnp.concatenate([pltpu.roll(packed, RANK, 1), packed], axis=0)
    low = lanes_of((RANK, WIDE)) < RANK
    for example in range(rows_ref.shape[0]):
        joined = jnp.where(low, rows_ref[example], gram)
        done = eliminated([joined[at : at + 8] for at in range(0, RANK, 8)])
        solved = (jnp.concatenate(done, axis=0) * factor).T
        out_ref[example] = solved[:rows_each, :]


def whiten(rows, gram, rows_each, factor):
    return pl.pallas_call(
        functools.partial(whiten_kernel, factor, rows_each),
        out_shape=jax.ShapeDtypeStruct((rows.shape[0], rows_each, RANK), jnp.float32),
        in_specs=[whole_vmem] * 2,
        out_specs=whole_vmem,
        compiler_params=small,
        name="whiten",
    )(rows, gram)


def summed_over_groups(value):
    groups, model_shards = lax.axis_size("dp"), lax.axis_size("mp")
    other = 1 if model_shards % 2 == 0 else 0
    for level in range(groups.bit_length() - 1):
        pairs = [
            (group * model_shards + shard, (group ^ 2**level) * model_shards + (shard ^ other))
            for group in range(groups)
            for shard in range(model_shards)
        ]
        value = value + lax.ppermute(value, ("dp", "mp"), pairs)
    return value


def shards(tokens_in, gate_pre, up_pre, hidden_grad, out_grad, proj_model, proj_hidden):
    model_shards = lax.axis_size("mp")
    rows_each = WIDE // model_shards
    local_examples = tokens_in.shape[0] // LEN
    place = lax.axis_index("mp").astype(jnp.int32).reshape(1)
    part = project(
        gate_pre, up_pre, hidden_grad, proj_hidden, tokens_in, out_grad, proj_model
    )
    parts = [part]
    for away in range(1, model_shards):
        pairs = [(source, (source + away) % model_shards) for source in range(model_shards)]
        parts.append(lax.ppermute(part, "mp", pairs))
    rows, gram = gram_of(place, parts, rows_each)
    gram = summed_over_groups(gram)
    factor = math.sqrt(local_examples * lax.axis_size("dp") * 2 * RANK)
    return whiten(rows, gram, rows_each, factor)


def solution(mesh):
    in_specs = (
        P("dp", "mp"),
        P("dp", "mp"),
        P("dp", "mp"),
        P("dp", "mp"),
        P("dp", "mp"),
        P("mp", None),
        P("mp", None),
    )
    out_specs = P("dp", "mp", None)
    return jax.shard_map(shards, mesh=mesh, in_specs=in_specs, out_specs=out_specs, check_vma=False)
```

```python
import functools
import math

import jax
import jax.numpy as jnp
from jax import lax
from jax.experimental import pallas as pl
from jax.experimental.pallas import tpu as pltpu
from jax.sharding import PartitionSpec as P

RANK = 64
LEN = 128
WIDE = 2 * RANK
EACH = 1024
STEP = 256
AHEAD = 4

highest = lax.Precision.HIGHEST
whole_vmem = pl.BlockSpec(memory_space=pltpu.VMEM)
left_in_hbm = pl.BlockSpec(memory_space=pl.ANY)
small = pltpu.CompilerParams(vmem_limit_bytes=8 * 2**20)


def lanes_of(shape):
    return lax.broadcasted_iota(jnp.int32, shape, len(shape) - 1)


def project_kernel(gate, up, grad, proj_hidden, tokens, outer, proj_model, out, *rest):
    gate_v, up_v, grad_v, hidden_w, tokens_v, outer_v, model_w = rest[:7]
    hidden_sum, model_sum, sems, model_sems = rest[7:]
    rows = gate.shape[0]
    hidden_each, model_each = math.gcd(gate.shape[1], EACH), math.gcd(tokens.shape[1], EACH)
    hidden_count = gate.shape[1] // hidden_each
    model_count = tokens.shape[1] // model_each

    def hidden_copies(piece):
        cut = pl.ds(pl.multiple_of(piece * hidden_each, hidden_each), hidden_each)
        pairs = [
            (gate.at[:, cut], gate_v.at[:, cut]),
            (grad.at[:, cut], grad_v.at[:, cut]),
            (up.at[:, cut], up_v.at[:, cut]),
            (proj_hidden.at[cut, :], hidden_w.at[cut, :]),
        ]
        return [
            pltpu.make_async_copy(source, target, sems.at[piece, which])
            for which, (source, target) in enumerate(pairs)
        ]

    def model_copies(piece):
        cut = pl.ds(pl.multiple_of(piece * model_each, model_each), model_each)
        pairs = [
            (tokens.at[:, cut], tokens_v.at[:, cut]),
            (outer.at[:, cut], outer_v.at[:, cut]),
            (proj_model.at[cut, :], model_w.at[cut, :]),
        ]
        return [
            pltpu.make_async_copy(source, target, model_sems.at[piece, which])
            for which, (source, target) in enumerate(pairs)
        ]

    def start(copies):
        for copy in copies:
            copy.start()

    def arrive(copies):
        for copy in copies:
            copy.wait()

    ahead = min(AHEAD, hidden_count)
    for piece in range(ahead):
        start(hidden_copies(piece))
    hidden_sum[...] = jnp.zeros_like(hidden_sum)
    model_sum[...] = jnp.zeros_like(model_sum)

    @pl.loop(0, hidden_count)
    def _(piece):
        arrive(hidden_copies(piece))

        @pl.when(piece + ahead < hidden_count)
        def _():
            start(hidden_copies(piece + ahead))

        @pl.when(piece + ahead == hidden_count)
        def _():
            for other in range(model_count):
                start(model_copies(other))

        base = piece * hidden_each
        totals = []
        for first in range(0, hidden_each, STEP):
            step = min(STEP, hidden_each - first)
            cut = pl.ds(pl.multiple_of(base + first, 128), step)
            half = gate_v[:, cut].astype(jnp.float32) * 0.5
            act = half + half * jnp.tanh(half)
            up_grad = (grad_v[:, cut].astype(jnp.float32) * act).astype(jnp.bfloat16)
            hidden = (act * up_v[:, cut].astype(jnp.float32)).astype(jnp.bfloat16)
            weights = hidden_w[cut, :]
            parts = [
                jnp.dot(side, weights, preferred_element_type=jnp.float32)
                for side in (up_grad, hidden)
            ]
            totals = [old + new for old, new in zip(totals, parts)] if totals else parts
        for which, total in enumerate(totals):
            hidden_sum[which * rows : (which + 1) * rows, :] += total

    @pl.loop(0, model_count)
    def _(piece):
        arrive(model_copies(piece))
        cut = pl.ds(pl.multiple_of(piece * model_each, model_each), model_each)
        weights = model_w[cut, :]
        for which, side in enumerate((tokens_v, outer_v)):
            model_sum[which * rows : (which + 1) * rows, :] += jnp.dot(
                side[:, cut], weights, preferred_element_type=jnp.float32
            )

    low = lanes_of((rows, WIDE)) < RANK
    upward = pltpu.roll(hidden_sum[:rows, :], RANK, 1)
    hidden_side = pltpu.roll(hidden_sum[rows:, :], RANK, 1)
    out[:, :WIDE] = jnp.where(low, model_sum[:rows, :], upward)
    out[:, WIDE:] = jnp.where(low, hidden_side, model_sum[rows:, :])


def project(gate_pre, up_pre, hidden_grad, proj_hidden, tokens_in, out_grad, proj_model):
    rows, hidden_width = gate_pre.shape
    model_width = tokens_in.shape[1]
    held = jnp.bfloat16
    return pl.pallas_call(
        project_kernel,
        out_shape=jax.ShapeDtypeStruct((rows, 2 * WIDE), jnp.float32),
        in_specs=[left_in_hbm] * 7,
        out_specs=whole_vmem,
        scratch_shapes=[
            pltpu.VMEM((rows, hidden_width), held),
            pltpu.VMEM((rows, hidden_width), held),
            pltpu.VMEM((rows, hidden_width), held),
            pltpu.VMEM((hidden_width, WIDE), held),
            pltpu.VMEM((rows, model_width), held),
            pltpu.VMEM((rows, model_width), held),
            pltpu.VMEM((model_width, WIDE), held),
            pltpu.VMEM((2 * rows, WIDE), jnp.float32),
            pltpu.VMEM((2 * rows, WIDE), jnp.float32),
            pltpu.SemaphoreType.DMA((hidden_width // math.gcd(hidden_width, EACH), 4)),
            pltpu.SemaphoreType.DMA((model_width // math.gcd(model_width, EACH), 3)),
        ],
        compiler_params=pltpu.CompilerParams(vmem_limit_bytes=56 * 10**6),
        name="project",
    )(gate_pre, up_pre, hidden_grad, proj_hidden, tokens_in, out_grad, proj_model)


def gram_kernel(rows_each, count, *refs):
    place, parts, (rows_ref, gram_ref) = refs[0], refs[1 : 1 + count], refs[1 + count :]
    total = parts[0][...]
    for part in parts[1:]:
        total += part[...]
    row = lax.broadcasted_iota(jnp.int32, (WIDE, WIDE), 0)
    lane = lanes_of((WIDE, WIDE))
    low = lanes_of((RANK, WIDE)) < RANK
    gram = jnp.zeros((RANK, WIDE), jnp.float32)
    shift = lax.rem(WIDE - place[0] * rows_each, WIDE)
    for example in range(total.shape[0] // LEN):
        mixed = []
        for at in (0, WIDE):
            sides = total[example * LEN : (example + 1) * LEN, at : at + WIDE]
            crossed = jnp.dot(
                sides.T, sides, precision=highest, preferred_element_type=jnp.float32
            )
            mixed.append(jnp.where((row < RANK) != (lane < RANK), crossed, 0.0))
        up_block, down_block = mixed[0][RANK:], mixed[1][RANK:]
        across = jnp.where(low, up_block, pltpu.roll(down_block, RANK, 1))
        rows_ref[example] = jnp.where(low, pltpu.roll(across, shift, 1), 0.0)
        gram += jnp.dot(
            jnp.concatenate([up_block, down_block], axis=1),
            jnp.concatenate(mixed, axis=0),
            precision=highest,
            preferred_element_type=jnp.float32,
        )
    top, bottom = gram[: RANK // 2], gram[RANK // 2 :]
    gram_ref[...] = jnp.where(
        lanes_of(top.shape) < RANK, pltpu.roll(top, RANK, 1), bottom
    )


def gram_of(place, parts, rows_each):
    examples = parts[0].shape[0] // LEN
    return pl.pallas_call(
        functools.partial(gram_kernel, rows_each, len(parts)),
        out_shape=[
            jax.ShapeDtypeStruct((examples, RANK, WIDE), jnp.float32),
            jax.ShapeDtypeStruct((RANK // 2, WIDE), jnp.float32),
        ],
        in_specs=[pl.BlockSpec(memory_space=pltpu.SMEM)] + [whole_vmem] * len(parts),
        out_specs=[whole_vmem] * 2,
        compiler_params=small,
        name="gram",
    )(place, *parts)


def eliminated(state, spread):
    height = 8
    blocks = len(state)
    state = list(state)
    sub = lax.broadcasted_iota(jnp.int32, state[0].shape, 0)

    def across(block, at):
        return jnp.broadcast_to(block[:, at : at + 1], block.shape)

    def down(which, at):
        return spread[which, pl.ds(at, height, stride=0), :]

    done = []
    for held in range(blocks):
        base = RANK + held * height
        own = state[held]
        first_slot = (held % 2) * (height + 1)
        for k in range(height):
            spread[first_slot + k] = across(own, base + k)
        spread[first_slot + height] = own
        corner = {
            (k, m): down(first_slot + m, k) for k in range(height) for m in range(k, height)
        }
        rows = [down(first_slot + height, k) for k in range(height)]
        ahead = None
        if held + 1 < blocks:
            ahead = [across(state[held + 1], base + k) for k in range(height)]
        factors = {}
        solved = [None] * height
        for k in range(0, height, 2):
            first, cross, second = corner[k, k], corner[k, k + 1], corner[k + 1, k + 1]
            determinant = first * second - cross * cross
            inverse = pl.reciprocal(determinant, approx=True)
            solved[k] = (second * rows[k] - cross * rows[k + 1]) * inverse
            solved[k + 1] = (first * rows[k + 1] - cross * rows[k]) * inverse
            for m in range(k + 2, height):
                left, right = corner[k, m], corner[k + 1, m]
                upper = second * left - cross * right
                lower = first * right - cross * left
                for n in range(m, height):
                    taken = upper * corner[k, n] + lower * corner[k + 1, n]
                    corner[m, n] = corner[m, n] - taken * inverse
                factors[k, m], factors[k + 1, m] = upper * inverse, lower * inverse
                for several in (rows, ahead):
                    if several is not None:
                        several[m] = several[m] - (
                            factors[k, m] * several[k] + factors[k + 1, m] * several[k + 1]
                        )
        if ahead is not None:
            taken = [ahead[k] * solved[k] for k in range(height)]
            while len(taken) > 1:
                taken = [left + right for left, right in zip(taken[::2], taken[1::2])]
            state[held + 1] = state[held + 1] - taken[0]
        if held + 2 < blocks:
            back = list(solved)
            for m in reversed(range(2, height)):
                for k in range(m - m % 2):
                    back[k] = back[k] - factors[k, m] * back[m]
            packed = back[0]
            for k in range(1, height):
                packed = jnp.where(sub == k, back[k], packed)
            weights = [jnp.zeros_like(own)] * (2 * blocks)
            weights[blocks + held] = packed
            later = jnp.concatenate(state[held + 2 :], axis=0)
            later = later - jnp.dot(
                later,
                jnp.concatenate(weights, axis=0),
                precision=highest,
                preferred_element_type=jnp.float32,
            )
            for other in range(held + 2, blocks):
                at = (other - held - 2) * height
                state[other] = later[at : at + height]
        block = jnp.zeros_like(own)
        for k in range(0, height, 2):
            first, cross, second = corner[k, k], corner[k, k + 1], corner[k + 1, k + 1]
            ratio = cross * pl.reciprocal(first, approx=True)
            final = second - cross * ratio
            block = jnp.where(sub == k, rows[k] * lax.rsqrt(first), block)
            block = jnp.where(
                sub == k + 1, (rows[k + 1] - ratio * rows[k]) * lax.rsqrt(final), block
            )
        done.append(block)
    return done


def whiten_kernel(factor, rows_each, rows_ref, gram_ref, out_ref, spread):
    packed = gram_ref[...]
    gram = jnp.concatenate([pltpu.roll(packed, RANK, 1), packed], axis=0)
    low = lanes_of((RANK, WIDE)) < RANK
    for example in range(rows_ref.shape[0]):
        joined = jnp.where(low, rows_ref[example], gram)
        done = eliminated([joined[at : at + 8] for at in range(0, RANK, 8)], spread)
        solved = (jnp.concatenate(done, axis=0) * factor).T
        out_ref[example] = solved[:rows_each, :]


def whiten(rows, gram, rows_each, factor):
    return pl.pallas_call(
        functools.partial(whiten_kernel, factor, rows_each),
        out_shape=jax.ShapeDtypeStruct((rows.shape[0], rows_each, RANK), jnp.float32),
        in_specs=[whole_vmem] * 2,
        out_specs=whole_vmem,
        scratch_shapes=[pltpu.VMEM((18, 8, WIDE), jnp.float32)],
        compiler_params=small,
        name="whiten",
    )(rows, gram)


def summed_over_groups(value):
    groups, model_shards = lax.axis_size("dp"), lax.axis_size("mp")
    other = 1 if model_shards % 2 == 0 else 0
    for level in range(groups.bit_length() - 1):
        pairs = [
            (group * model_shards + shard, (group ^ 2**level) * model_shards + (shard ^ other))
            for group in range(groups)
            for shard in range(model_shards)
        ]
        value = value + lax.ppermute(value, ("dp", "mp"), pairs)
    return value


def shards(tokens_in, gate_pre, up_pre, hidden_grad, out_grad, proj_model, proj_hidden):
    model_shards = lax.axis_size("mp")
    rows_each = WIDE // model_shards
    local_examples = tokens_in.shape[0] // LEN
    place = lax.axis_index("mp").astype(jnp.int32).reshape(1)
    part = project(
        gate_pre, up_pre, hidden_grad, proj_hidden, tokens_in, out_grad, proj_model
    )
    parts = [part]
    for away in range(1, model_shards):
        pairs = [(source, (source + away) % model_shards) for source in range(model_shards)]
        parts.append(lax.ppermute(part, "mp", pairs))
    rows, gram = gram_of(place, parts, rows_each)
    gram = summed_over_groups(gram)
    factor = math.sqrt(local_examples * lax.axis_size("dp") * 2 * RANK)
    return whiten(rows, gram, rows_each, factor)


def solution(mesh):
    in_specs = (
        P("dp", "mp"),
        P("dp", "mp"),
        P("dp", "mp"),
        P("dp", "mp"),
        P("dp", "mp"),
        P("mp", None),
        P("mp", None),
    )
    out_specs = P("dp", "mp", None)
    return jax.shard_map(shards, mesh=mesh, in_specs=in_specs, out_specs=out_specs, check_vma=False)
```

```python
import functools
import math

import jax
import jax.numpy as jnp
from jax import lax
from jax.experimental import pallas as pl
from jax.experimental.pallas import tpu as pltpu
from jax.sharding import PartitionSpec as P

RANK = 64
LEN = 128
WIDE = 2 * RANK
EACH = 2048
STEP = 512
AHEAD = 3

highest = lax.Precision.HIGHEST
whole_vmem = pl.BlockSpec(memory_space=pltpu.VMEM)
left_in_hbm = pl.BlockSpec(memory_space=pl.ANY)
small = pltpu.CompilerParams(vmem_limit_bytes=8 * 2**20)


def cuts_of(width):
    ends = [min(EACH // 2, width)]
    while ends[-1] < width:
        ends.append(min(ends[-1] + EACH, width))
    return [(begin, end - begin) for begin, end in zip([0] + ends, ends)]


def lanes_of(shape):
    return lax.broadcasted_iota(jnp.int32, shape, len(shape) - 1)


def project_kernel(gate, up, grad, proj_hidden, tokens, outer, proj_model, out, *rest):
    gate_v, up_v, grad_v, hidden_w, tokens_v, outer_v, model_w = rest[:7]
    hidden_sum, model_sum, sems, model_sems = rest[7:]
    rows = gate.shape[0]
    hidden_cuts, model_cuts = cuts_of(gate.shape[1]), cuts_of(tokens.shape[1])

    copies = []
    for piece, (begin, size) in enumerate(hidden_cuts):
        cut = pl.ds(begin, size)
        pairs = [
            (gate.at[:, cut], gate_v.at[:, cut]),
            (grad.at[:, cut], grad_v.at[:, cut]),
            (up.at[:, cut], up_v.at[:, cut]),
            (proj_hidden.at[cut, :], hidden_w.at[cut, :]),
        ]
        copies.append(
            [
                pltpu.make_async_copy(source, target, sems.at[piece, which])
                for which, (source, target) in enumerate(pairs)
            ]
        )
    for piece, (begin, size) in enumerate(model_cuts):
        cut = pl.ds(begin, size)
        pairs = [
            (tokens.at[:, cut], tokens_v.at[:, cut]),
            (outer.at[:, cut], outer_v.at[:, cut]),
            (proj_model.at[cut, :], model_w.at[cut, :]),
        ]
        copies.append(
            [
                pltpu.make_async_copy(source, target, model_sems.at[piece, which])
                for which, (source, target) in enumerate(pairs)
            ]
        )

    def start(which):
        if which < len(copies):
            for copy in copies[which]:
                copy.start()

    def arrive(which):
        for copy in copies[which]:
            copy.wait()

    for which in range(AHEAD):
        start(which)
    hidden_sum[...] = jnp.zeros_like(hidden_sum)
    model_sum[...] = jnp.zeros_like(model_sum)

    for piece, (begin, size) in enumerate(hidden_cuts):
        arrive(piece)
        start(piece + AHEAD)
        step = math.gcd(STEP, size)

        @pl.loop(0, size // step)
        def _(part, begin=begin, step=step):
            cut = pl.ds(pl.multiple_of(begin + part * step, 128), step)
            half = (gate_v[:, cut] * 0.5).astype(jnp.float32)
            act = half + half * jnp.tanh(half)
            up_grad = (grad_v[:, cut].astype(jnp.float32) * act).astype(jnp.bfloat16)
            hidden = (act * up_v[:, cut].astype(jnp.float32)).astype(jnp.bfloat16)
            weights = hidden_w[cut, :]
            for which, side in enumerate((up_grad, hidden)):
                hidden_sum[which * rows : (which + 1) * rows, :] += jnp.dot(
                    side, weights, preferred_element_type=jnp.float32
                )

    for piece, (begin, size) in enumerate(model_cuts):
        arrive(len(hidden_cuts) + piece)
        start(len(hidden_cuts) + piece + AHEAD)
        cut = slice(begin, begin + size)
        weights = model_w[cut, :]
        for which, side in enumerate((tokens_v, outer_v)):
            model_sum[which * rows : (which + 1) * rows, :] += jnp.dot(
                side[:, cut], weights, preferred_element_type=jnp.float32
            )

    low = lanes_of((rows, WIDE)) < RANK
    upward = pltpu.roll(hidden_sum[:rows, :], RANK, 1)
    hidden_side = pltpu.roll(hidden_sum[rows:, :], RANK, 1)
    out[:, :WIDE] = jnp.where(low, model_sum[:rows, :], upward)
    out[:, WIDE:] = jnp.where(low, hidden_side, model_sum[rows:, :])


def project(gate_pre, up_pre, hidden_grad, proj_hidden, tokens_in, out_grad, proj_model):
    rows, hidden_width = gate_pre.shape
    model_width = tokens_in.shape[1]
    held = jnp.bfloat16
    return pl.pallas_call(
        project_kernel,
        out_shape=jax.ShapeDtypeStruct((rows, 2 * WIDE), jnp.float32),
        in_specs=[left_in_hbm] * 7,
        out_specs=whole_vmem,
        scratch_shapes=[
            pltpu.VMEM((rows, hidden_width), held),
            pltpu.VMEM((rows, hidden_width), held),
            pltpu.VMEM((rows, hidden_width), held),
            pltpu.VMEM((hidden_width, WIDE), held),
            pltpu.VMEM((rows, model_width), held),
            pltpu.VMEM((rows, model_width), held),
            pltpu.VMEM((model_width, WIDE), held),
            pltpu.VMEM((2 * rows, WIDE), jnp.float32),
            pltpu.VMEM((2 * rows, WIDE), jnp.float32),
            pltpu.SemaphoreType.DMA((len(cuts_of(hidden_width)), 4)),
            pltpu.SemaphoreType.DMA((len(cuts_of(model_width)), 3)),
        ],
        compiler_params=pltpu.CompilerParams(vmem_limit_bytes=56 * 10**6),
        name="project",
    )(gate_pre, up_pre, hidden_grad, proj_hidden, tokens_in, out_grad, proj_model)


def gram_kernel(rows_each, count, *refs):
    place, parts, (rows_ref, gram_ref) = refs[0], refs[1 : 1 + count], refs[1 + count :]
    total = parts[0][...]
    for part in parts[1:]:
        total += part[...]
    row = lax.broadcasted_iota(jnp.int32, (WIDE, WIDE), 0)
    lane = lanes_of((WIDE, WIDE))
    low = lanes_of((RANK, WIDE)) < RANK
    gram = jnp.zeros((RANK, WIDE), jnp.float32)
    shift = lax.rem(WIDE - place[0] * rows_each, WIDE)
    for example in range(total.shape[0] // LEN):
        mixed = []
        for at in (0, WIDE):
            sides = total[example * LEN : (example + 1) * LEN, at : at + WIDE]
            crossed = jnp.dot(
                sides.T, sides, precision=highest, preferred_element_type=jnp.float32
            )
            mixed.append(jnp.where((row < RANK) != (lane < RANK), crossed, 0.0))
        up_block, down_block = mixed[0][RANK:], mixed[1][RANK:]
        across = jnp.where(low, up_block, pltpu.roll(down_block, RANK, 1))
        rows_ref[example] = jnp.where(low, pltpu.roll(across, shift, 1), 0.0)
        gram += jnp.dot(
            jnp.concatenate([up_block, down_block], axis=1),
            jnp.concatenate(mixed, axis=0),
            precision=highest,
            preferred_element_type=jnp.float32,
        )
    top, bottom = gram[: RANK // 2], gram[RANK // 2 :]
    packed = jnp.where(lanes_of(top.shape) < RANK, pltpu.roll(top, RANK, 1), bottom)
    height = packed.shape[0] // count
    mine = packed[:height]
    for shard in range(1, count):
        block = packed[shard * height : (shard + 1) * height]
        mine = jnp.where(place[0] == shard, block, mine)
    for group in range(gram_ref.shape[0]):
        gram_ref[group] = mine


def gram_of(place, parts, rows_each):
    examples = parts[0].shape[0] // LEN
    return pl.pallas_call(
        functools.partial(gram_kernel, rows_each, len(parts)),
        out_shape=[
            jax.ShapeDtypeStruct((examples, RANK, WIDE), jnp.float32),
            jax.ShapeDtypeStruct(
                (lax.axis_size("dp"), RANK // 2 // len(parts), WIDE), jnp.float32
            ),
        ],
        in_specs=[pl.BlockSpec(memory_space=pltpu.SMEM)] + [whole_vmem] * len(parts),
        out_specs=[whole_vmem] * 2,
        compiler_params=small,
        name="gram",
    )(place, *parts)


def eliminated(state, spread):
    height = 8
    blocks = len(state)
    state = list(state)
    sub = lax.broadcasted_iota(jnp.int32, state[0].shape, 0)

    def across(block, at):
        return jnp.broadcast_to(block[:, at : at + 1], block.shape)

    def down(which, at):
        return spread[which, pl.ds(at, height, stride=0), :]

    done = []
    for held in range(blocks):
        base = RANK + held * height
        own = state[held]
        first_slot = (held % 2) * (height + 1)
        for k in range(height):
            spread[first_slot + k] = across(own, base + k)
        spread[first_slot + height] = own
        corner = {
            (k, m): down(first_slot + m, k) for k in range(height) for m in range(k, height)
        }
        rows = [down(first_slot + height, k) for k in range(height)]
        ahead = None
        if held + 1 < blocks:
            ahead = [across(state[held + 1], base + k) for k in range(height)]
        factors = {}
        solved = [None] * height
        for k in range(0, height, 2):
            first, cross, second = corner[k, k], corner[k, k + 1], corner[k + 1, k + 1]
            determinant = first * second - cross * cross
            inverse = pl.reciprocal(determinant, approx=True)
            solved[k] = (second * rows[k] - cross * rows[k + 1]) * inverse
            solved[k + 1] = (first * rows[k + 1] - cross * rows[k]) * inverse
            for m in range(k + 2, height):
                left, right = corner[k, m], corner[k + 1, m]
                upper = second * left - cross * right
                lower = first * right - cross * left
                for n in range(m, height):
                    taken = upper * corner[k, n] + lower * corner[k + 1, n]
                    corner[m, n] = corner[m, n] - taken * inverse
                factors[k, m], factors[k + 1, m] = upper * inverse, lower * inverse
                for several in (rows, ahead):
                    if several is not None:
                        several[m] = several[m] - (
                            factors[k, m] * several[k] + factors[k + 1, m] * several[k + 1]
                        )
        if ahead is not None:
            taken = [ahead[k] * solved[k] for k in range(height)]
            while len(taken) > 1:
                taken = [left + right for left, right in zip(taken[::2], taken[1::2])]
            state[held + 1] = state[held + 1] - taken[0]
        if held + 2 < blocks:
            back = list(solved)
            for m in reversed(range(2, height)):
                for k in range(m - m % 2):
                    back[k] = back[k] - factors[k, m] * back[m]
            packed = back[0]
            for k in range(1, height):
                packed = jnp.where(sub == k, back[k], packed)
            weights = [jnp.zeros_like(own)] * (2 * blocks)
            weights[blocks + held] = packed
            later = jnp.concatenate(state[held + 2 :], axis=0)
            later = later - jnp.dot(
                later,
                jnp.concatenate(weights, axis=0),
                precision=highest,
                preferred_element_type=jnp.float32,
            )
            for other in range(held + 2, blocks):
                at = (other - held - 2) * height
                state[other] = later[at : at + height]
        block = jnp.zeros_like(own)
        for k in range(0, height, 2):
            first, cross, second = corner[k, k], corner[k, k + 1], corner[k + 1, k + 1]
            ratio = cross * pl.reciprocal(first, approx=True)
            final = second - cross * ratio
            block = jnp.where(sub == k, rows[k] * lax.rsqrt(first), block)
            block = jnp.where(
                sub == k + 1, (rows[k + 1] - ratio * rows[k]) * lax.rsqrt(final), block
            )
        done.append(block)
    return done


def whiten_kernel(factor, rows_each, place, rows_ref, *refs):
    halves, (out_ref, spread) = refs[:-2], refs[-2:]
    count = len(halves)
    ordered = []
    for shard in range(count):
        block = halves[0][...]
        for away in range(1, count):
            block = jnp.where(place[0] == (shard + away) % count, halves[away][...], block)
        ordered.append(block)
    packed = jnp.concatenate(ordered, axis=0)
    gram = jnp.concatenate([pltpu.roll(packed, RANK, 1), packed], axis=0)
    low = lanes_of((RANK, WIDE)) < RANK
    for example in range(rows_ref.shape[0]):
        joined = jnp.where(low, rows_ref[example], gram)
        done = eliminated([joined[at : at + 8] for at in range(0, RANK, 8)], spread)
        solved = (jnp.concatenate(done, axis=0) * factor).T
        out_ref[example] = solved[:rows_each, :]


def whiten(place, rows, gram, rows_each, factor):
    return pl.pallas_call(
        functools.partial(whiten_kernel, factor, rows_each),
        out_shape=jax.ShapeDtypeStruct((rows.shape[0], rows_each, RANK), jnp.float32),
        in_specs=[pl.BlockSpec(memory_space=pltpu.SMEM)] + [whole_vmem] * (1 + len(gram)),
        out_specs=whole_vmem,
        scratch_shapes=[pltpu.VMEM((18, 8, WIDE), jnp.float32)],
        compiler_params=small,
        name="whiten",
    )(place, rows, *gram)


def summed_over_groups(copies):
    received = lax.all_to_all(copies, "dp", 0, 0, tiled=True)
    total = jnp.sum(received, axis=0)
    return [total] + from_shards(total)


def from_shards(value):
    shards = lax.axis_size("mp")
    return [
        lax.ppermute(value, "mp", [(source, (source + away) % shards) for source in range(shards)])
        for away in range(1, shards)
    ]


def shards(tokens_in, gate_pre, up_pre, hidden_grad, out_grad, proj_model, proj_hidden):
    rows_each = WIDE // lax.axis_size("mp")
    local_examples = tokens_in.shape[0] // LEN
    place = lax.axis_index("mp").astype(jnp.int32).reshape(1)
    part = project(
        gate_pre, up_pre, hidden_grad, proj_hidden, tokens_in, out_grad, proj_model
    )
    rows, copies = gram_of(place, [part] + from_shards(part), rows_each)
    gram = summed_over_groups(copies)
    factor = math.sqrt(local_examples * lax.axis_size("dp") * 2 * RANK)
    return whiten(place, rows, gram, rows_each, factor)


def solution(mesh):
    in_specs = (
        P("dp", "mp"),
        P("dp", "mp"),
        P("dp", "mp"),
        P("dp", "mp"),
        P("dp", "mp"),
        P("mp", None),
        P("mp", None),
    )
    out_specs = P("dp", "mp", None)
    return jax.shard_map(shards, mesh=mesh, in_specs=in_specs, out_specs=out_specs, check_vma=False)
```

```python
import functools
import math

import jax
import jax.numpy as jnp
from jax import lax
from jax.experimental import pallas as pl
from jax.experimental.pallas import tpu as pltpu
from jax.sharding import PartitionSpec as P

RANK = 64
LEN = 128
WIDE = 2 * RANK
EACH = 1024
STEP = 256
AHEAD = 4

highest = lax.Precision.HIGHEST
whole_vmem = pl.BlockSpec(memory_space=pltpu.VMEM)
left_in_hbm = pl.BlockSpec(memory_space=pl.ANY)
small = pltpu.CompilerParams(vmem_limit_bytes=8 * 2**20)


def lanes_of(shape):
    return lax.broadcasted_iota(jnp.int32, shape, len(shape) - 1)


def across_columns(weights, sides):
    return lax.dot_general(
        weights, sides, (((0,), (1,)), ((), ())), preferred_element_type=jnp.float32
    )


def project_kernel(gate, up, grad, proj_hidden, tokens, outer, proj_model, out, *rest):
    gate_v, up_v, grad_v, hidden_w, tokens_v, outer_v, model_w = rest[:7]
    hidden_sum, model_sum, sems, model_sems = rest[7:]
    rows = gate.shape[0]
    hidden_each, model_each = math.gcd(gate.shape[1], EACH), math.gcd(tokens.shape[1], EACH)
    hidden_count = gate.shape[1] // hidden_each
    model_count = tokens.shape[1] // model_each

    def hidden_copies(piece):
        cut = pl.ds(pl.multiple_of(piece * hidden_each, hidden_each), hidden_each)
        pairs = [
            (gate.at[:, cut], gate_v.at[:, cut]),
            (grad.at[:, cut], grad_v.at[:, cut]),
            (up.at[:, cut], up_v.at[:, cut]),
            (proj_hidden.at[cut, :], hidden_w.at[cut, :]),
        ]
        return [
            pltpu.make_async_copy(source, target, sems.at[piece, which])
            for which, (source, target) in enumerate(pairs)
        ]

    def model_copies(piece):
        cut = pl.ds(pl.multiple_of(piece * model_each, model_each), model_each)
        pairs = [
            (tokens.at[:, cut], tokens_v.at[:, cut]),
            (outer.at[:, cut], outer_v.at[:, cut]),
            (proj_model.at[cut, :], model_w.at[cut, :]),
        ]
        return [
            pltpu.make_async_copy(source, target, model_sems.at[piece, which])
            for which, (source, target) in enumerate(pairs)
        ]

    def start(copies):
        for copy in copies:
            copy.start()

    def arrive(copies):
        for copy in copies:
            copy.wait()

    ahead = min(AHEAD, hidden_count)
    for piece in range(ahead):
        start(hidden_copies(piece))
    hidden_sum[...] = jnp.zeros_like(hidden_sum)
    model_sum[...] = jnp.zeros_like(model_sum)

    @pl.loop(0, hidden_count)
    def _(piece):
        arrive(hidden_copies(piece))

        @pl.when(piece + ahead < hidden_count)
        def _():
            start(hidden_copies(piece + ahead))

        @pl.when(piece + ahead == hidden_count)
        def _():
            for other in range(model_count):
                start(model_copies(other))

        base = piece * hidden_each
        total = None
        for first in range(0, hidden_each, STEP):
            step = min(STEP, hidden_each - first)
            cut = pl.ds(pl.multiple_of(base + first, 128), step)
            half = gate_v[:, cut].astype(jnp.float32) * 0.5
            act = half + half * jnp.tanh(half)
            up_grad = (grad_v[:, cut].astype(jnp.float32) * act).astype(jnp.bfloat16)
            hidden = (act * up_v[:, cut].astype(jnp.float32)).astype(jnp.bfloat16)
            both = jnp.concatenate([up_grad, hidden], axis=0)
            part = across_columns(hidden_w[cut, :], both)
            total = part if total is None else total + part
        hidden_sum[...] += total

    @pl.loop(0, model_count)
    def _(piece):
        arrive(model_copies(piece))
        cut = pl.ds(pl.multiple_of(piece * model_each, model_each), model_each)
        both = jnp.concatenate([tokens_v[:, cut], outer_v[:, cut]], axis=0)
        model_sum[...] += across_columns(model_w[cut, :], both)

    out[:RANK, :] = model_sum[:RANK, :rows]
    out[RANK:WIDE, :] = hidden_sum[:RANK, :rows]
    out[WIDE : WIDE + RANK, :] = hidden_sum[RANK:, rows:]
    out[WIDE + RANK :, :] = model_sum[RANK:, rows:]


def project(gate_pre, up_pre, hidden_grad, proj_hidden, tokens_in, out_grad, proj_model):
    rows, hidden_width = gate_pre.shape
    model_width = tokens_in.shape[1]
    held = jnp.bfloat16
    return pl.pallas_call(
        project_kernel,
        out_shape=jax.ShapeDtypeStruct((2 * WIDE, rows), jnp.float32),
        in_specs=[left_in_hbm] * 7,
        out_specs=whole_vmem,
        scratch_shapes=[
            pltpu.VMEM((rows, hidden_width), held),
            pltpu.VMEM((rows, hidden_width), held),
            pltpu.VMEM((rows, hidden_width), held),
            pltpu.VMEM((hidden_width, WIDE), held),
            pltpu.VMEM((rows, model_width), held),
            pltpu.VMEM((rows, model_width), held),
            pltpu.VMEM((model_width, WIDE), held),
            pltpu.VMEM((WIDE, 2 * rows), jnp.float32),
            pltpu.VMEM((WIDE, 2 * rows), jnp.float32),
            pltpu.SemaphoreType.DMA((hidden_width // math.gcd(hidden_width, EACH), 4)),
            pltpu.SemaphoreType.DMA((model_width // math.gcd(model_width, EACH), 3)),
        ],
        compiler_params=pltpu.CompilerParams(vmem_limit_bytes=56 * 10**6),
        name="project",
    )(gate_pre, up_pre, hidden_grad, proj_hidden, tokens_in, out_grad, proj_model)


def gram_kernel(rows_each, count, *refs):
    place, parts, (rows_ref, gram_ref) = refs[0], refs[1 : 1 + count], refs[1 + count :]
    total = parts[0][...]
    for part in parts[1:]:
        total += part[...]
    row = lax.broadcasted_iota(jnp.int32, (WIDE, WIDE), 0)
    lane = lanes_of((WIDE, WIDE))
    low = lanes_of((RANK, WIDE)) < RANK
    gram = jnp.zeros((RANK, WIDE), jnp.float32)
    shift = lax.rem(WIDE - place[0] * rows_each, WIDE)
    for example in range(total.shape[1] // LEN):
        mixed = []
        for at in (0, WIDE):
            sides = total[at : at + WIDE, example * LEN : (example + 1) * LEN]
            crossed = lax.dot_general(
                sides,
                sides,
                (((1,), (1,)), ((), ())),
                precision=highest,
                preferred_element_type=jnp.float32,
            )
            mixed.append(jnp.where((row < RANK) != (lane < RANK), crossed, 0.0))
        up_block, down_block = mixed[0][RANK:], mixed[1][RANK:]
        across = jnp.where(low, up_block, pltpu.roll(down_block, RANK, 1))
        rows_ref[example] = jnp.where(low, pltpu.roll(across, shift, 1), 0.0)
        gram += jnp.dot(
            jnp.concatenate([up_block, down_block], axis=1),
            jnp.concatenate(mixed, axis=0),
            precision=highest,
            preferred_element_type=jnp.float32,
        )
    top, bottom = gram[: RANK // 2], gram[RANK // 2 :]
    gram_ref[...] = jnp.where(
        lanes_of(top.shape) < RANK, pltpu.roll(top, RANK, 1), bottom
    )


def gram_of(place, parts, rows_each):
    examples = parts[0].shape[1] // LEN
    return pl.pallas_call(
        functools.partial(gram_kernel, rows_each, len(parts)),
        out_shape=[
            jax.ShapeDtypeStruct((examples, RANK, WIDE), jnp.float32),
            jax.ShapeDtypeStruct((RANK // 2, WIDE), jnp.float32),
        ],
        in_specs=[pl.BlockSpec(memory_space=pltpu.SMEM)] + [whole_vmem] * len(parts),
        out_specs=[whole_vmem] * 2,
        compiler_params=small,
        name="gram",
    )(place, *parts)


def eliminated(state, spread):
    height = 8
    blocks = len(state)
    state = list(state)
    sub = lax.broadcasted_iota(jnp.int32, state[0].shape, 0)

    def across(block, at):
        return jnp.broadcast_to(block[:, at : at + 1], block.shape)

    def down(which, at):
        return spread[which, pl.ds(at, height, stride=0), :]

    done = []
    for held in range(blocks):
        base = RANK + held * height
        own = state[held]
        first_slot = (held % 2) * (height + 1)
        for k in range(height):
            spread[first_slot + k] = across(own, base + k)
        spread[first_slot + height] = own
        corner = {
            (k, m): down(first_slot + m, k) for k in range(height) for m in range(k, height)
        }
        rows = [down(first_slot + height, k) for k in range(height)]
        ahead = None
        if held + 1 < blocks:
            ahead = [across(state[held + 1], base + k) for k in range(height)]
        factors = {}
        solved = [None] * height
        for k in range(0, height, 2):
            first, cross, second = corner[k, k], corner[k, k + 1], corner[k + 1, k + 1]
            determinant = first * second - cross * cross
            inverse = pl.reciprocal(determinant, approx=True)
            solved[k] = (second * rows[k] - cross * rows[k + 1]) * inverse
            solved[k + 1] = (first * rows[k + 1] - cross * rows[k]) * inverse
            for m in range(k + 2, height):
                left, right = corner[k, m], corner[k + 1, m]
                upper = second * left - cross * right
                lower = first * right - cross * left
                for n in range(m, height):
                    taken = upper * corner[k, n] + lower * corner[k + 1, n]
                    corner[m, n] = corner[m, n] - taken * inverse
                factors[k, m], factors[k + 1, m] = upper * inverse, lower * inverse
                for several in (rows, ahead):
                    if several is not None:
                        several[m] = several[m] - (
                            factors[k, m] * several[k] + factors[k + 1, m] * several[k + 1]
                        )
        if ahead is not None:
            taken = [ahead[k] * solved[k] for k in range(height)]
            while len(taken) > 1:
                taken = [left + right for left, right in zip(taken[::2], taken[1::2])]
            state[held + 1] = state[held + 1] - taken[0]
        if held + 2 < blocks:
            back = list(solved)
            for m in reversed(range(2, height)):
                for k in range(m - m % 2):
                    back[k] = back[k] - factors[k, m] * back[m]
            packed = back[0]
            for k in range(1, height):
                packed = jnp.where(sub == k, back[k], packed)
            weights = [jnp.zeros_like(own)] * (2 * blocks)
            weights[blocks + held] = packed
            later = jnp.concatenate(state[held + 2 :], axis=0)
            later = later - jnp.dot(
                later,
                jnp.concatenate(weights, axis=0),
                precision=highest,
                preferred_element_type=jnp.float32,
            )
            for other in range(held + 2, blocks):
                at = (other - held - 2) * height
                state[other] = later[at : at + height]
        block = jnp.zeros_like(own)
        for k in range(0, height, 2):
            first, cross, second = corner[k, k], corner[k, k + 1], corner[k + 1, k + 1]
            ratio = cross * pl.reciprocal(first, approx=True)
            final = second - cross * ratio
            block = jnp.where(sub == k, rows[k] * lax.rsqrt(first), block)
            block = jnp.where(
                sub == k + 1, (rows[k + 1] - ratio * rows[k]) * lax.rsqrt(final), block
            )
        done.append(block)
    return done


def whiten_kernel(factor, rows_each, rows_ref, gram_ref, out_ref, spread):
    packed = gram_ref[...]
    gram = jnp.concatenate([pltpu.roll(packed, RANK, 1), packed], axis=0)
    low = lanes_of((RANK, WIDE)) < RANK
    for example in range(rows_ref.shape[0]):
        joined = jnp.where(low, rows_ref[example], gram)
        done = eliminated([joined[at : at + 8] for at in range(0, RANK, 8)], spread)
        solved = (jnp.concatenate(done, axis=0) * factor).T
        out_ref[example] = solved[:rows_each, :]


def whiten(rows, gram, rows_each, factor):
    return pl.pallas_call(
        functools.partial(whiten_kernel, factor, rows_each),
        out_shape=jax.ShapeDtypeStruct((rows.shape[0], rows_each, RANK), jnp.float32),
        in_specs=[whole_vmem] * 2,
        out_specs=whole_vmem,
        scratch_shapes=[pltpu.VMEM((18, 8, WIDE), jnp.float32)],
        compiler_params=small,
        name="whiten",
    )(rows, gram)


def summed_over_groups(value):
    groups, model_shards = lax.axis_size("dp"), lax.axis_size("mp")
    other = 1 if model_shards % 2 == 0 else 0
    for level in range(groups.bit_length() - 1):
        pairs = [
            (group * model_shards + shard, (group ^ 2**level) * model_shards + (shard ^ other))
            for group in range(groups)
            for shard in range(model_shards)
        ]
        value = value + lax.ppermute(value, ("dp", "mp"), pairs)
    return value


def shards(tokens_in, gate_pre, up_pre, hidden_grad, out_grad, proj_model, proj_hidden):
    model_shards = lax.axis_size("mp")
    rows_each = WIDE // model_shards
    local_examples = tokens_in.shape[0] // LEN
    place = lax.axis_index("mp").astype(jnp.int32).reshape(1)
    part = project(
        gate_pre, up_pre, hidden_grad, proj_hidden, tokens_in, out_grad, proj_model
    )
    parts = [part]
    for away in range(1, model_shards):
        pairs = [(source, (source + away) % model_shards) for source in range(model_shards)]
        parts.append(lax.ppermute(part, "mp", pairs))
    rows, gram = gram_of(place, parts, rows_each)
    gram = summed_over_groups(gram)
    factor = math.sqrt(local_examples * lax.axis_size("dp") * 2 * RANK)
    return whiten(rows, gram, rows_each, factor)


def solution(mesh):
    in_specs = (
        P("dp", "mp"),
        P("dp", "mp"),
        P("dp", "mp"),
        P("dp", "mp"),
        P("dp", "mp"),
        P("mp", None),
        P("mp", None),
    )
    out_specs = P("dp", "mp", None)
    return jax.shard_map(shards, mesh=mesh, in_specs=in_specs, out_specs=out_specs, check_vma=False)
```

```python
import functools
import math

import jax
import jax.numpy as jnp
from jax import lax
from jax.experimental import pallas as pl
from jax.experimental.pallas import tpu as pltpu
from jax.sharding import PartitionSpec as P

RANK = 64
LEN = 128
WIDE = 2 * RANK
EACH = 1024
STEP = 256
AHEAD = 4

highest = lax.Precision.HIGHEST
whole_vmem = pl.BlockSpec(memory_space=pltpu.VMEM)
left_in_hbm = pl.BlockSpec(memory_space=pl.ANY)
small = pltpu.CompilerParams(vmem_limit_bytes=8 * 2**20)


def lanes_of(shape):
    return lax.broadcasted_iota(jnp.int32, shape, len(shape) - 1)


def project_kernel(gate, up, grad, proj_hidden, tokens, outer, proj_model, out, *rest):
    gate_v, up_v, grad_v, hidden_w, tokens_v, outer_v, model_w = rest[:7]
    hidden_sum, model_sum, sems, model_sems = rest[7:]
    rows, hidden_width = gate.shape
    each = math.gcd(hidden_width, STEP)
    full, spare = divmod(hidden_width - each, EACH)
    model_each = math.gcd(tokens.shape[1], EACH)
    model_count = tokens.shape[1] // model_each

    def hidden_copies(piece, begin, size):
        cut = pl.ds(pl.multiple_of(begin, 128), size)
        pairs = [
            (gate.at[:, cut], gate_v.at[:, cut]),
            (grad.at[:, cut], grad_v.at[:, cut]),
            (up.at[:, cut], up_v.at[:, cut]),
            (proj_hidden.at[cut, :], hidden_w.at[cut, :]),
        ]
        return [
            pltpu.make_async_copy(source, target, sems.at[piece, which])
            for which, (source, target) in enumerate(pairs)
        ]

    def full_copies(piece):
        return hidden_copies(piece + 1, each + piece * EACH, EACH)

    def spare_copies():
        return hidden_copies(full + 1, each + full * EACH, spare) if spare else []

    def model_copies(piece):
        cut = pl.ds(pl.multiple_of(piece * model_each, model_each), model_each)
        pairs = [
            (tokens.at[:, cut], tokens_v.at[:, cut]),
            (outer.at[:, cut], outer_v.at[:, cut]),
            (proj_model.at[cut, :], model_w.at[cut, :]),
        ]
        return [
            pltpu.make_async_copy(source, target, model_sems.at[piece, which])
            for which, (source, target) in enumerate(pairs)
        ]

    def start(copies):
        for copy in copies:
            copy.start()

    def arrive(copies):
        for copy in copies:
            copy.wait()

    def gated(begin):
        cut = pl.ds(pl.multiple_of(begin, 128), each)
        half = (gate_v[:, cut] * 0.5).astype(jnp.float32)
        act = half + half * jnp.tanh(half)
        up_grad = (grad_v[:, cut].astype(jnp.float32) * act).astype(jnp.bfloat16)
        hidden = (act * up_v[:, cut].astype(jnp.float32)).astype(jnp.bfloat16)
        return up_grad, hidden

    def projected(begin, sides):
        weights = hidden_w[pl.ds(pl.multiple_of(begin, 128), each), :]
        return [jnp.dot(side, weights, preferred_element_type=jnp.float32) for side in sides]

    def advance(begin, size, sides):
        totals = None
        for first in range(0, size, each):
            parts = projected(begin + first - each, sides)
            totals = [old + new for old, new in zip(totals, parts)] if totals else parts
            sides = gated(begin + first)
        for which, total in enumerate(totals):
            hidden_sum[which * rows : (which + 1) * rows, :] += total
        return sides

    ahead = min(AHEAD, full)
    start(hidden_copies(0, 0, each))
    for piece in range(ahead):
        start(full_copies(piece))
    if not full:
        start(spare_copies())
        for other in range(model_count):
            start(model_copies(other))
    hidden_sum[...] = jnp.zeros_like(hidden_sum)
    model_sum[...] = jnp.zeros_like(model_sum)
    arrive(hidden_copies(0, 0, each))

    def body(piece, sides):
        arrive(full_copies(piece))

        @pl.when(piece + ahead < full)
        def _():
            start(full_copies(piece + ahead))

        @pl.when(piece + ahead == full)
        def _():
            start(spare_copies())
            for other in range(model_count):
                start(model_copies(other))

        return advance(each + piece * EACH, EACH, sides)

    sides = lax.fori_loop(0, full, body, gated(0))
    if spare:
        arrive(spare_copies())
        sides = advance(each + full * EACH, spare, sides)
    for which, total in enumerate(projected(hidden_width - each, sides)):
        hidden_sum[which * rows : (which + 1) * rows, :] += total

    @pl.loop(0, model_count)
    def _(piece):
        arrive(model_copies(piece))
        cut = pl.ds(pl.multiple_of(piece * model_each, model_each), model_each)
        weights = model_w[cut, :]
        for which, side in enumerate((tokens_v, outer_v)):
            model_sum[which * rows : (which + 1) * rows, :] += jnp.dot(
                side[:, cut], weights, preferred_element_type=jnp.float32
            )

    low = lanes_of((rows, WIDE)) < RANK
    upward = pltpu.roll(hidden_sum[:rows, :], RANK, 1)
    hidden_side = pltpu.roll(hidden_sum[rows:, :], RANK, 1)
    out[:, :WIDE] = jnp.where(low, model_sum[:rows, :], upward)
    out[:, WIDE:] = jnp.where(low, hidden_side, model_sum[rows:, :])


def project(gate_pre, up_pre, hidden_grad, proj_hidden, tokens_in, out_grad, proj_model):
    rows, hidden_width = gate_pre.shape
    model_width = tokens_in.shape[1]
    held = jnp.bfloat16
    return pl.pallas_call(
        project_kernel,
        out_shape=jax.ShapeDtypeStruct((rows, 2 * WIDE), jnp.float32),
        in_specs=[left_in_hbm] * 7,
        out_specs=whole_vmem,
        scratch_shapes=[
            pltpu.VMEM((rows, hidden_width), held),
            pltpu.VMEM((rows, hidden_width), held),
            pltpu.VMEM((rows, hidden_width), held),
            pltpu.VMEM((hidden_width, WIDE), held),
            pltpu.VMEM((rows, model_width), held),
            pltpu.VMEM((rows, model_width), held),
            pltpu.VMEM((model_width, WIDE), held),
            pltpu.VMEM((2 * rows, WIDE), jnp.float32),
            pltpu.VMEM((2 * rows, WIDE), jnp.float32),
            pltpu.SemaphoreType.DMA((hidden_width // EACH + 2, 4)),
            pltpu.SemaphoreType.DMA((model_width // math.gcd(model_width, EACH), 3)),
        ],
        compiler_params=pltpu.CompilerParams(vmem_limit_bytes=56 * 10**6),
        name="project",
    )(gate_pre, up_pre, hidden_grad, proj_hidden, tokens_in, out_grad, proj_model)


def gram_kernel(rows_each, count, *refs):
    place, parts, (rows_ref, gram_ref) = refs[0], refs[1 : 1 + count], refs[1 + count :]
    total = parts[0][...]
    for part in parts[1:]:
        total += part[...]
    row = lax.broadcasted_iota(jnp.int32, (WIDE, WIDE), 0)
    lane = lanes_of((WIDE, WIDE))
    low = lanes_of((RANK, WIDE)) < RANK
    gram = jnp.zeros((RANK, WIDE), jnp.float32)
    shift = lax.rem(WIDE - place[0] * rows_each, WIDE)
    for example in range(total.shape[0] // LEN):
        mixed = []
        for at in (0, WIDE):
            sides = total[example * LEN : (example + 1) * LEN, at : at + WIDE]
            crossed = jnp.dot(
                sides.T, sides, precision=highest, preferred_element_type=jnp.float32
            )
            mixed.append(jnp.where((row < RANK) != (lane < RANK), crossed, 0.0))
        up_block, down_block = mixed[0][RANK:], mixed[1][RANK:]
        across = jnp.where(low, up_block, pltpu.roll(down_block, RANK, 1))
        rows_ref[example] = jnp.where(low, pltpu.roll(across, shift, 1), 0.0)
        gram += jnp.dot(
            jnp.concatenate([up_block, down_block], axis=1),
            jnp.concatenate(mixed, axis=0),
            precision=highest,
            preferred_element_type=jnp.float32,
        )
    top, bottom = gram[: RANK // 2], gram[RANK // 2 :]
    gram_ref[...] = jnp.where(
        lanes_of(top.shape) < RANK, pltpu.roll(top, RANK, 1), bottom
    )


def gram_of(place, parts, rows_each):
    examples = parts[0].shape[0] // LEN
    return pl.pallas_call(
        functools.partial(gram_kernel, rows_each, len(parts)),
        out_shape=[
            jax.ShapeDtypeStruct((examples, RANK, WIDE), jnp.float32),
            jax.ShapeDtypeStruct((RANK // 2, WIDE), jnp.float32),
        ],
        in_specs=[pl.BlockSpec(memory_space=pltpu.SMEM)] + [whole_vmem] * len(parts),
        out_specs=[whole_vmem] * 2,
        compiler_params=small,
        name="gram",
    )(place, *parts)


def eliminated(state, spread):
    height = 8
    blocks = len(state)
    state = list(state)
    sub = lax.broadcasted_iota(jnp.int32, state[0].shape, 0)

    def across(block, at):
        return jnp.broadcast_to(block[:, at : at + 1], block.shape)

    def down(which, at):
        return spread[which, pl.ds(at, height, stride=0), :]

    done = []
    for held in range(blocks):
        base = RANK + held * height
        own = state[held]
        first_slot = (held % 2) * (height + 1)
        for k in range(height):
            spread[first_slot + k] = across(own, base + k)
        spread[first_slot + height] = own
        corner = {
            (k, m): down(first_slot + m, k) for k in range(height) for m in range(k, height)
        }
        rows = [down(first_slot + height, k) for k in range(height)]
        ahead = None
        if held + 1 < blocks:
            ahead = [across(state[held + 1], base + k) for k in range(height)]
        factors = {}
        solved = [None] * height
        for k in range(0, height, 2):
            first, cross, second = corner[k, k], corner[k, k + 1], corner[k + 1, k + 1]
            determinant = first * second - cross * cross
            inverse = pl.reciprocal(determinant, approx=True)
            solved[k] = (second * rows[k] - cross * rows[k + 1]) * inverse
            solved[k + 1] = (first * rows[k + 1] - cross * rows[k]) * inverse
            for m in range(k + 2, height):
                left, right = corner[k, m], corner[k + 1, m]
                upper = second * left - cross * right
                lower = first * right - cross * left
                for n in range(m, height):
                    taken = upper * corner[k, n] + lower * corner[k + 1, n]
                    corner[m, n] = corner[m, n] - taken * inverse
                factors[k, m], factors[k + 1, m] = upper * inverse, lower * inverse
                for several in (rows, ahead):
                    if several is not None:
                        several[m] = several[m] - (
                            factors[k, m] * several[k] + factors[k + 1, m] * several[k + 1]
                        )
        if ahead is not None:
            taken = [ahead[k] * solved[k] for k in range(height)]
            while len(taken) > 1:
                taken = [left + right for left, right in zip(taken[::2], taken[1::2])]
            state[held + 1] = state[held + 1] - taken[0]
        if held + 2 < blocks:
            back = list(solved)
            for m in reversed(range(2, height)):
                for k in range(m - m % 2):
                    back[k] = back[k] - factors[k, m] * back[m]
            packed = back[0]
            for k in range(1, height):
                packed = jnp.where(sub == k, back[k], packed)
            weights = [jnp.zeros_like(own)] * (2 * blocks)
            weights[blocks + held] = packed
            later = jnp.concatenate(state[held + 2 :], axis=0)
            later = later - jnp.dot(
                later,
                jnp.concatenate(weights, axis=0),
                precision=highest,
                preferred_element_type=jnp.float32,
            )
            for other in range(held + 2, blocks):
                at = (other - held - 2) * height
                state[other] = later[at : at + height]
        block = jnp.zeros_like(own)
        for k in range(0, height, 2):
            first, cross, second = corner[k, k], corner[k, k + 1], corner[k + 1, k + 1]
            ratio = cross * pl.reciprocal(first, approx=True)
            final = second - cross * ratio
            block = jnp.where(sub == k, rows[k] * lax.rsqrt(first), block)
            block = jnp.where(
                sub == k + 1, (rows[k + 1] - ratio * rows[k]) * lax.rsqrt(final), block
            )
        done.append(block)
    return done


def whiten_kernel(factor, rows_each, rows_ref, gram_ref, out_ref, spread):
    packed = gram_ref[...]
    gram = jnp.concatenate([pltpu.roll(packed, RANK, 1), packed], axis=0)
    low = lanes_of((RANK, WIDE)) < RANK
    for example in range(rows_ref.shape[0]):
        joined = jnp.where(low, rows_ref[example], gram)
        done = eliminated([joined[at : at + 8] for at in range(0, RANK, 8)], spread)
        solved = (jnp.concatenate(done, axis=0) * factor).T
        out_ref[example] = solved[:rows_each, :]


def whiten(rows, gram, rows_each, factor):
    return pl.pallas_call(
        functools.partial(whiten_kernel, factor, rows_each),
        out_shape=jax.ShapeDtypeStruct((rows.shape[0], rows_each, RANK), jnp.float32),
        in_specs=[whole_vmem] * 2,
        out_specs=whole_vmem,
        scratch_shapes=[pltpu.VMEM((18, 8, WIDE), jnp.float32)],
        compiler_params=small,
        name="whiten",
    )(rows, gram)


def summed_over_groups(value):
    groups, model_shards = lax.axis_size("dp"), lax.axis_size("mp")
    other = 1 if model_shards % 2 == 0 else 0
    for level in range(groups.bit_length() - 1):
        pairs = [
            (group * model_shards + shard, (group ^ 2**level) * model_shards + (shard ^ other))
            for group in range(groups)
            for shard in range(model_shards)
        ]
        value = value + lax.ppermute(value, ("dp", "mp"), pairs)
    return value


def shards(tokens_in, gate_pre, up_pre, hidden_grad, out_grad, proj_model, proj_hidden):
    model_shards = lax.axis_size("mp")
    rows_each = WIDE // model_shards
    local_examples = tokens_in.shape[0] // LEN
    place = lax.axis_index("mp").astype(jnp.int32).reshape(1)
    part = project(
        gate_pre, up_pre, hidden_grad, proj_hidden, tokens_in, out_grad, proj_model
    )
    parts = [part]
    for away in range(1, model_shards):
        pairs = [(source, (source + away) % model_shards) for source in range(model_shards)]
        parts.append(lax.ppermute(part, "mp", pairs))
    rows, gram = gram_of(place, parts, rows_each)
    gram = summed_over_groups(gram)
    factor = math.sqrt(local_examples * lax.axis_size("dp") * 2 * RANK)
    return whiten(rows, gram, rows_each, factor)


def solution(mesh):
    in_specs = (
        P("dp", "mp"),
        P("dp", "mp"),
        P("dp", "mp"),
        P("dp", "mp"),
        P("dp", "mp"),
        P("mp", None),
        P("mp", None),
    )
    out_specs = P("dp", "mp", None)
    return jax.shard_map(shards, mesh=mesh, in_specs=in_specs, out_specs=out_specs, check_vma=False)
```

```python
import functools
import math

import jax
import jax.numpy as jnp
from jax import lax
from jax.experimental import pallas as pl
from jax.experimental.pallas import tpu as pltpu
from jax.sharding import PartitionSpec as P

RANK = 64
LEN = 128
WIDE = 2 * RANK
EACH = 1024
STEP = 256
AHEAD = 8

highest = lax.Precision.HIGHEST
whole_vmem = pl.BlockSpec(memory_space=pltpu.VMEM)
left_in_hbm = pl.BlockSpec(memory_space=pl.ANY)
small = pltpu.CompilerParams(vmem_limit_bytes=8 * 2**20)


def lanes_of(shape):
    return lax.broadcasted_iota(jnp.int32, shape, len(shape) - 1)


def project_kernel(gate, up, grad, proj_hidden, tokens, outer, proj_model, out, *rest):
    gate_v, up_v, grad_v, hidden_w, tokens_v, outer_v, model_w = rest[:7]
    hidden_sum, model_sum, sems, model_sems = rest[7:]
    rows = gate.shape[0]
    hidden_each, model_each = math.gcd(gate.shape[1], EACH), math.gcd(tokens.shape[1], EACH)
    hidden_count = gate.shape[1] // hidden_each
    model_count = tokens.shape[1] // model_each

    def hidden_copies(piece):
        cut = pl.ds(pl.multiple_of(piece * hidden_each, hidden_each), hidden_each)
        pairs = [
            (gate.at[:, cut], gate_v.at[:, cut]),
            (grad.at[:, cut], grad_v.at[:, cut]),
            (up.at[:, cut], up_v.at[:, cut]),
            (proj_hidden.at[cut, :], hidden_w.at[cut, :]),
        ]
        return [
            pltpu.make_async_copy(source, target, sems.at[piece, which])
            for which, (source, target) in enumerate(pairs)
        ]

    def model_copies(piece):
        cut = pl.ds(pl.multiple_of(piece * model_each, model_each), model_each)
        pairs = [
            (tokens.at[:, cut], tokens_v.at[:, cut]),
            (outer.at[:, cut], outer_v.at[:, cut]),
            (proj_model.at[cut, :], model_w.at[cut, :]),
        ]
        return [
            pltpu.make_async_copy(source, target, model_sems.at[piece, which])
            for which, (source, target) in enumerate(pairs)
        ]

    def start(copies):
        for copy in copies:
            copy.start()

    def arrive(copies):
        for copy in copies:
            copy.wait()

    ahead = min(AHEAD, hidden_count)
    for piece in range(ahead):
        start(hidden_copies(piece))
    hidden_sum[...] = jnp.zeros_like(hidden_sum)
    model_sum[...] = jnp.zeros_like(model_sum)

    @pl.loop(0, hidden_count)
    def _(piece):
        arrive(hidden_copies(piece))

        @pl.when(piece + ahead < hidden_count)
        def _():
            start(hidden_copies(piece + ahead))

        @pl.when(piece + ahead == hidden_count)
        def _():
            for other in range(model_count):
                start(model_copies(other))

        base = piece * hidden_each
        totals = []
        for first in range(0, hidden_each, STEP):
            step = min(STEP, hidden_each - first)
            cut = pl.ds(pl.multiple_of(base + first, 128), step)
            half = gate_v[:, cut].astype(jnp.float32) * 0.5
            act = half + half * jnp.tanh(half)
            up_grad = (grad_v[:, cut].astype(jnp.float32) * act).astype(jnp.bfloat16)
            hidden = (act * up_v[:, cut].astype(jnp.float32)).astype(jnp.bfloat16)
            weights = hidden_w[cut, :]
            parts = [
                jnp.dot(side, weights, preferred_element_type=jnp.float32)
                for side in (up_grad, hidden)
            ]
            totals = [old + new for old, new in zip(totals, parts)] if totals else parts
        for which, total in enumerate(totals):
            hidden_sum[which * rows : (which + 1) * rows, :] += total

    @pl.loop(0, model_count)
    def _(piece):
        arrive(model_copies(piece))
        cut = pl.ds(pl.multiple_of(piece * model_each, model_each), model_each)
        weights = model_w[cut, :]
        for which, side in enumerate((tokens_v, outer_v)):
            model_sum[which * rows : (which + 1) * rows, :] += jnp.dot(
                side[:, cut], weights, preferred_element_type=jnp.float32
            )

    low = lanes_of((rows, WIDE)) < RANK
    upward = pltpu.roll(hidden_sum[:rows, :], RANK, 1)
    hidden_side = pltpu.roll(hidden_sum[rows:, :], RANK, 1)
    out[:, :WIDE] = jnp.where(low, model_sum[:rows, :], upward)
    out[:, WIDE:] = jnp.where(low, hidden_side, model_sum[rows:, :])


def project(gate_pre, up_pre, hidden_grad, proj_hidden, tokens_in, out_grad, proj_model):
    rows, hidden_width = gate_pre.shape
    model_width = tokens_in.shape[1]
    held = jnp.bfloat16
    return pl.pallas_call(
        project_kernel,
        out_shape=jax.ShapeDtypeStruct((rows, 2 * WIDE), jnp.float32),
        in_specs=[left_in_hbm] * 7,
        out_specs=whole_vmem,
        scratch_shapes=[
            pltpu.VMEM((rows, hidden_width), held),
            pltpu.VMEM((rows, hidden_width), held),
            pltpu.VMEM((rows, hidden_width), held),
            pltpu.VMEM((hidden_width, WIDE), held),
            pltpu.VMEM((rows, model_width), held),
            pltpu.VMEM((rows, model_width), held),
            pltpu.VMEM((model_width, WIDE), held),
            pltpu.VMEM((2 * rows, WIDE), jnp.float32),
            pltpu.VMEM((2 * rows, WIDE), jnp.float32),
            pltpu.SemaphoreType.DMA((hidden_width // math.gcd(hidden_width, EACH), 4)),
            pltpu.SemaphoreType.DMA((model_width // math.gcd(model_width, EACH), 3)),
        ],
        compiler_params=pltpu.CompilerParams(vmem_limit_bytes=56 * 10**6),
        name="project",
    )(gate_pre, up_pre, hidden_grad, proj_hidden, tokens_in, out_grad, proj_model)


def gram_kernel(rows_each, count, *refs):
    place, parts, (rows_ref, gram_ref) = refs[0], refs[1 : 1 + count], refs[1 + count :]
    total = parts[0][...]
    for part in parts[1:]:
        total += part[...]
    row = lax.broadcasted_iota(jnp.int32, (WIDE, WIDE), 0)
    lane = lanes_of((WIDE, WIDE))
    low = lanes_of((RANK, WIDE)) < RANK
    gram = jnp.zeros((RANK, WIDE), jnp.float32)
    shift = lax.rem(WIDE - place[0] * rows_each, WIDE)
    for example in range(total.shape[0] // LEN):
        mixed = []
        for at in (0, WIDE):
            sides = total[example * LEN : (example + 1) * LEN, at : at + WIDE]
            crossed = jnp.dot(
                sides.T, sides, precision=highest, preferred_element_type=jnp.float32
            )
            mixed.append(jnp.where((row < RANK) != (lane < RANK), crossed, 0.0))
        up_block, down_block = mixed[0][RANK:], mixed[1][RANK:]
        across = jnp.where(low, up_block, pltpu.roll(down_block, RANK, 1))
        rows_ref[example] = jnp.where(low, pltpu.roll(across, shift, 1), 0.0)
        gram += jnp.dot(
            jnp.concatenate([up_block, down_block], axis=1),
            jnp.concatenate(mixed, axis=0),
            precision=highest,
            preferred_element_type=jnp.float32,
        )
    top, bottom = gram[: RANK // 2], gram[RANK // 2 :]
    gram_ref[...] = jnp.where(
        lanes_of(top.shape) < RANK, pltpu.roll(top, RANK, 1), bottom
    )


def gram_of(place, parts, rows_each):
    examples = parts[0].shape[0] // LEN
    return pl.pallas_call(
        functools.partial(gram_kernel, rows_each, len(parts)),
        out_shape=[
            jax.ShapeDtypeStruct((examples, RANK, WIDE), jnp.float32),
            jax.ShapeDtypeStruct((RANK // 2, WIDE), jnp.float32),
        ],
        in_specs=[pl.BlockSpec(memory_space=pltpu.SMEM)] + [whole_vmem] * len(parts),
        out_specs=[whole_vmem] * 2,
        compiler_params=small,
        name="gram",
    )(place, *parts)


def eliminated(state, spread):
    height = 8
    blocks = len(state)
    state = list(state)
    sub = lax.broadcasted_iota(jnp.int32, state[0].shape, 0)

    def across(block, at):
        return jnp.broadcast_to(block[:, at : at + 1], block.shape)

    def down(which, at):
        return spread[which, pl.ds(at, height, stride=0), :]

    done = []
    for held in range(blocks):
        base = RANK + held * height
        own = state[held]
        first_slot = (held % 2) * (height + 1)
        for k in range(height):
            spread[first_slot + k] = across(own, base + k)
        spread[first_slot + height] = own
        corner = {
            (k, m): down(first_slot + m, k) for k in range(height) for m in range(k, height)
        }
        rows = [down(first_slot + height, k) for k in range(height)]
        ahead = None
        if held + 1 < blocks:
            ahead = [across(state[held + 1], base + k) for k in range(height)]
        factors = {}
        solved = [None] * height
        for k in range(0, height, 2):
            first, cross, second = corner[k, k], corner[k, k + 1], corner[k + 1, k + 1]
            determinant = first * second - cross * cross
            inverse = pl.reciprocal(determinant, approx=True)
            solved[k] = (second * rows[k] - cross * rows[k + 1]) * inverse
            solved[k + 1] = (first * rows[k + 1] - cross * rows[k]) * inverse
            for m in range(k + 2, height):
                left, right = corner[k, m], corner[k + 1, m]
                upper = second * left - cross * right
                lower = first * right - cross * left
                for n in range(m, height):
                    taken = upper * corner[k, n] + lower * corner[k + 1, n]
                    corner[m, n] = corner[m, n] - taken * inverse
                factors[k, m], factors[k + 1, m] = upper * inverse, lower * inverse
                for several in (rows, ahead):
                    if several is not None:
                        several[m] = several[m] - (
                            factors[k, m] * several[k] + factors[k + 1, m] * several[k + 1]
                        )
        if ahead is not None:
            taken = [ahead[k] * solved[k] for k in range(height)]
            while len(taken) > 1:
                taken = [left + right for left, right in zip(taken[::2], taken[1::2])]
            state[held + 1] = state[held + 1] - taken[0]
        if held + 2 < blocks:
            back = list(solved)
            for m in reversed(range(2, height)):
                for k in range(m - m % 2):
                    back[k] = back[k] - factors[k, m] * back[m]
            packed = back[0]
            for k in range(1, height):
                packed = jnp.where(sub == k, back[k], packed)
            weights = [jnp.zeros_like(own)] * (2 * blocks)
            weights[blocks + held] = packed
            later = jnp.concatenate(state[held + 2 :], axis=0)
            later = later - jnp.dot(
                later,
                jnp.concatenate(weights, axis=0),
                precision=highest,
                preferred_element_type=jnp.float32,
            )
            for other in range(held + 2, blocks):
                at = (other - held - 2) * height
                state[other] = later[at : at + height]
        block = jnp.zeros_like(own)
        for k in range(0, height, 2):
            first, cross, second = corner[k, k], corner[k, k + 1], corner[k + 1, k + 1]
            ratio = cross * pl.reciprocal(first, approx=True)
            final = second - cross * ratio
            block = jnp.where(sub == k, rows[k] * lax.rsqrt(first), block)
            block = jnp.where(
                sub == k + 1, (rows[k + 1] - ratio * rows[k]) * lax.rsqrt(final), block
            )
        done.append(block)
    return done


def whiten_kernel(factor, rows_each, rows_ref, gram_ref, out_ref, spread):
    packed = gram_ref[...]
    gram = jnp.concatenate([pltpu.roll(packed, RANK, 1), packed], axis=0)
    low = lanes_of((RANK, WIDE)) < RANK
    for example in range(rows_ref.shape[0]):
        joined = jnp.where(low, rows_ref[example], gram)
        done = eliminated([joined[at : at + 8] for at in range(0, RANK, 8)], spread)
        solved = (jnp.concatenate(done, axis=0) * factor).T
        out_ref[example] = solved[:rows_each, :]


def whiten(rows, gram, rows_each, factor):
    return pl.pallas_call(
        functools.partial(whiten_kernel, factor, rows_each),
        out_shape=jax.ShapeDtypeStruct((rows.shape[0], rows_each, RANK), jnp.float32),
        in_specs=[whole_vmem] * 2,
        out_specs=whole_vmem,
        scratch_shapes=[pltpu.VMEM((18, 8, WIDE), jnp.float32)],
        compiler_params=small,
        name="whiten",
    )(rows, gram)


def summed_over_groups(value):
    groups, model_shards = lax.axis_size("dp"), lax.axis_size("mp")
    place = lax.axis_index("mp")

    def over_groups(value):
        for level in range(groups.bit_length() - 1):
            pairs = [(source, source ^ 2**level) for source in range(groups)]
            value = value + lax.ppermute(value, "dp", pairs)
        return value

    value = lax.cond(place == model_shards - 1, over_groups, lambda value: value, value)
    result = value
    for away in range(1, model_shards):
        pairs = [(source, (source + away) % model_shards) for source in range(model_shards)]
        received = lax.ppermute(value, "mp", pairs)
        result = jnp.where(place == away - 1, received, result)
    return result


def shards(tokens_in, gate_pre, up_pre, hidden_grad, out_grad, proj_model, proj_hidden):
    model_shards = lax.axis_size("mp")
    rows_each = WIDE // model_shards
    local_examples = tokens_in.shape[0] // LEN
    place = lax.axis_index("mp").astype(jnp.int32).reshape(1)
    part = project(
        gate_pre, up_pre, hidden_grad, proj_hidden, tokens_in, out_grad, proj_model
    )
    parts = [part]
    for away in range(1, model_shards):
        pairs = [(source, (source + away) % model_shards) for source in range(model_shards)]
        parts.append(lax.ppermute(part, "mp", pairs))
    rows, gram = gram_of(place, parts, rows_each)
    gram = summed_over_groups(gram)
    factor = math.sqrt(local_examples * lax.axis_size("dp") * 2 * RANK)
    return whiten(rows, gram, rows_each, factor)


def solution(mesh):
    in_specs = (
        P("dp", "mp"),
        P("dp", "mp"),
        P("dp", "mp"),
        P("dp", "mp"),
        P("dp", "mp"),
        P("mp", None),
        P("mp", None),
    )
    out_specs = P("dp", "mp", None)
    return jax.shard_map(shards, mesh=mesh, in_specs=in_specs, out_specs=out_specs, check_vma=False)
```

```python
import functools
import math

import jax
import jax.numpy as jnp
from jax import lax
from jax.experimental import pallas as pl
from jax.experimental.pallas import tpu as pltpu
from jax.sharding import PartitionSpec as P

RANK = 64
LEN = 128
WIDE = 2 * RANK
EACH = 2048
MODEL_EACH = 512
STEP = 512
AHEAD = 4

highest = lax.Precision.HIGHEST
whole_vmem = pl.BlockSpec(memory_space=pltpu.VMEM)
left_in_hbm = pl.BlockSpec(memory_space=pl.ANY)
small = pltpu.CompilerParams(vmem_limit_bytes=8 * 2**20)


def lanes_of(shape):
    return lax.broadcasted_iota(jnp.int32, shape, len(shape) - 1)


def project_kernel(gate, up, grad, proj_hidden, tokens, outer, proj_model, out, *rest):
    gate_v, up_v, grad_v, hidden_w, tokens_v, outer_v, model_w = rest[:7]
    hidden_sum, model_sum, sems, model_sems = rest[7:]
    rows = gate.shape[0]
    hidden_each, model_each = math.gcd(gate.shape[1], EACH), math.gcd(tokens.shape[1], MODEL_EACH)
    hidden_count = gate.shape[1] // hidden_each
    model_count = tokens.shape[1] // model_each

    def hidden_copies(piece):
        cut = pl.ds(pl.multiple_of(piece * hidden_each, hidden_each), hidden_each)
        pairs = [
            (gate.at[:, cut], gate_v.at[:, cut]),
            (grad.at[:, cut], grad_v.at[:, cut]),
            (up.at[:, cut], up_v.at[:, cut]),
            (proj_hidden.at[cut, :], hidden_w.at[cut, :]),
        ]
        return [
            pltpu.make_async_copy(source, target, sems.at[piece, which])
            for which, (source, target) in enumerate(pairs)
        ]

    def model_copies(piece):
        cut = pl.ds(pl.multiple_of(piece * model_each, model_each), model_each)
        pairs = [
            (tokens.at[:, cut], tokens_v.at[:, cut]),
            (outer.at[:, cut], outer_v.at[:, cut]),
            (proj_model.at[cut, :], model_w.at[cut, :]),
        ]
        return [
            pltpu.make_async_copy(source, target, model_sems.at[piece, which])
            for which, (source, target) in enumerate(pairs)
        ]

    def start(copies):
        for copy in copies:
            copy.start()

    def arrive(copies):
        for copy in copies:
            copy.wait()

    ahead = min(AHEAD, hidden_count)
    for piece in range(ahead):
        start(hidden_copies(piece))
    hidden_sum[...] = jnp.zeros_like(hidden_sum)
    model_sum[...] = jnp.zeros_like(model_sum)

    @pl.loop(0, hidden_count)
    def _(piece):
        arrive(hidden_copies(piece))

        @pl.when(piece + ahead < hidden_count)
        def _():
            start(hidden_copies(piece + ahead))

        @pl.when(piece + ahead == hidden_count)
        def _():
            for other in range(model_count):
                start(model_copies(other))

        base = piece * hidden_each
        totals = []
        for first in range(0, hidden_each, STEP):
            step = min(STEP, hidden_each - first)
            cut = pl.ds(pl.multiple_of(base + first, 128), step)
            half = (gate_v[:, cut] * 0.5).astype(jnp.float32)
            act = half + half * jnp.tanh(half)
            up_grad = (grad_v[:, cut].astype(jnp.float32) * act).astype(jnp.bfloat16)
            hidden = (act * up_v[:, cut].astype(jnp.float32)).astype(jnp.bfloat16)
            weights = hidden_w[cut, :]
            parts = [
                jnp.dot(side, weights, preferred_element_type=jnp.float32)
                for side in (up_grad, hidden)
            ]
            totals = [old + new for old, new in zip(totals, parts)] if totals else parts
        for which, total in enumerate(totals):
            hidden_sum[which * rows : (which + 1) * rows, :] += total

    @pl.loop(0, model_count)
    def _(piece):
        arrive(model_copies(piece))
        cut = pl.ds(pl.multiple_of(piece * model_each, model_each), model_each)
        weights = model_w[cut, :]
        for which, side in enumerate((tokens_v, outer_v)):
            model_sum[which * rows : (which + 1) * rows, :] += jnp.dot(
                side[:, cut], weights, preferred_element_type=jnp.float32
            )

    low = lanes_of((rows, WIDE)) < RANK
    upward = pltpu.roll(hidden_sum[:rows, :], RANK, 1)
    hidden_side = pltpu.roll(hidden_sum[rows:, :], RANK, 1)
    out[:, :WIDE] = jnp.where(low, model_sum[:rows, :], upward)
    out[:, WIDE:] = jnp.where(low, hidden_side, model_sum[rows:, :])


def project(gate_pre, up_pre, hidden_grad, proj_hidden, tokens_in, out_grad, proj_model):
    rows, hidden_width = gate_pre.shape
    model_width = tokens_in.shape[1]
    held = jnp.bfloat16
    return pl.pallas_call(
        project_kernel,
        out_shape=jax.ShapeDtypeStruct((rows, 2 * WIDE), jnp.float32),
        in_specs=[left_in_hbm] * 7,
        out_specs=whole_vmem,
        scratch_shapes=[
            pltpu.VMEM((rows, hidden_width), held),
            pltpu.VMEM((rows, hidden_width), held),
            pltpu.VMEM((rows, hidden_width), held),
            pltpu.VMEM((hidden_width, WIDE), held),
            pltpu.VMEM((rows, model_width), held),
            pltpu.VMEM((rows, model_width), held),
            pltpu.VMEM((model_width, WIDE), held),
            pltpu.VMEM((2 * rows, WIDE), jnp.float32),
            pltpu.VMEM((2 * rows, WIDE), jnp.float32),
            pltpu.SemaphoreType.DMA((hidden_width // math.gcd(hidden_width, EACH), 4)),
            pltpu.SemaphoreType.DMA((model_width // math.gcd(model_width, MODEL_EACH), 3)),
        ],
        compiler_params=pltpu.CompilerParams(vmem_limit_bytes=56 * 10**6),
        name="project",
    )(gate_pre, up_pre, hidden_grad, proj_hidden, tokens_in, out_grad, proj_model)


def gram_kernel(rows_each, count, *refs):
    place, parts, (rows_ref, gram_ref) = refs[0], refs[1 : 1 + count], refs[1 + count :]
    total = parts[0][...]
    for part in parts[1:]:
        total += part[...]
    row = lax.broadcasted_iota(jnp.int32, (WIDE, WIDE), 0)
    lane = lanes_of((WIDE, WIDE))
    low = lanes_of((RANK, WIDE)) < RANK
    gram = jnp.zeros((RANK, WIDE), jnp.float32)
    shift = lax.rem(WIDE - place[0] * rows_each, WIDE)
    for example in range(total.shape[0] // LEN):
        mixed = []
        for at in (0, WIDE):
            sides = total[example * LEN : (example + 1) * LEN, at : at + WIDE]
            crossed = jnp.dot(
                sides.T, sides, precision=highest, preferred_element_type=jnp.float32
            )
            mixed.append(jnp.where((row < RANK) != (lane < RANK), crossed, 0.0))
        up_block, down_block = mixed[0][RANK:], mixed[1][RANK:]
        across = jnp.where(low, up_block, pltpu.roll(down_block, RANK, 1))
        rows_ref[example] = jnp.where(low, pltpu.roll(across, shift, 1), 0.0)
        gram += jnp.dot(
            jnp.concatenate([up_block, down_block], axis=1),
            jnp.concatenate(mixed, axis=0),
            precision=highest,
            preferred_element_type=jnp.float32,
        )
    top, bottom = gram[: RANK // 2], gram[RANK // 2 :]
    gram_ref[...] = jnp.where(
        lanes_of(top.shape) < RANK, pltpu.roll(top, RANK, 1), bottom
    )


def gram_of(place, parts, rows_each):
    examples = parts[0].shape[0] // LEN
    return pl.pallas_call(
        functools.partial(gram_kernel, rows_each, len(parts)),
        out_shape=[
            jax.ShapeDtypeStruct((examples, RANK, WIDE), jnp.float32),
            jax.ShapeDtypeStruct((RANK // 2, WIDE), jnp.float32),
        ],
        in_specs=[pl.BlockSpec(memory_space=pltpu.SMEM)] + [whole_vmem] * len(parts),
        out_specs=[whole_vmem] * 2,
        compiler_params=small,
        name="gram",
    )(place, *parts)


def eliminated(state, spread):
    height = 8
    blocks = len(state)
    state = list(state)
    sub = lax.broadcasted_iota(jnp.int32, state[0].shape, 0)

    def across(block, at):
        return jnp.broadcast_to(block[:, at : at + 1], block.shape)

    def down(which, at):
        return spread[which, pl.ds(at, height, stride=0), :]

    done = []
    for held in range(blocks):
        base = RANK + held * height
        own = state[held]
        first_slot = (held % 2) * (height + 1)
        for k in range(height):
            spread[first_slot + k] = across(own, base + k)
        spread[first_slot + height] = own
        corner = {
            (k, m): down(first_slot + m, k) for k in range(height) for m in range(k, height)
        }
        rows = [down(first_slot + height, k) for k in range(height)]
        ahead = None
        if held + 1 < blocks:
            ahead = [across(state[held + 1], base + k) for k in range(height)]
        factors = {}
        solved = [None] * height
        for k in range(0, height, 2):
            first, cross, second = corner[k, k], corner[k, k + 1], corner[k + 1, k + 1]
            determinant = first * second - cross * cross
            inverse = pl.reciprocal(determinant, approx=True)
            solved[k] = (second * rows[k] - cross * rows[k + 1]) * inverse
            solved[k + 1] = (first * rows[k + 1] - cross * rows[k]) * inverse
            for m in range(k + 2, height):
                left, right = corner[k, m], corner[k + 1, m]
                upper = second * left - cross * right
                lower = first * right - cross * left
                for n in range(m, height):
                    taken = upper * corner[k, n] + lower * corner[k + 1, n]
                    corner[m, n] = corner[m, n] - taken * inverse
                factors[k, m], factors[k + 1, m] = upper * inverse, lower * inverse
                for several in (rows, ahead):
                    if several is not None:
                        several[m] = several[m] - (
                            factors[k, m] * several[k] + factors[k + 1, m] * several[k + 1]
                        )
        if ahead is not None:
            taken = [ahead[k] * solved[k] for k in range(height)]
            while len(taken) > 1:
                taken = [left + right for left, right in zip(taken[::2], taken[1::2])]
            state[held + 1] = state[held + 1] - taken[0]
        if held + 2 < blocks:
            back = list(solved)
            for m in reversed(range(2, height)):
                for k in range(m - m % 2):
                    back[k] = back[k] - factors[k, m] * back[m]
            packed = back[0]
            for k in range(1, height):
                packed = jnp.where(sub == k, back[k], packed)
            weights = [jnp.zeros_like(own)] * (2 * blocks)
            weights[blocks + held] = packed
            later = jnp.concatenate(state[held + 2 :], axis=0)
            later = later - jnp.dot(
                later,
                jnp.concatenate(weights, axis=0),
                precision=highest,
                preferred_element_type=jnp.float32,
            )
            for other in range(held + 2, blocks):
                at = (other - held - 2) * height
                state[other] = later[at : at + height]
        block = jnp.zeros_like(own)
        for k in range(0, height, 2):
            first, cross, second = corner[k, k], corner[k, k + 1], corner[k + 1, k + 1]
            ratio = cross * pl.reciprocal(first, approx=True)
            final = second - cross * ratio
            block = jnp.where(sub == k, rows[k] * lax.rsqrt(first), block)
            block = jnp.where(
                sub == k + 1, (rows[k + 1] - ratio * rows[k]) * lax.rsqrt(final), block
            )
        done.append(block)
    return done


def whiten_kernel(factor, rows_each, rows_ref, gram_ref, out_ref, spread):
    packed = gram_ref[...]
    gram = jnp.concatenate([pltpu.roll(packed, RANK, 1), packed], axis=0)
    low = lanes_of((RANK, WIDE)) < RANK
    for example in range(rows_ref.shape[0]):
        joined = jnp.where(low, rows_ref[example], gram)
        done = eliminated([joined[at : at + 8] for at in range(0, RANK, 8)], spread)
        solved = (jnp.concatenate(done, axis=0) * factor).T
        out_ref[example] = solved[:rows_each, :]


def whiten(rows, gram, rows_each, factor):
    return pl.pallas_call(
        functools.partial(whiten_kernel, factor, rows_each),
        out_shape=jax.ShapeDtypeStruct((rows.shape[0], rows_each, RANK), jnp.float32),
        in_specs=[whole_vmem] * 2,
        out_specs=whole_vmem,
        scratch_shapes=[pltpu.VMEM((18, 8, WIDE), jnp.float32)],
        compiler_params=small,
        name="whiten",
    )(rows, gram)


def summed_over_groups(value):
    groups, model_shards = lax.axis_size("dp"), lax.axis_size("mp")
    place = lax.axis_index("mp")

    def over_groups(value):
        for level in range(groups.bit_length() - 1):
            pairs = [(source, source ^ 2**level) for source in range(groups)]
            value = value + lax.ppermute(value, "dp", pairs)
        return value

    value = lax.cond(place == model_shards - 1, over_groups, lambda value: value, value)
    result = value
    for away in range(1, model_shards):
        pairs = [(source, (source + away) % model_shards) for source in range(model_shards)]
        received = lax.ppermute(value, "mp", pairs)
        result = jnp.where(place == away - 1, received, result)
    return result


def shards(tokens_in, gate_pre, up_pre, hidden_grad, out_grad, proj_model, proj_hidden):
    model_shards = lax.axis_size("mp")
    rows_each = WIDE // model_shards
    local_examples = tokens_in.shape[0] // LEN
    place = lax.axis_index("mp").astype(jnp.int32).reshape(1)
    part = project(
        gate_pre, up_pre, hidden_grad, proj_hidden, tokens_in, out_grad, proj_model
    )
    parts = [part]
    for away in range(1, model_shards):
        pairs = [(source, (source + away) % model_shards) for source in range(model_shards)]
        parts.append(lax.ppermute(part, "mp", pairs))
    rows, gram = gram_of(place, parts, rows_each)
    gram = summed_over_groups(gram)
    factor = math.sqrt(local_examples * lax.axis_size("dp") * 2 * RANK)
    return whiten(rows, gram, rows_each, factor)


def solution(mesh):
    in_specs = (
        P("dp", "mp"),
        P("dp", "mp"),
        P("dp", "mp"),
        P("dp", "mp"),
        P("dp", "mp"),
        P("mp", None),
        P("mp", None),
    )
    out_specs = P("dp", "mp", None)
    return jax.shard_map(shards, mesh=mesh, in_specs=in_specs, out_specs=out_specs, check_vma=False)
```

```python
import functools
import math

import jax
import jax.numpy as jnp
from jax import lax
from jax.experimental import pallas as pl
from jax.experimental.pallas import tpu as pltpu
from jax.sharding import PartitionSpec as P

RANK = 64
LEN = 128
WIDE = 2 * RANK
EACH = 1024
STEP = 256
AHEAD = 8

highest = lax.Precision.HIGHEST
whole_vmem = pl.BlockSpec(memory_space=pltpu.VMEM)
left_in_hbm = pl.BlockSpec(memory_space=pl.ANY)
small = pltpu.CompilerParams(vmem_limit_bytes=8 * 2**20)


def lanes_of(shape):
    return lax.broadcasted_iota(jnp.int32, shape, len(shape) - 1)


def project_kernel(gate, up, grad, proj_hidden, tokens, outer, proj_model, out, *rest):
    gate_v, up_v, grad_v, hidden_w, tokens_v, outer_v, model_w = rest[:7]
    hidden_sum, model_sum, sems, model_sems = rest[7:]
    rows = gate.shape[0]
    hidden_each, model_each = math.gcd(gate.shape[1], EACH), math.gcd(tokens.shape[1], EACH)
    hidden_count = gate.shape[1] // hidden_each
    model_count = tokens.shape[1] // model_each

    def hidden_copies(piece):
        cut = pl.ds(pl.multiple_of(piece * hidden_each, hidden_each), hidden_each)
        pairs = [
            (gate.at[:, cut], gate_v.at[:, cut]),
            (grad.at[:, cut], grad_v.at[:, cut]),
            (up.at[:, cut], up_v.at[:, cut]),
            (proj_hidden.at[cut, :], hidden_w.at[cut, :]),
        ]
        return [
            pltpu.make_async_copy(source, target, sems.at[piece, which])
            for which, (source, target) in enumerate(pairs)
        ]

    def model_copies(piece):
        cut = pl.ds(pl.multiple_of(piece * model_each, model_each), model_each)
        pairs = [
            (tokens.at[:, cut], tokens_v.at[:, cut]),
            (outer.at[:, cut], outer_v.at[:, cut]),
            (proj_model.at[cut, :], model_w.at[cut, :]),
        ]
        return [
            pltpu.make_async_copy(source, target, model_sems.at[piece, which])
            for which, (source, target) in enumerate(pairs)
        ]

    def start(copies):
        for which, copy in enumerate(copies):
            copy.start(priority=which % 2)

    def arrive(copies):
        for copy in copies:
            copy.wait()

    ahead = min(AHEAD, hidden_count)
    for piece in range(ahead):
        start(hidden_copies(piece))
    hidden_sum[...] = jnp.zeros_like(hidden_sum)
    model_sum[...] = jnp.zeros_like(model_sum)

    @pl.loop(0, hidden_count)
    def _(piece):
        arrive(hidden_copies(piece))

        @pl.when(piece + ahead < hidden_count)
        def _():
            start(hidden_copies(piece + ahead))

        @pl.when(piece + ahead == hidden_count)
        def _():
            for other in range(model_count):
                start(model_copies(other))

        base = piece * hidden_each
        totals = []
        for first in range(0, hidden_each, STEP):
            step = min(STEP, hidden_each - first)
            cut = pl.ds(pl.multiple_of(base + first, 128), step)
            half = gate_v[:, cut].astype(jnp.float32) * 0.5
            act = half + half * jnp.tanh(half)
            up_grad = (grad_v[:, cut].astype(jnp.float32) * act).astype(jnp.bfloat16)
            hidden = (act * up_v[:, cut].astype(jnp.float32)).astype(jnp.bfloat16)
            weights = hidden_w[cut, :]
            parts = [
                jnp.dot(side, weights, preferred_element_type=jnp.float32)
                for side in (up_grad, hidden)
            ]
            totals = [old + new for old, new in zip(totals, parts)] if totals else parts
        for which, total in enumerate(totals):
            hidden_sum[which * rows : (which + 1) * rows, :] += total

    @pl.loop(0, model_count)
    def _(piece):
        arrive(model_copies(piece))
        cut = pl.ds(pl.multiple_of(piece * model_each, model_each), model_each)
        weights = model_w[cut, :]
        for which, side in enumerate((tokens_v, outer_v)):
            model_sum[which * rows : (which + 1) * rows, :] += jnp.dot(
                side[:, cut], weights, preferred_element_type=jnp.float32
            )

    low = lanes_of((rows, WIDE)) < RANK
    upward = pltpu.roll(hidden_sum[:rows, :], RANK, 1)
    hidden_side = pltpu.roll(hidden_sum[rows:, :], RANK, 1)
    out[:, :WIDE] = jnp.where(low, model_sum[:rows, :], upward)
    out[:, WIDE:] = jnp.where(low, hidden_side, model_sum[rows:, :])


def project(gate_pre, up_pre, hidden_grad, proj_hidden, tokens_in, out_grad, proj_model):
    rows, hidden_width = gate_pre.shape
    model_width = tokens_in.shape[1]
    held = jnp.bfloat16
    return pl.pallas_call(
        project_kernel,
        out_shape=jax.ShapeDtypeStruct((rows, 2 * WIDE), jnp.float32),
        in_specs=[left_in_hbm] * 7,
        out_specs=whole_vmem,
        scratch_shapes=[
            pltpu.VMEM((rows, hidden_width), held),
            pltpu.VMEM((rows, hidden_width), held),
            pltpu.VMEM((rows, hidden_width), held),
            pltpu.VMEM((hidden_width, WIDE), held),
            pltpu.VMEM((rows, model_width), held),
            pltpu.VMEM((rows, model_width), held),
            pltpu.VMEM((model_width, WIDE), held),
            pltpu.VMEM((2 * rows, WIDE), jnp.float32),
            pltpu.VMEM((2 * rows, WIDE), jnp.float32),
            pltpu.SemaphoreType.DMA((hidden_width // math.gcd(hidden_width, EACH), 4)),
            pltpu.SemaphoreType.DMA((model_width // math.gcd(model_width, EACH), 3)),
        ],
        compiler_params=pltpu.CompilerParams(vmem_limit_bytes=56 * 10**6),
        name="project",
    )(gate_pre, up_pre, hidden_grad, proj_hidden, tokens_in, out_grad, proj_model)


def gram_kernel(rows_each, count, *refs):
    place, parts, (rows_ref, gram_ref) = refs[0], refs[1 : 1 + count], refs[1 + count :]
    total = parts[0][...]
    for part in parts[1:]:
        total += part[...]
    row = lax.broadcasted_iota(jnp.int32, (WIDE, WIDE), 0)
    lane = lanes_of((WIDE, WIDE))
    low = lanes_of((RANK, WIDE)) < RANK
    gram = jnp.zeros((RANK, WIDE), jnp.float32)
    shift = lax.rem(WIDE - place[0] * rows_each, WIDE)
    for example in range(total.shape[0] // LEN):
        mixed = []
        for at in (0, WIDE):
            sides = total[example * LEN : (example + 1) * LEN, at : at + WIDE]
            crossed = jnp.dot(
                sides.T, sides, precision=highest, preferred_element_type=jnp.float32
            )
            mixed.append(jnp.where((row < RANK) != (lane < RANK), crossed, 0.0))
        up_block, down_block = mixed[0][RANK:], mixed[1][RANK:]
        across = jnp.where(low, up_block, pltpu.roll(down_block, RANK, 1))
        rows_ref[example] = jnp.where(low, pltpu.roll(across, shift, 1), 0.0)
        gram += jnp.dot(
            jnp.concatenate([up_block, down_block], axis=1),
            jnp.concatenate(mixed, axis=0),
            precision=highest,
            preferred_element_type=jnp.float32,
        )
    top, bottom = gram[: RANK // 2], gram[RANK // 2 :]
    gram_ref[...] = jnp.where(
        lanes_of(top.shape) < RANK, pltpu.roll(top, RANK, 1), bottom
    )


def gram_of(place, parts, rows_each):
    examples = parts[0].shape[0] // LEN
    return pl.pallas_call(
        functools.partial(gram_kernel, rows_each, len(parts)),
        out_shape=[
            jax.ShapeDtypeStruct((examples, RANK, WIDE), jnp.float32),
            jax.ShapeDtypeStruct((RANK // 2, WIDE), jnp.float32),
        ],
        in_specs=[pl.BlockSpec(memory_space=pltpu.SMEM)] + [whole_vmem] * len(parts),
        out_specs=[whole_vmem] * 2,
        compiler_params=small,
        name="gram",
    )(place, *parts)


def eliminated(state, spread):
    height = 8
    blocks = len(state)
    state = list(state)
    sub = lax.broadcasted_iota(jnp.int32, state[0].shape, 0)

    def across(block, at):
        return jnp.broadcast_to(block[:, at : at + 1], block.shape)

    def down(which, at):
        return spread[which, pl.ds(at, height, stride=0), :]

    done = []
    for held in range(blocks):
        base = RANK + held * height
        own = state[held]
        first_slot = (held % 2) * (height + 1)
        for k in range(height):
            spread[first_slot + k] = across(own, base + k)
        spread[first_slot + height] = own
        corner = {
            (k, m): down(first_slot + m, k) for k in range(height) for m in range(k, height)
        }
        rows = [down(first_slot + height, k) for k in range(height)]
        ahead = None
        if held + 1 < blocks:
            ahead = [across(state[held + 1], base + k) for k in range(height)]
        factors = {}
        solved = [None] * height
        for k in range(0, height, 2):
            first, cross, second = corner[k, k], corner[k, k + 1], corner[k + 1, k + 1]
            determinant = first * second - cross * cross
            inverse = pl.reciprocal(determinant, approx=True)
            solved[k] = (second * rows[k] - cross * rows[k + 1]) * inverse
            solved[k + 1] = (first * rows[k + 1] - cross * rows[k]) * inverse
            for m in range(k + 2, height):
                left, right = corner[k, m], corner[k + 1, m]
                upper = second * left - cross * right
                lower = first * right - cross * left
                for n in range(m, height):
                    taken = upper * corner[k, n] + lower * corner[k + 1, n]
                    corner[m, n] = corner[m, n] - taken * inverse
                factors[k, m], factors[k + 1, m] = upper * inverse, lower * inverse
                for several in (rows, ahead):
                    if several is not None:
                        several[m] = several[m] - (
                            factors[k, m] * several[k] + factors[k + 1, m] * several[k + 1]
                        )
        if ahead is not None:
            taken = [ahead[k] * solved[k] for k in range(height)]
            while len(taken) > 1:
                taken = [left + right for left, right in zip(taken[::2], taken[1::2])]
            state[held + 1] = state[held + 1] - taken[0]
        if held + 2 < blocks:
            back = list(solved)
            for m in reversed(range(2, height)):
                for k in range(m - m % 2):
                    back[k] = back[k] - factors[k, m] * back[m]
            packed = back[0]
            for k in range(1, height):
                packed = jnp.where(sub == k, back[k], packed)
            weights = [jnp.zeros_like(own)] * (2 * blocks)
            weights[blocks + held] = packed
            later = jnp.concatenate(state[held + 2 :], axis=0)
            later = later - jnp.dot(
                later,
                jnp.concatenate(weights, axis=0),
                precision=highest,
                preferred_element_type=jnp.float32,
            )
            for other in range(held + 2, blocks):
                at = (other - held - 2) * height
                state[other] = later[at : at + height]
        block = jnp.zeros_like(own)
        for k in range(0, height, 2):
            first, cross, second = corner[k, k], corner[k, k + 1], corner[k + 1, k + 1]
            ratio = cross * pl.reciprocal(first, approx=True)
            final = second - cross * ratio
            block = jnp.where(sub == k, rows[k] * lax.rsqrt(first), block)
            block = jnp.where(
                sub == k + 1, (rows[k + 1] - ratio * rows[k]) * lax.rsqrt(final), block
            )
        done.append(block)
    return done


def whiten_kernel(factor, rows_each, rows_ref, gram_ref, out_ref, spread):
    packed = gram_ref[...]
    gram = jnp.concatenate([pltpu.roll(packed, RANK, 1), packed], axis=0)
    low = lanes_of((RANK, WIDE)) < RANK
    for example in range(rows_ref.shape[0]):
        joined = jnp.where(low, rows_ref[example], gram)
        done = eliminated([joined[at : at + 8] for at in range(0, RANK, 8)], spread)
        solved = (jnp.concatenate(done, axis=0) * factor).T
        out_ref[example] = solved[:rows_each, :]


def whiten(rows, gram, rows_each, factor):
    return pl.pallas_call(
        functools.partial(whiten_kernel, factor, rows_each),
        out_shape=jax.ShapeDtypeStruct((rows.shape[0], rows_each, RANK), jnp.float32),
        in_specs=[whole_vmem] * 2,
        out_specs=whole_vmem,
        scratch_shapes=[pltpu.VMEM((18, 8, WIDE), jnp.float32)],
        compiler_params=small,
        name="whiten",
    )(rows, gram)


def summed_over_groups(value):
    groups, model_shards = lax.axis_size("dp"), lax.axis_size("mp")
    place = lax.axis_index("mp")

    def over_groups(value):
        for level in range(groups.bit_length() - 1):
            pairs = [(source, source ^ 2**level) for source in range(groups)]
            value = value + lax.ppermute(value, "dp", pairs)
        return value

    value = lax.cond(place == model_shards - 1, over_groups, lambda value: value, value)
    result = value
    for away in range(1, model_shards):
        pairs = [(source, (source + away) % model_shards) for source in range(model_shards)]
        received = lax.ppermute(value, "mp", pairs)
        result = jnp.where(place == away - 1, received, result)
    return result


def shards(tokens_in, gate_pre, up_pre, hidden_grad, out_grad, proj_model, proj_hidden):
    model_shards = lax.axis_size("mp")
    rows_each = WIDE // model_shards
    local_examples = tokens_in.shape[0] // LEN
    place = lax.axis_index("mp").astype(jnp.int32).reshape(1)
    part = project(
        gate_pre, up_pre, hidden_grad, proj_hidden, tokens_in, out_grad, proj_model
    )
    parts = [part]
    for away in range(1, model_shards):
        pairs = [(source, (source + away) % model_shards) for source in range(model_shards)]
        parts.append(lax.ppermute(part, "mp", pairs))
    rows, gram = gram_of(place, parts, rows_each)
    gram = summed_over_groups(gram)
    factor = math.sqrt(local_examples * lax.axis_size("dp") * 2 * RANK)
    return whiten(rows, gram, rows_each, factor)


def solution(mesh):
    in_specs = (
        P("dp", "mp"),
        P("dp", "mp"),
        P("dp", "mp"),
        P("dp", "mp"),
        P("dp", "mp"),
        P("mp", None),
        P("mp", None),
    )
    out_specs = P("dp", "mp", None)
    return jax.shard_map(shards, mesh=mesh, in_specs=in_specs, out_specs=out_specs, check_vma=False)
```

```python
import functools
import math

import jax
import jax.numpy as jnp
from jax import lax
from jax.experimental import pallas as pl
from jax.experimental.pallas import tpu as pltpu
from jax.sharding import PartitionSpec as P

RANK = 64
LEN = 128
WIDE = 2 * RANK
EACH = 2048
HEAD = 512
MODEL_EACH = 1024
STEP = 256
AHEAD = 3

highest = lax.Precision.HIGHEST
whole_vmem = pl.BlockSpec(memory_space=pltpu.VMEM)
left_in_hbm = pl.BlockSpec(memory_space=pl.ANY)
small = pltpu.CompilerParams(vmem_limit_bytes=8 * 2**20)


def cuts_of(width):
    full = max((width - 1) // EACH, 0)
    head = width - full * EACH
    ends = [0, min(HEAD, head)]
    while ends[-1] < head:
        ends.append(min(ends[-1] + EACH // 2, head))
    return [(begin, end - begin) for begin, end in zip(ends, ends[1:])], full


def lanes_of(shape):
    return lax.broadcasted_iota(jnp.int32, shape, len(shape) - 1)


def project_kernel(gate, up, grad, proj_hidden, tokens, outer, proj_model, out, *rest):
    gate_v, up_v, grad_v, hidden_w, tokens_v, outer_v, model_w = rest[:7]
    hidden_sum, model_sum, sems, model_sems = rest[7:]
    rows = gate.shape[0]
    model_each = math.gcd(tokens.shape[1], MODEL_EACH)
    model_count = tokens.shape[1] // model_each
    head, full = cuts_of(gate.shape[1])
    head_width = gate.shape[1] - full * EACH

    def hidden_copies(slot, begin, size):
        cut = pl.ds(pl.multiple_of(begin, 128), size)
        pairs = [
            (gate.at[:, cut], gate_v.at[:, cut]),
            (grad.at[:, cut], grad_v.at[:, cut]),
            (up.at[:, cut], up_v.at[:, cut]),
            (proj_hidden.at[cut, :], hidden_w.at[cut, :]),
        ]
        return [
            pltpu.make_async_copy(source, target, sems.at[slot, which])
            for which, (source, target) in enumerate(pairs)
        ]

    def full_copies(piece):
        return hidden_copies(len(head) + piece, head_width + piece * EACH, EACH)

    def model_copies(piece):
        cut = pl.ds(pl.multiple_of(piece * model_each, model_each), model_each)
        pairs = [
            (tokens.at[:, cut], tokens_v.at[:, cut]),
            (outer.at[:, cut], outer_v.at[:, cut]),
            (proj_model.at[cut, :], model_w.at[cut, :]),
        ]
        return [
            pltpu.make_async_copy(source, target, model_sems.at[piece, which])
            for which, (source, target) in enumerate(pairs)
        ]

    def start(copies):
        for copy in copies:
            copy.start()

    def arrive(copies):
        for copy in copies:
            copy.wait()

    def start_models():
        for other in range(model_count):
            start(model_copies(other))

    def advance(begin, size):
        totals = []
        for first in range(0, size, STEP):
            step = min(STEP, size - first)
            cut = pl.ds(pl.multiple_of(begin + first, 128), step)
            half = (gate_v[:, cut] * 0.5).astype(jnp.float32)
            act = half + half * jnp.tanh(half)
            up_grad = (grad_v[:, cut].astype(jnp.float32) * act).astype(jnp.bfloat16)
            hidden = (act * up_v[:, cut].astype(jnp.float32)).astype(jnp.bfloat16)
            weights = hidden_w[cut, :]
            parts = [
                jnp.dot(side, weights, preferred_element_type=jnp.float32)
                for side in (up_grad, hidden)
            ]
            totals = [old + new for old, new in zip(totals, parts)] if totals else parts
        for which, total in enumerate(totals):
            hidden_sum[which * rows : (which + 1) * rows, :] += total

    ahead = min(AHEAD, full)
    for slot, (begin, size) in enumerate(head):
        start(hidden_copies(slot, begin, size))
    for piece in range(ahead):
        start(full_copies(piece))
    if not full:
        start_models()
    hidden_sum[...] = jnp.zeros_like(hidden_sum)
    model_sum[...] = jnp.zeros_like(model_sum)
    for slot, (begin, size) in enumerate(head):
        arrive(hidden_copies(slot, begin, size))
        advance(begin, size)

    @pl.loop(0, full)
    def _(piece):
        arrive(full_copies(piece))

        @pl.when(piece + ahead < full)
        def _():
            start(full_copies(piece + ahead))

        @pl.when(piece + ahead == full)
        def _():
            start_models()

        advance(head_width + piece * EACH, EACH)

    @pl.loop(0, model_count)
    def _(piece):
        arrive(model_copies(piece))
        cut = pl.ds(pl.multiple_of(piece * model_each, model_each), model_each)
        weights = model_w[cut, :]
        for which, side in enumerate((tokens_v, outer_v)):
            model_sum[which * rows : (which + 1) * rows, :] += jnp.dot(
                side[:, cut], weights, preferred_element_type=jnp.float32
            )

    low = lanes_of((rows, WIDE)) < RANK
    upward = pltpu.roll(hidden_sum[:rows, :], RANK, 1)
    hidden_side = pltpu.roll(hidden_sum[rows:, :], RANK, 1)
    out[:, :WIDE] = jnp.where(low, model_sum[:rows, :], upward)
    out[:, WIDE:] = jnp.where(low, hidden_side, model_sum[rows:, :])


def project(gate_pre, up_pre, hidden_grad, proj_hidden, tokens_in, out_grad, proj_model):
    rows, hidden_width = gate_pre.shape
    model_width = tokens_in.shape[1]
    head, full = cuts_of(hidden_width)
    hidden_slots = len(head) + full
    held = jnp.bfloat16
    return pl.pallas_call(
        project_kernel,
        out_shape=jax.ShapeDtypeStruct((rows, 2 * WIDE), jnp.float32),
        in_specs=[left_in_hbm] * 7,
        out_specs=whole_vmem,
        scratch_shapes=[
            pltpu.VMEM((rows, hidden_width), held),
            pltpu.VMEM((rows, hidden_width), held),
            pltpu.VMEM((rows, hidden_width), held),
            pltpu.VMEM((hidden_width, WIDE), held),
            pltpu.VMEM((rows, model_width), held),
            pltpu.VMEM((rows, model_width), held),
            pltpu.VMEM((model_width, WIDE), held),
            pltpu.VMEM((2 * rows, WIDE), jnp.float32),
            pltpu.VMEM((2 * rows, WIDE), jnp.float32),
            pltpu.SemaphoreType.DMA((hidden_slots, 4)),
            pltpu.SemaphoreType.DMA((model_width // math.gcd(model_width, MODEL_EACH), 3)),
        ],
        compiler_params=pltpu.CompilerParams(vmem_limit_bytes=56 * 10**6),
        name="project",
    )(gate_pre, up_pre, hidden_grad, proj_hidden, tokens_in, out_grad, proj_model)


def gram_kernel(rows_each, count, *refs):
    place, parts, (rows_ref, gram_ref) = refs[0], refs[1 : 1 + count], refs[1 + count :]
    total = parts[0][...]
    for part in parts[1:]:
        total += part[...]
    row = lax.broadcasted_iota(jnp.int32, (WIDE, WIDE), 0)
    lane = lanes_of((WIDE, WIDE))
    low = lanes_of((RANK, WIDE)) < RANK
    gram = jnp.zeros((RANK, WIDE), jnp.float32)
    shift = lax.rem(WIDE - place[0] * rows_each, WIDE)
    for example in range(total.shape[0] // LEN):
        mixed = []
        for at in (0, WIDE):
            sides = total[example * LEN : (example + 1) * LEN, at : at + WIDE]
            crossed = jnp.dot(
                sides.T, sides, precision=highest, preferred_element_type=jnp.float32
            )
            mixed.append(jnp.where((row < RANK) != (lane < RANK), crossed, 0.0))
        up_block, down_block = mixed[0][RANK:], mixed[1][RANK:]
        across = jnp.where(low, up_block, pltpu.roll(down_block, RANK, 1))
        rows_ref[example] = jnp.where(low, pltpu.roll(across, shift, 1), 0.0)
        gram += jnp.dot(
            jnp.concatenate([up_block, down_block], axis=1),
            jnp.concatenate(mixed, axis=0),
            precision=highest,
            preferred_element_type=jnp.float32,
        )
    top, bottom = gram[: RANK // 2], gram[RANK // 2 :]
    gram_ref[...] = jnp.where(
        lanes_of(top.shape) < RANK, pltpu.roll(top, RANK, 1), bottom
    )


def gram_of(place, parts, rows_each):
    examples = parts[0].shape[0] // LEN
    return pl.pallas_call(
        functools.partial(gram_kernel, rows_each, len(parts)),
        out_shape=[
            jax.ShapeDtypeStruct((examples, RANK, WIDE), jnp.float32),
            jax.ShapeDtypeStruct((RANK // 2, WIDE), jnp.float32),
        ],
        in_specs=[pl.BlockSpec(memory_space=pltpu.SMEM)] + [whole_vmem] * len(parts),
        out_specs=[whole_vmem] * 2,
        compiler_params=small,
        name="gram",
    )(place, *parts)


def eliminated(state, spread):
    height = 8
    blocks = len(state)
    state = list(state)
    sub = lax.broadcasted_iota(jnp.int32, state[0].shape, 0)

    def across(block, at):
        return jnp.broadcast_to(block[:, at : at + 1], block.shape)

    def down(which, at):
        return spread[which, pl.ds(at, height, stride=0), :]

    done = []
    for held in range(blocks):
        base = RANK + held * height
        own = state[held]
        first_slot = (held % 2) * (height + 1)
        for k in range(height):
            spread[first_slot + k] = across(own, base + k)
        spread[first_slot + height] = own
        corner = {
            (k, m): down(first_slot + m, k) for k in range(height) for m in range(k, height)
        }
        rows = [down(first_slot + height, k) for k in range(height)]
        ahead = None
        if held + 1 < blocks:
            ahead = [across(state[held + 1], base + k) for k in range(height)]
        factors = {}
        solved = [None] * height
        for k in range(0, height, 2):
            first, cross, second = corner[k, k], corner[k, k + 1], corner[k + 1, k + 1]
            determinant = first * second - cross * cross
            inverse = pl.reciprocal(determinant, approx=True)
            solved[k] = (second * rows[k] - cross * rows[k + 1]) * inverse
            solved[k + 1] = (first * rows[k + 1] - cross * rows[k]) * inverse
            for m in range(k + 2, height):
                left, right = corner[k, m], corner[k + 1, m]
                upper = second * left - cross * right
                lower = first * right - cross * left
                for n in range(m, height):
                    taken = upper * corner[k, n] + lower * corner[k + 1, n]
                    corner[m, n] = corner[m, n] - taken * inverse
                factors[k, m], factors[k + 1, m] = upper * inverse, lower * inverse
                for several in (rows, ahead):
                    if several is not None:
                        several[m] = several[m] - (
                            factors[k, m] * several[k] + factors[k + 1, m] * several[k + 1]
                        )
        if ahead is not None:
            taken = [ahead[k] * solved[k] for k in range(height)]
            while len(taken) > 1:
                taken = [left + right for left, right in zip(taken[::2], taken[1::2])]
            state[held + 1] = state[held + 1] - taken[0]
        if held + 2 < blocks:
            back = list(solved)
            for m in reversed(range(2, height)):
                for k in range(m - m % 2):
                    back[k] = back[k] - factors[k, m] * back[m]
            packed = back[0]
            for k in range(1, height):
                packed = jnp.where(sub == k, back[k], packed)
            weights = [jnp.zeros_like(own)] * (2 * blocks)
            weights[blocks + held] = packed
            later = jnp.concatenate(state[held + 2 :], axis=0)
            later = later - jnp.dot(
                later,
                jnp.concatenate(weights, axis=0),
                precision=highest,
                preferred_element_type=jnp.float32,
            )
            for other in range(held + 2, blocks):
                at = (other - held - 2) * height
                state[other] = later[at : at + height]
        block = jnp.zeros_like(own)
        for k in range(0, height, 2):
            first, cross, second = corner[k, k], corner[k, k + 1], corner[k + 1, k + 1]
            ratio = cross * pl.reciprocal(first, approx=True)
            final = second - cross * ratio
            block = jnp.where(sub == k, rows[k] * lax.rsqrt(first), block)
            block = jnp.where(
                sub == k + 1, (rows[k + 1] - ratio * rows[k]) * lax.rsqrt(final), block
            )
        done.append(block)
    return done


def whiten_kernel(factor, rows_each, rows_ref, gram_ref, out_ref, spread):
    packed = gram_ref[...]
    gram = jnp.concatenate([pltpu.roll(packed, RANK, 1), packed], axis=0)
    low = lanes_of((RANK, WIDE)) < RANK
    for example in range(rows_ref.shape[0]):
        joined = jnp.where(low, rows_ref[example], gram)
        done = eliminated([joined[at : at + 8] for at in range(0, RANK, 8)], spread)
        solved = (jnp.concatenate(done, axis=0) * factor).T
        out_ref[example] = solved[:rows_each, :]


def whiten(rows, gram, rows_each, factor):
    return pl.pallas_call(
        functools.partial(whiten_kernel, factor, rows_each),
        out_shape=jax.ShapeDtypeStruct((rows.shape[0], rows_each, RANK), jnp.float32),
        in_specs=[whole_vmem] * 2,
        out_specs=whole_vmem,
        scratch_shapes=[pltpu.VMEM((18, 8, WIDE), jnp.float32)],
        compiler_params=small,
        name="whiten",
    )(rows, gram)


def summed_over_groups(value):
    groups, model_shards = lax.axis_size("dp"), lax.axis_size("mp")
    place = lax.axis_index("mp")

    def over_groups(value):
        for level in range(groups.bit_length() - 1):
            pairs = [(source, source ^ 2**level) for source in range(groups)]
            value = value + lax.ppermute(value, "dp", pairs)
        return value

    value = lax.cond(place == model_shards - 1, over_groups, lambda value: value, value)
    result = value
    for away in range(1, model_shards):
        pairs = [(source, (source + away) % model_shards) for source in range(model_shards)]
        received = lax.ppermute(value, "mp", pairs)
        result = jnp.where(place == away - 1, received, result)
    return result


def shards(tokens_in, gate_pre, up_pre, hidden_grad, out_grad, proj_model, proj_hidden):
    model_shards = lax.axis_size("mp")
    rows_each = WIDE // model_shards
    local_examples = tokens_in.shape[0] // LEN
    place = lax.axis_index("mp").astype(jnp.int32).reshape(1)
    part = project(
        gate_pre, up_pre, hidden_grad, proj_hidden, tokens_in, out_grad, proj_model
    )
    parts = [part]
    for away in range(1, model_shards):
        pairs = [(source, (source + away) % model_shards) for source in range(model_shards)]
        parts.append(lax.ppermute(part, "mp", pairs))
    rows, gram = gram_of(place, parts, rows_each)
    gram = summed_over_groups(gram)
    factor = math.sqrt(local_examples * lax.axis_size("dp") * 2 * RANK)
    return whiten(rows, gram, rows_each, factor)


def solution(mesh):
    in_specs = (
        P("dp", "mp"),
        P("dp", "mp"),
        P("dp", "mp"),
        P("dp", "mp"),
        P("dp", "mp"),
        P("mp", None),
        P("mp", None),
    )
    out_specs = P("dp", "mp", None)
    return jax.shard_map(shards, mesh=mesh, in_specs=in_specs, out_specs=out_specs, check_vma=False)
```

```python
import functools
import math

import jax
import jax.numpy as jnp
from jax import lax
from jax.experimental import pallas as pl
from jax.experimental.pallas import tpu as pltpu
from jax.sharding import PartitionSpec as P

RANK = 64
LEN = 128
WIDE = 2 * RANK
EACH = 2048
HEAD = 512
STEP = 256
AHEAD = 3

highest = lax.Precision.HIGHEST
whole_vmem = pl.BlockSpec(memory_space=pltpu.VMEM)
left_in_hbm = pl.BlockSpec(memory_space=pl.ANY)
small = pltpu.CompilerParams(vmem_limit_bytes=8 * 2**20)


def cuts_of(width):
    full = max((width - 1) // EACH, 0)
    head = width - full * EACH
    ends = [0, min(HEAD, head)]
    while ends[-1] < head:
        ends.append(min(ends[-1] + EACH // 2, head))
    return [(begin, end - begin) for begin, end in zip(ends, ends[1:])], full


def shares_of(width, slots):
    count = max(slots - 1, 1)
    while width % (count * 128):
        count -= 1
    return width // count, count


def lanes_of(shape):
    return lax.broadcasted_iota(jnp.int32, shape, len(shape) - 1)


def project_kernel(gate, up, grad, proj_hidden, tokens, outer, proj_model, out, *rest):
    gate_v, up_v, grad_v, hidden_w, tokens_v, outer_v, model_w = rest[:7]
    hidden_sum, model_sum, sems, model_sems = rest[7:]
    rows = gate.shape[0]
    head, full = cuts_of(gate.shape[1])
    head_width = gate.shape[1] - full * EACH
    model_each, model_count = shares_of(tokens.shape[1], len(head) + full)

    def hidden_copies(slot, begin, size):
        cut = pl.ds(pl.multiple_of(begin, 128), size)
        pairs = [
            (gate.at[:, cut], gate_v.at[:, cut]),
            (grad.at[:, cut], grad_v.at[:, cut]),
            (up.at[:, cut], up_v.at[:, cut]),
            (proj_hidden.at[cut, :], hidden_w.at[cut, :]),
        ]
        return [
            pltpu.make_async_copy(source, target, sems.at[slot, which])
            for which, (source, target) in enumerate(pairs)
        ]

    def full_copies(piece):
        return hidden_copies(len(head) + piece, head_width + piece * EACH, EACH)

    def model_copies(piece):
        cut = pl.ds(pl.multiple_of(piece * model_each, model_each), model_each)
        pairs = [
            (tokens.at[:, cut], tokens_v.at[:, cut]),
            (outer.at[:, cut], outer_v.at[:, cut]),
            (proj_model.at[cut, :], model_w.at[cut, :]),
        ]
        return [
            pltpu.make_async_copy(source, target, model_sems.at[piece, which])
            for which, (source, target) in enumerate(pairs)
        ]

    def start(copies):
        for copy in copies:
            copy.start()

    def arrive(copies):
        for copy in copies:
            copy.wait()

    def model_dots(begin, size):
        cut = pl.ds(pl.multiple_of(begin, 128), size)
        weights = model_w[cut, :]
        for which, side in enumerate((tokens_v, outer_v)):
            model_sum[which * rows : (which + 1) * rows, :] += jnp.dot(
                side[:, cut], weights, preferred_element_type=jnp.float32
            )

    def advance(begin, size, share=None):
        if share is not None:
            model_dots(share * model_each, model_each)
        totals = []
        for first in range(0, size, STEP):
            step = min(STEP, size - first)
            cut = pl.ds(pl.multiple_of(begin + first, 128), step)
            half = (gate_v[:, cut] * 0.5).astype(jnp.float32)
            act = half + half * jnp.tanh(half)
            up_grad = (grad_v[:, cut].astype(jnp.float32) * act).astype(jnp.bfloat16)
            hidden = (act * up_v[:, cut].astype(jnp.float32)).astype(jnp.bfloat16)
            weights = hidden_w[cut, :]
            parts = [
                jnp.dot(side, weights, preferred_element_type=jnp.float32)
                for side in (up_grad, hidden)
            ]
            totals = [old + new for old, new in zip(totals, parts)] if totals else parts
        for which, total in enumerate(totals):
            hidden_sum[which * rows : (which + 1) * rows, :] += total

    taken = min(len(head) - 1, model_count)
    looped = full if model_count - taken >= full else 0
    ahead = min(AHEAD, full)

    def start_full(piece):
        start(full_copies(piece))
        if looped:
            start(model_copies(taken + piece))

    for slot, (begin, size) in enumerate(head):
        start(hidden_copies(slot, begin, size))
        if 0 < slot <= taken:
            start(model_copies(slot - 1))
    for piece in range(ahead):
        start_full(piece)
    for share in range(taken + looped, model_count):
        start(model_copies(share))
    hidden_sum[...] = jnp.zeros_like(hidden_sum)
    model_sum[...] = jnp.zeros_like(model_sum)
    for slot, (begin, size) in enumerate(head):
        arrive(hidden_copies(slot, begin, size))
        if 0 < slot <= taken:
            arrive(model_copies(slot - 1))
        advance(begin, size, slot - 1 if 0 < slot <= taken else None)

    @pl.loop(0, full)
    def _(piece):
        arrive(full_copies(piece))
        if looped:
            arrive(model_copies(taken + piece))

        @pl.when(piece + ahead < full)
        def _():
            start_full(piece + ahead)

        advance(head_width + piece * EACH, EACH, taken + piece if looped else None)

    for share in range(taken + looped, model_count):
        arrive(model_copies(share))
        model_dots(share * model_each, model_each)

    low = lanes_of((rows, WIDE)) < RANK
    upward = pltpu.roll(hidden_sum[:rows, :], RANK, 1)
    hidden_side = pltpu.roll(hidden_sum[rows:, :], RANK, 1)
    out[:, :WIDE] = jnp.where(low, model_sum[:rows, :], upward)
    out[:, WIDE:] = jnp.where(low, hidden_side, model_sum[rows:, :])


def project(gate_pre, up_pre, hidden_grad, proj_hidden, tokens_in, out_grad, proj_model):
    rows, hidden_width = gate_pre.shape
    model_width = tokens_in.shape[1]
    head, full = cuts_of(hidden_width)
    hidden_slots = len(head) + full
    held = jnp.bfloat16
    return pl.pallas_call(
        project_kernel,
        out_shape=jax.ShapeDtypeStruct((rows, 2 * WIDE), jnp.float32),
        in_specs=[left_in_hbm] * 7,
        out_specs=whole_vmem,
        scratch_shapes=[
            pltpu.VMEM((rows, hidden_width), held),
            pltpu.VMEM((rows, hidden_width), held),
            pltpu.VMEM((rows, hidden_width), held),
            pltpu.VMEM((hidden_width, WIDE), held),
            pltpu.VMEM((rows, model_width), held),
            pltpu.VMEM((rows, model_width), held),
            pltpu.VMEM((model_width, WIDE), held),
            pltpu.VMEM((2 * rows, WIDE), jnp.float32),
            pltpu.VMEM((2 * rows, WIDE), jnp.float32),
            pltpu.SemaphoreType.DMA((hidden_slots, 4)),
            pltpu.SemaphoreType.DMA((shares_of(model_width, hidden_slots)[1], 3)),
        ],
        compiler_params=pltpu.CompilerParams(vmem_limit_bytes=56 * 10**6),
        name="project",
    )(gate_pre, up_pre, hidden_grad, proj_hidden, tokens_in, out_grad, proj_model)


def gram_kernel(rows_each, count, *refs):
    place, parts, (rows_ref, gram_ref) = refs[0], refs[1 : 1 + count], refs[1 + count :]
    total = parts[0][...]
    for part in parts[1:]:
        total += part[...]
    row = lax.broadcasted_iota(jnp.int32, (WIDE, WIDE), 0)
    lane = lanes_of((WIDE, WIDE))
    low = lanes_of((RANK, WIDE)) < RANK
    gram = jnp.zeros((RANK, WIDE), jnp.float32)
    shift = lax.rem(WIDE - place[0] * rows_each, WIDE)
    for example in range(total.shape[0] // LEN):
        mixed = []
        for at in (0, WIDE):
            sides = total[example * LEN : (example + 1) * LEN, at : at + WIDE]
            crossed = jnp.dot(
                sides.T, sides, precision=highest, preferred_element_type=jnp.float32
            )
            mixed.append(jnp.where((row < RANK) != (lane < RANK), crossed, 0.0))
        up_block, down_block = mixed[0][RANK:], mixed[1][RANK:]
        across = jnp.where(low, up_block, pltpu.roll(down_block, RANK, 1))
        rows_ref[example] = jnp.where(low, pltpu.roll(across, shift, 1), 0.0)
        gram += jnp.dot(
            jnp.concatenate([up_block, down_block], axis=1),
            jnp.concatenate(mixed, axis=0),
            precision=highest,
            preferred_element_type=jnp.float32,
        )
    top, bottom = gram[: RANK // 2], gram[RANK // 2 :]
    gram_ref[...] = jnp.where(
        lanes_of(top.shape) < RANK, pltpu.roll(top, RANK, 1), bottom
    )


def gram_of(place, parts, rows_each):
    examples = parts[0].shape[0] // LEN
    return pl.pallas_call(
        functools.partial(gram_kernel, rows_each, len(parts)),
        out_shape=[
            jax.ShapeDtypeStruct((examples, RANK, WIDE), jnp.float32),
            jax.ShapeDtypeStruct((RANK // 2, WIDE), jnp.float32),
        ],
        in_specs=[pl.BlockSpec(memory_space=pltpu.SMEM)] + [whole_vmem] * len(parts),
        out_specs=[whole_vmem] * 2,
        compiler_params=small,
        name="gram",
    )(place, *parts)


def eliminated(state, spread):
    height = 8
    blocks = len(state)
    state = list(state)
    sub = lax.broadcasted_iota(jnp.int32, state[0].shape, 0)

    def across(block, at):
        return jnp.broadcast_to(block[:, at : at + 1], block.shape)

    def down(which, at):
        return spread[which, pl.ds(at, height, stride=0), :]

    done = []
    for held in range(blocks):
        base = RANK + held * height
        own = state[held]
        first_slot = (held % 2) * (height + 1)
        for k in range(height):
            spread[first_slot + k] = across(own, base + k)
        spread[first_slot + height] = own
        corner = {
            (k, m): down(first_slot + m, k) for k in range(height) for m in range(k, height)
        }
        rows = [down(first_slot + height, k) for k in range(height)]
        ahead = None
        if held + 1 < blocks:
            ahead = [across(state[held + 1], base + k) for k in range(height)]
        factors = {}
        solved = [None] * height
        for k in range(0, height, 2):
            first, cross, second = corner[k, k], corner[k, k + 1], corner[k + 1, k + 1]
            determinant = first * second - cross * cross
            inverse = pl.reciprocal(determinant, approx=True)
            solved[k] = (second * rows[k] - cross * rows[k + 1]) * inverse
            solved[k + 1] = (first * rows[k + 1] - cross * rows[k]) * inverse
            for m in range(k + 2, height):
                left, right = corner[k, m], corner[k + 1, m]
                upper = second * left - cross * right
                lower = first * right - cross * left
                for n in range(m, height):
                    taken = upper * corner[k, n] + lower * corner[k + 1, n]
                    corner[m, n] = corner[m, n] - taken * inverse
                factors[k, m], factors[k + 1, m] = upper * inverse, lower * inverse
                for several in (rows, ahead):
                    if several is not None:
                        several[m] = several[m] - (
                            factors[k, m] * several[k] + factors[k + 1, m] * several[k + 1]
                        )
        if ahead is not None:
            taken = [ahead[k] * solved[k] for k in range(height)]
            while len(taken) > 1:
                taken = [left + right for left, right in zip(taken[::2], taken[1::2])]
            state[held + 1] = state[held + 1] - taken[0]
        if held + 2 < blocks:
            back = list(solved)
            for m in reversed(range(2, height)):
                for k in range(m - m % 2):
                    back[k] = back[k] - factors[k, m] * back[m]
            packed = back[0]
            for k in range(1, height):
                packed = jnp.where(sub == k, back[k], packed)
            weights = [jnp.zeros_like(own)] * (2 * blocks)
            weights[blocks + held] = packed
            later = jnp.concatenate(state[held + 2 :], axis=0)
            later = later - jnp.dot(
                later,
                jnp.concatenate(weights, axis=0),
                precision=highest,
                preferred_element_type=jnp.float32,
            )
            for other in range(held + 2, blocks):
                at = (other - held - 2) * height
                state[other] = later[at : at + height]
        block = jnp.zeros_like(own)
        for k in range(0, height, 2):
            first, cross, second = corner[k, k], corner[k, k + 1], corner[k + 1, k + 1]
            ratio = cross * pl.reciprocal(first, approx=True)
            final = second - cross * ratio
            block = jnp.where(sub == k, rows[k] * lax.rsqrt(first), block)
            block = jnp.where(
                sub == k + 1, (rows[k + 1] - ratio * rows[k]) * lax.rsqrt(final), block
            )
        done.append(block)
    return done


def whiten_kernel(factor, rows_each, rows_ref, gram_ref, out_ref, spread):
    packed = gram_ref[...]
    gram = jnp.concatenate([pltpu.roll(packed, RANK, 1), packed], axis=0)
    low = lanes_of((RANK, WIDE)) < RANK
    for example in range(rows_ref.shape[0]):
        joined = jnp.where(low, rows_ref[example], gram)
        done = eliminated([joined[at : at + 8] for at in range(0, RANK, 8)], spread)
        solved = (jnp.concatenate(done, axis=0) * factor).T
        out_ref[example] = solved[:rows_each, :]


def whiten(rows, gram, rows_each, factor):
    return pl.pallas_call(
        functools.partial(whiten_kernel, factor, rows_each),
        out_shape=jax.ShapeDtypeStruct((rows.shape[0], rows_each, RANK), jnp.float32),
        in_specs=[whole_vmem] * 2,
        out_specs=whole_vmem,
        scratch_shapes=[pltpu.VMEM((18, 8, WIDE), jnp.float32)],
        compiler_params=small,
        name="whiten",
    )(rows, gram)


def summed_over_groups(value):
    groups, model_shards = lax.axis_size("dp"), lax.axis_size("mp")
    place = lax.axis_index("mp")

    def over_groups(value):
        for level in range(groups.bit_length() - 1):
            pairs = [(source, source ^ 2**level) for source in range(groups)]
            value = value + lax.ppermute(value, "dp", pairs)
        return value

    value = lax.cond(place == model_shards - 1, over_groups, lambda value: value, value)
    result = value
    for away in range(1, model_shards):
        pairs = [(source, (source + away) % model_shards) for source in range(model_shards)]
        received = lax.ppermute(value, "mp", pairs)
        result = jnp.where(place == away - 1, received, result)
    return result


def shards(tokens_in, gate_pre, up_pre, hidden_grad, out_grad, proj_model, proj_hidden):
    model_shards = lax.axis_size("mp")
    rows_each = WIDE // model_shards
    local_examples = tokens_in.shape[0] // LEN
    place = lax.axis_index("mp").astype(jnp.int32).reshape(1)
    part = project(
        gate_pre, up_pre, hidden_grad, proj_hidden, tokens_in, out_grad, proj_model
    )
    parts = [part]
    for away in range(1, model_shards):
        pairs = [(source, (source + away) % model_shards) for source in range(model_shards)]
        parts.append(lax.ppermute(part, "mp", pairs))
    rows, gram = gram_of(place, parts, rows_each)
    gram = summed_over_groups(gram)
    factor = math.sqrt(local_examples * lax.axis_size("dp") * 2 * RANK)
    return whiten(rows, gram, rows_each, factor)


def solution(mesh):
    in_specs = (
        P("dp", "mp"),
        P("dp", "mp"),
        P("dp", "mp"),
        P("dp", "mp"),
        P("dp", "mp"),
        P("mp", None),
        P("mp", None),
    )
    out_specs = P("dp", "mp", None)
    return jax.shard_map(shards, mesh=mesh, in_specs=in_specs, out_specs=out_specs, check_vma=False)
```

```python
import functools
import math

import jax
import jax.numpy as jnp
from jax import lax
from jax.experimental import pallas as pl
from jax.experimental.pallas import tpu as pltpu
from jax.sharding import PartitionSpec as P

RANK = 64
LEN = 128
WIDE = 2 * RANK
EACH = 2048
HEAD = 512
MODEL_EACH = 1024
STEP = 256
AHEAD = 3

highest = lax.Precision.HIGHEST
whole_vmem = pl.BlockSpec(memory_space=pltpu.VMEM)
left_in_hbm = pl.BlockSpec(memory_space=pl.ANY)
small = pltpu.CompilerParams(vmem_limit_bytes=8 * 2**20)


def cuts_of(width):
    full = max((width - 1) // EACH, 0)
    head = width - full * EACH
    ends = [0, min(HEAD, head)]
    while ends[-1] < head:
        ends.append(min(ends[-1] + EACH // 2, head))
    return [(begin, end - begin) for begin, end in zip(ends, ends[1:])], full


def lanes_of(shape):
    return lax.broadcasted_iota(jnp.int32, shape, len(shape) - 1)


def project_kernel(gate, up, grad, proj_hidden, tokens, outer, proj_model, out, *rest):
    gate_v, up_v, grad_v, hidden_w, tokens_v, outer_v, model_w = rest[:7]
    hidden_sum, model_sum, sems, model_sems = rest[7:]
    rows = gate.shape[0]
    model_each = math.gcd(tokens.shape[1], MODEL_EACH)
    model_count = tokens.shape[1] // model_each
    head, full = cuts_of(gate.shape[1])
    head_width = gate.shape[1] - full * EACH

    def hidden_copies(slot, begin, size):
        cut = pl.ds(pl.multiple_of(begin, 128), size)
        pairs = [
            (gate.at[:, cut], gate_v.at[:, cut]),
            (grad.at[:, cut], grad_v.at[:, cut]),
            (up.at[:, cut], up_v.at[:, cut]),
            (proj_hidden.at[cut, :], hidden_w.at[cut, :]),
        ]
        return [
            pltpu.make_async_copy(source, target, sems.at[slot, which])
            for which, (source, target) in enumerate(pairs)
        ]

    def full_copies(piece):
        return hidden_copies(len(head) + piece, head_width + piece * EACH, EACH)

    def model_copies(piece):
        cut = pl.ds(pl.multiple_of(piece * model_each, model_each), model_each)
        pairs = [
            (tokens.at[:, cut], tokens_v.at[:, cut]),
            (outer.at[:, cut], outer_v.at[:, cut]),
            (proj_model.at[cut, :], model_w.at[cut, :]),
        ]
        return [
            pltpu.make_async_copy(source, target, model_sems.at[piece, which])
            for which, (source, target) in enumerate(pairs)
        ]

    def start(copies):
        for copy in copies:
            copy.start()

    def arrive(copies):
        for copy in copies:
            copy.wait()

    def start_models():
        for other in range(model_count):
            start(model_copies(other))

    def advance(begin, size):
        for first in range(0, size, STEP):
            step = min(STEP, size - first)
            cut = pl.ds(pl.multiple_of(begin + first, 128), step)
            half = (gate_v[:, cut] * 0.5).astype(jnp.float32)
            act = half + half * jnp.tanh(half)
            up_grad = (grad_v[:, cut].astype(jnp.float32) * act).astype(jnp.bfloat16)
            hidden = (act * up_v[:, cut].astype(jnp.float32)).astype(jnp.bfloat16)
            weights = hidden_w[cut, :]
            for which, side in enumerate((up_grad, hidden)):
                hidden_sum[which * rows : (which + 1) * rows, :] += jnp.dot(
                    side, weights, preferred_element_type=jnp.float32
                )

    ahead = min(AHEAD, full)
    for slot, (begin, size) in enumerate(head):
        start(hidden_copies(slot, begin, size))
    for piece in range(ahead):
        start(full_copies(piece))
    if not full:
        start_models()
    hidden_sum[...] = jnp.zeros_like(hidden_sum)
    model_sum[...] = jnp.zeros_like(model_sum)
    for slot, (begin, size) in enumerate(head):
        arrive(hidden_copies(slot, begin, size))
        advance(begin, size)

    @pl.loop(0, full)
    def _(piece):
        arrive(full_copies(piece))

        @pl.when(piece + ahead < full)
        def _():
            start(full_copies(piece + ahead))

        @pl.when(piece + ahead == full)
        def _():
            start_models()

        advance(head_width + piece * EACH, EACH)

    @pl.loop(0, model_count)
    def _(piece):
        arrive(model_copies(piece))
        cut = pl.ds(pl.multiple_of(piece * model_each, model_each), model_each)
        weights = model_w[cut, :]
        for which, side in enumerate((tokens_v, outer_v)):
            model_sum[which * rows : (which + 1) * rows, :] += jnp.dot(
                side[:, cut], weights, preferred_element_type=jnp.float32
            )

    low = lanes_of((rows, WIDE)) < RANK
    upward = pltpu.roll(hidden_sum[:rows, :], RANK, 1)
    hidden_side = pltpu.roll(hidden_sum[rows:, :], RANK, 1)
    out[:, :WIDE] = jnp.where(low, model_sum[:rows, :], upward)
    out[:, WIDE:] = jnp.where(low, hidden_side, model_sum[rows:, :])


def project(gate_pre, up_pre, hidden_grad, proj_hidden, tokens_in, out_grad, proj_model):
    rows, hidden_width = gate_pre.shape
    model_width = tokens_in.shape[1]
    head, full = cuts_of(hidden_width)
    hidden_slots = len(head) + full
    held = jnp.bfloat16
    return pl.pallas_call(
        project_kernel,
        out_shape=jax.ShapeDtypeStruct((rows, 2 * WIDE), jnp.float32),
        in_specs=[left_in_hbm] * 7,
        out_specs=whole_vmem,
        scratch_shapes=[
            pltpu.VMEM((rows, hidden_width), held),
            pltpu.VMEM((rows, hidden_width), held),
            pltpu.VMEM((rows, hidden_width), held),
            pltpu.VMEM((hidden_width, WIDE), held),
            pltpu.VMEM((rows, model_width), held),
            pltpu.VMEM((rows, model_width), held),
            pltpu.VMEM((model_width, WIDE), held),
            pltpu.VMEM((2 * rows, WIDE), jnp.float32),
            pltpu.VMEM((2 * rows, WIDE), jnp.float32),
            pltpu.SemaphoreType.DMA((hidden_slots, 4)),
            pltpu.SemaphoreType.DMA((model_width // math.gcd(model_width, MODEL_EACH), 3)),
        ],
        compiler_params=pltpu.CompilerParams(vmem_limit_bytes=56 * 10**6),
        name="project",
    )(gate_pre, up_pre, hidden_grad, proj_hidden, tokens_in, out_grad, proj_model)


def gram_kernel(rows_each, count, *refs):
    place, parts, (rows_ref, gram_ref) = refs[0], refs[1 : 1 + count], refs[1 + count :]
    total = parts[0][...]
    for part in parts[1:]:
        total += part[...]
    row = lax.broadcasted_iota(jnp.int32, (WIDE, WIDE), 0)
    lane = lanes_of((WIDE, WIDE))
    low = lanes_of((RANK, WIDE)) < RANK
    gram = jnp.zeros((RANK, WIDE), jnp.float32)
    shift = lax.rem(WIDE - place[0] * rows_each, WIDE)
    for example in range(total.shape[0] // LEN):
        mixed = []
        for at in (0, WIDE):
            sides = total[example * LEN : (example + 1) * LEN, at : at + WIDE]
            crossed = jnp.dot(
                sides.T, sides, precision=highest, preferred_element_type=jnp.float32
            )
            mixed.append(jnp.where((row < RANK) != (lane < RANK), crossed, 0.0))
        up_block, down_block = mixed[0][RANK:], mixed[1][RANK:]
        across = jnp.where(low, up_block, pltpu.roll(down_block, RANK, 1))
        rows_ref[example] = jnp.where(low, pltpu.roll(across, shift, 1), 0.0)
        gram += jnp.dot(
            jnp.concatenate([up_block, down_block], axis=1),
            jnp.concatenate(mixed, axis=0),
            precision=highest,
            preferred_element_type=jnp.float32,
        )
    top, bottom = gram[: RANK // 2], gram[RANK // 2 :]
    gram_ref[...] = jnp.where(
        lanes_of(top.shape) < RANK, pltpu.roll(top, RANK, 1), bottom
    )


def gram_of(place, parts, rows_each):
    examples = parts[0].shape[0] // LEN
    return pl.pallas_call(
        functools.partial(gram_kernel, rows_each, len(parts)),
        out_shape=[
            jax.ShapeDtypeStruct((examples, RANK, WIDE), jnp.float32),
            jax.ShapeDtypeStruct((RANK // 2, WIDE), jnp.float32),
        ],
        in_specs=[pl.BlockSpec(memory_space=pltpu.SMEM)] + [whole_vmem] * len(parts),
        out_specs=[whole_vmem] * 2,
        compiler_params=small,
        name="gram",
    )(place, *parts)


def eliminated(state, spread):
    height = 8
    blocks = len(state)
    state = list(state)
    sub = lax.broadcasted_iota(jnp.int32, state[0].shape, 0)

    def across(block, at):
        return jnp.broadcast_to(block[:, at : at + 1], block.shape)

    def down(which, at):
        return spread[which, pl.ds(at, height, stride=0), :]

    done = []
    for held in range(blocks):
        base = RANK + held * height
        own = state[held]
        first_slot = (held % 2) * (height + 1)
        for k in range(height):
            spread[first_slot + k] = across(own, base + k)
        spread[first_slot + height] = own
        corner = {
            (k, m): down(first_slot + m, k) for k in range(height) for m in range(k, height)
        }
        rows = [down(first_slot + height, k) for k in range(height)]
        ahead = None
        if held + 1 < blocks:
            ahead = [across(state[held + 1], base + k) for k in range(height)]
        factors = {}
        solved = [None] * height
        for k in range(0, height, 2):
            first, cross, second = corner[k, k], corner[k, k + 1], corner[k + 1, k + 1]
            determinant = first * second - cross * cross
            inverse = pl.reciprocal(determinant, approx=True)
            solved[k] = (second * rows[k] - cross * rows[k + 1]) * inverse
            solved[k + 1] = (first * rows[k + 1] - cross * rows[k]) * inverse
            for m in range(k + 2, height):
                left, right = corner[k, m], corner[k + 1, m]
                upper = second * left - cross * right
                lower = first * right - cross * left
                for n in range(m, height):
                    taken = upper * corner[k, n] + lower * corner[k + 1, n]
                    corner[m, n] = corner[m, n] - taken * inverse
                factors[k, m], factors[k + 1, m] = upper * inverse, lower * inverse
                for several in (rows, ahead):
                    if several is not None:
                        several[m] = several[m] - (
                            factors[k, m] * several[k] + factors[k + 1, m] * several[k + 1]
                        )
        if ahead is not None:
            taken = [ahead[k] * solved[k] for k in range(height)]
            while len(taken) > 1:
                taken = [left + right for left, right in zip(taken[::2], taken[1::2])]
            state[held + 1] = state[held + 1] - taken[0]
        if held + 2 < blocks:
            back = list(solved)
            for m in reversed(range(2, height)):
                for k in range(m - m % 2):
                    back[k] = back[k] - factors[k, m] * back[m]
            near = state[held + 2]
            taken = [across(near, base + k) * back[k] for k in range(height)]
            while len(taken) > 1:
                taken = [left + right for left, right in zip(taken[::2], taken[1::2])]
            state[held + 2] = near - taken[0]
        if held + 3 < blocks:
            packed = back[0]
            for k in range(1, height):
                packed = jnp.where(sub == k, back[k], packed)
            weights = [jnp.zeros_like(own)] * (2 * blocks)
            weights[blocks + held] = packed
            later = jnp.concatenate(state[held + 3 :], axis=0)
            later = later - jnp.dot(
                later,
                jnp.concatenate(weights, axis=0),
                precision=highest,
                preferred_element_type=jnp.float32,
            )
            for other in range(held + 3, blocks):
                at = (other - held - 3) * height
                state[other] = later[at : at + height]
        block = jnp.zeros_like(own)
        for k in range(0, height, 2):
            first, cross, second = corner[k, k], corner[k, k + 1], corner[k + 1, k + 1]
            ratio = cross * pl.reciprocal(first, approx=True)
            final = second - cross * ratio
            block = jnp.where(sub == k, rows[k] * lax.rsqrt(first), block)
            block = jnp.where(
                sub == k + 1, (rows[k + 1] - ratio * rows[k]) * lax.rsqrt(final), block
            )
        done.append(block)
    return done


def whiten_kernel(factor, rows_each, rows_ref, gram_ref, out_ref, spread):
    packed = gram_ref[...]
    gram = jnp.concatenate([pltpu.roll(packed, RANK, 1), packed], axis=0)
    low = lanes_of((RANK, WIDE)) < RANK
    for example in range(rows_ref.shape[0]):
        joined = jnp.where(low, rows_ref[example], gram)
        done = eliminated([joined[at : at + 8] for at in range(0, RANK, 8)], spread)
        solved = (jnp.concatenate(done, axis=0) * factor).T
        out_ref[example] = solved[:rows_each, :]


def whiten(rows, gram, rows_each, factor):
    return pl.pallas_call(
        functools.partial(whiten_kernel, factor, rows_each),
        out_shape=jax.ShapeDtypeStruct((rows.shape[0], rows_each, RANK), jnp.float32),
        in_specs=[whole_vmem] * 2,
        out_specs=whole_vmem,
        scratch_shapes=[pltpu.VMEM((18, 8, WIDE), jnp.float32)],
        compiler_params=small,
        name="whiten",
    )(rows, gram)


def summed_over_groups(value):
    groups, model_shards = lax.axis_size("dp"), lax.axis_size("mp")
    place = lax.axis_index("mp")

    def over_groups(value):
        for level in range(groups.bit_length() - 1):
            pairs = [(source, source ^ 2**level) for source in range(groups)]
            value = value + lax.ppermute(value, "dp", pairs)
        return value

    value = lax.cond(place == model_shards - 1, over_groups, lambda value: value, value)
    result = value
    for away in range(1, model_shards):
        pairs = [(source, (source + away) % model_shards) for source in range(model_shards)]
        received = lax.ppermute(value, "mp", pairs)
        result = jnp.where(place == away - 1, received, result)
    return result


def shards(tokens_in, gate_pre, up_pre, hidden_grad, out_grad, proj_model, proj_hidden):
    model_shards = lax.axis_size("mp")
    rows_each = WIDE // model_shards
    local_examples = tokens_in.shape[0] // LEN
    place = lax.axis_index("mp").astype(jnp.int32).reshape(1)
    part = project(
        gate_pre, up_pre, hidden_grad, proj_hidden, tokens_in, out_grad, proj_model
    )
    parts = [part]
    for away in range(1, model_shards):
        pairs = [(source, (source + away) % model_shards) for source in range(model_shards)]
        parts.append(lax.ppermute(part, "mp", pairs))
    rows, gram = gram_of(place, parts, rows_each)
    gram = summed_over_groups(gram)
    factor = math.sqrt(local_examples * lax.axis_size("dp") * 2 * RANK)
    return whiten(rows, gram, rows_each, factor)


def solution(mesh):
    in_specs = (
        P("dp", "mp"),
        P("dp", "mp"),
        P("dp", "mp"),
        P("dp", "mp"),
        P("dp", "mp"),
        P("mp", None),
        P("mp", None),
    )
    out_specs = P("dp", "mp", None)
    return jax.shard_map(shards, mesh=mesh, in_specs=in_specs, out_specs=out_specs, check_vma=False)
```

```python
import functools
import math

import jax
import jax.numpy as jnp
from jax import lax
from jax.experimental import pallas as pl
from jax.experimental.pallas import tpu as pltpu
from jax.sharding import PartitionSpec as P

RANK = 64
LEN = 128
WIDE = 2 * RANK
EACH = 2048
HEAD = 512
MODEL_EACH = 1024
STEP = 256
AHEAD = 6

highest = lax.Precision.HIGHEST
whole_vmem = pl.BlockSpec(memory_space=pltpu.VMEM)
left_in_hbm = pl.BlockSpec(memory_space=pl.ANY)
small = pltpu.CompilerParams(vmem_limit_bytes=8 * 2**20)


def cuts_of(width):
    full = max((width - 1) // EACH, 0)
    head = width - full * EACH
    ends = [0, min(HEAD, head)]
    while ends[-1] < head:
        ends.append(min(ends[-1] + EACH // 2, head))
    return [(begin, end - begin) for begin, end in zip(ends, ends[1:])], full


def lanes_of(shape):
    return lax.broadcasted_iota(jnp.int32, shape, len(shape) - 1)


def paired(left, right, weights):
    low = lanes_of(weights.shape) < RANK
    none = jnp.zeros_like(weights)
    return jnp.dot(
        jnp.concatenate([left, right], axis=1),
        jnp.concatenate([jnp.where(low, weights, none), jnp.where(low, none, weights)], axis=0),
        preferred_element_type=jnp.float32,
    )


def project_kernel(gate, up, grad, proj_hidden, tokens, outer, proj_model, out, *rest):
    gate_v, up_v, grad_v, hidden_w, tokens_v, outer_v, model_w = rest[:7]
    hidden_sum, model_sum, sems, model_sems = rest[7:]
    rows = gate.shape[0]
    model_each = math.gcd(tokens.shape[1], MODEL_EACH)
    model_count = tokens.shape[1] // model_each
    head, full = cuts_of(gate.shape[1])
    head_width = gate.shape[1] - full * EACH

    def hidden_copies(slot, begin, size):
        cut = pl.ds(pl.multiple_of(begin, 128), size)
        pairs = [
            (gate.at[:, cut], gate_v.at[:, cut]),
            (grad.at[:, cut], grad_v.at[:, cut]),
            (up.at[:, cut], up_v.at[:, cut]),
            (proj_hidden.at[cut, :], hidden_w.at[cut, :]),
        ]
        return [
            pltpu.make_async_copy(source, target, sems.at[slot, which])
            for which, (source, target) in enumerate(pairs)
        ]

    def full_copies(piece):
        return hidden_copies(len(head) + piece, head_width + piece * EACH, EACH)

    def model_copies(piece):
        cut = pl.ds(pl.multiple_of(piece * model_each, model_each), model_each)
        pairs = [
            (tokens.at[:, cut], tokens_v.at[:, cut]),
            (outer.at[:, cut], outer_v.at[:, cut]),
            (proj_model.at[cut, :], model_w.at[cut, :]),
        ]
        return [
            pltpu.make_async_copy(source, target, model_sems.at[piece, which])
            for which, (source, target) in enumerate(pairs)
        ]

    def start(copies):
        for copy in copies:
            copy.start()

    def arrive(copies):
        for copy in copies:
            copy.wait()

    def start_models():
        for other in range(model_count):
            start(model_copies(other))

    def advance(begin, size):
        total = None
        for first in range(0, size, STEP):
            step = min(STEP, size - first)
            cut = pl.ds(pl.multiple_of(begin + first, 128), step)
            half = (gate_v[:, cut] * 0.5).astype(jnp.float32)
            act = half + half * jnp.tanh(half)
            up_grad = (grad_v[:, cut].astype(jnp.float32) * act).astype(jnp.bfloat16)
            hidden = (act * up_v[:, cut].astype(jnp.float32)).astype(jnp.bfloat16)
            part = paired(up_grad, hidden, hidden_w[cut, :])
            total = part if total is None else total + part
        hidden_sum[...] += total

    ahead = min(AHEAD, full)
    for slot, (begin, size) in enumerate(head):
        start(hidden_copies(slot, begin, size))
    for piece in range(ahead):
        start(full_copies(piece))
    if not full:
        start_models()
    hidden_sum[...] = jnp.zeros_like(hidden_sum)
    model_sum[...] = jnp.zeros_like(model_sum)
    for slot, (begin, size) in enumerate(head):
        arrive(hidden_copies(slot, begin, size))
        advance(begin, size)

    @pl.loop(0, full)
    def _(piece):
        arrive(full_copies(piece))

        @pl.when(piece + ahead < full)
        def _():
            start(full_copies(piece + ahead))

        @pl.when(piece + ahead == full)
        def _():
            start_models()

        advance(head_width + piece * EACH, EACH)

    @pl.loop(0, model_count)
    def _(piece):
        arrive(model_copies(piece))
        cut = pl.ds(pl.multiple_of(piece * model_each, model_each), model_each)
        model_sum[...] += paired(tokens_v[:, cut], outer_v[:, cut], model_w[cut, :])

    low = lanes_of((rows, WIDE)) < RANK
    turned = pltpu.roll(hidden_sum[...], RANK, 1)
    out[:, :WIDE] = jnp.where(low, model_sum[...], turned)
    out[:, WIDE:] = jnp.where(low, turned, model_sum[...])


def project(gate_pre, up_pre, hidden_grad, proj_hidden, tokens_in, out_grad, proj_model):
    rows, hidden_width = gate_pre.shape
    model_width = tokens_in.shape[1]
    head, full = cuts_of(hidden_width)
    hidden_slots = len(head) + full
    held = jnp.bfloat16
    return pl.pallas_call(
        project_kernel,
        out_shape=jax.ShapeDtypeStruct((rows, 2 * WIDE), jnp.float32),
        in_specs=[left_in_hbm] * 7,
        out_specs=whole_vmem,
        scratch_shapes=[
            pltpu.VMEM((rows, hidden_width), held),
            pltpu.VMEM((rows, hidden_width), held),
            pltpu.VMEM((rows, hidden_width), held),
            pltpu.VMEM((hidden_width, WIDE), held),
            pltpu.VMEM((rows, model_width), held),
            pltpu.VMEM((rows, model_width), held),
            pltpu.VMEM((model_width, WIDE), held),
            pltpu.VMEM((rows, WIDE), jnp.float32),
            pltpu.VMEM((rows, WIDE), jnp.float32),
            pltpu.SemaphoreType.DMA((hidden_slots, 4)),
            pltpu.SemaphoreType.DMA((model_width // math.gcd(model_width, MODEL_EACH), 3)),
        ],
        compiler_params=pltpu.CompilerParams(vmem_limit_bytes=56 * 10**6),
        name="project",
    )(gate_pre, up_pre, hidden_grad, proj_hidden, tokens_in, out_grad, proj_model)


def gram_kernel(rows_each, count, *refs):
    place, parts, (rows_ref, gram_ref) = refs[0], refs[1 : 1 + count], refs[1 + count :]
    total = parts[0][...]
    for part in parts[1:]:
        total += part[...]
    row = lax.broadcasted_iota(jnp.int32, (WIDE, WIDE), 0)
    lane = lanes_of((WIDE, WIDE))
    low = lanes_of((RANK, WIDE)) < RANK
    gram = jnp.zeros((RANK, WIDE), jnp.float32)
    shift = lax.rem(WIDE - place[0] * rows_each, WIDE)
    for example in range(total.shape[0] // LEN):
        mixed = []
        for at in (0, WIDE):
            sides = total[example * LEN : (example + 1) * LEN, at : at + WIDE]
            crossed = jnp.dot(
                sides.T, sides, precision=highest, preferred_element_type=jnp.float32
            )
            mixed.append(jnp.where((row < RANK) != (lane < RANK), crossed, 0.0))
        up_block, down_block = mixed[0][RANK:], mixed[1][RANK:]
        across = jnp.where(low, up_block, pltpu.roll(down_block, RANK, 1))
        rows_ref[example] = jnp.where(low, pltpu.roll(across, shift, 1), 0.0)
        gram += jnp.dot(
            jnp.concatenate([up_block, down_block], axis=1),
            jnp.concatenate(mixed, axis=0),
            precision=highest,
            preferred_element_type=jnp.float32,
        )
    top, bottom = gram[: RANK // 2], gram[RANK // 2 :]
    gram_ref[...] = jnp.where(
        lanes_of(top.shape) < RANK, pltpu.roll(top, RANK, 1), bottom
    )


def gram_of(place, parts, rows_each):
    examples = parts[0].shape[0] // LEN
    return pl.pallas_call(
        functools.partial(gram_kernel, rows_each, len(parts)),
        out_shape=[
            jax.ShapeDtypeStruct((examples, RANK, WIDE), jnp.float32),
            jax.ShapeDtypeStruct((RANK // 2, WIDE), jnp.float32),
        ],
        in_specs=[pl.BlockSpec(memory_space=pltpu.SMEM)] + [whole_vmem] * len(parts),
        out_specs=[whole_vmem] * 2,
        compiler_params=small,
        name="gram",
    )(place, *parts)


def eliminated(state, spread):
    height = 8
    blocks = len(state)
    state = list(state)
    sub = lax.broadcasted_iota(jnp.int32, state[0].shape, 0)

    def across(block, at):
        return jnp.broadcast_to(block[:, at : at + 1], block.shape)

    def down(which, at):
        return spread[which, pl.ds(at, height, stride=0), :]

    done = []
    for held in range(blocks):
        base = RANK + held * height
        own = state[held]
        first_slot = (held % 2) * (height + 1)
        for k in range(height):
            spread[first_slot + k] = across(own, base + k)
        spread[first_slot + height] = own
        corner = {
            (k, m): down(first_slot + m, k) for k in range(height) for m in range(k, height)
        }
        rows = [down(first_slot + height, k) for k in range(height)]
        ahead = None
        if held + 1 < blocks:
            ahead = [across(state[held + 1], base + k) for k in range(height)]
        factors = {}
        solved = [None] * height
        for k in range(0, height, 2):
            first, cross, second = corner[k, k], corner[k, k + 1], corner[k + 1, k + 1]
            determinant = first * second - cross * cross
            inverse = pl.reciprocal(determinant, approx=True)
            solved[k] = (second * rows[k] - cross * rows[k + 1]) * inverse
            solved[k + 1] = (first * rows[k + 1] - cross * rows[k]) * inverse
            for m in range(k + 2, height):
                left, right = corner[k, m], corner[k + 1, m]
                upper = second * left - cross * right
                lower = first * right - cross * left
                for n in range(m, height):
                    taken = upper * corner[k, n] + lower * corner[k + 1, n]
                    corner[m, n] = corner[m, n] - taken * inverse
                factors[k, m], factors[k + 1, m] = upper * inverse, lower * inverse
                for several in (rows, ahead):
                    if several is not None:
                        several[m] = several[m] - (
                            factors[k, m] * several[k] + factors[k + 1, m] * several[k + 1]
                        )
        if ahead is not None:
            taken = [ahead[k] * solved[k] for k in range(height)]
            while len(taken) > 1:
                taken = [left + right for left, right in zip(taken[::2], taken[1::2])]
            state[held + 1] = state[held + 1] - taken[0]
        if held + 2 < blocks:
            back = list(solved)
            for m in reversed(range(2, height)):
                for k in range(m - m % 2):
                    back[k] = back[k] - factors[k, m] * back[m]
            near = state[held + 2]
            taken = [across(near, base + k) * back[k] for k in range(height)]
            while len(taken) > 1:
                taken = [left + right for left, right in zip(taken[::2], taken[1::2])]
            state[held + 2] = near - taken[0]
        if held + 3 < blocks:
            packed = back[0]
            for k in range(1, height):
                packed = jnp.where(sub == k, back[k], packed)
            weights = [jnp.zeros_like(own)] * (2 * blocks)
            weights[blocks + held] = packed
            later = jnp.concatenate(state[held + 3 :], axis=0)
            later = later - jnp.dot(
                later,
                jnp.concatenate(weights, axis=0),
                precision=highest,
                preferred_element_type=jnp.float32,
            )
            for other in range(held + 3, blocks):
                at = (other - held - 3) * height
                state[other] = later[at : at + height]
        block = jnp.zeros_like(own)
        for k in range(0, height, 2):
            first, cross, second = corner[k, k], corner[k, k + 1], corner[k + 1, k + 1]
            ratio = cross * pl.reciprocal(first, approx=True)
            final = second - cross * ratio
            block = jnp.where(sub == k, rows[k] * lax.rsqrt(first), block)
            block = jnp.where(
                sub == k + 1, (rows[k + 1] - ratio * rows[k]) * lax.rsqrt(final), block
            )
        done.append(block)
    return done


def whiten_kernel(factor, rows_each, rows_ref, gram_ref, out_ref, spread):
    packed = gram_ref[...]
    gram = jnp.concatenate([pltpu.roll(packed, RANK, 1), packed], axis=0)
    low = lanes_of((RANK, WIDE)) < RANK
    for example in range(rows_ref.shape[0]):
        joined = jnp.where(low, rows_ref[example], gram)
        done = eliminated([joined[at : at + 8] for at in range(0, RANK, 8)], spread)
        solved = (jnp.concatenate(done, axis=0) * factor).T
        out_ref[example] = solved[:rows_each, :]


def whiten(rows, gram, rows_each, factor):
    return pl.pallas_call(
        functools.partial(whiten_kernel, factor, rows_each),
        out_shape=jax.ShapeDtypeStruct((rows.shape[0], rows_each, RANK), jnp.float32),
        in_specs=[whole_vmem] * 2,
        out_specs=whole_vmem,
        scratch_shapes=[pltpu.VMEM((18, 8, WIDE), jnp.float32)],
        compiler_params=small,
        name="whiten",
    )(rows, gram)


def summed_over_groups(value):
    groups, model_shards = lax.axis_size("dp"), lax.axis_size("mp")
    place = lax.axis_index("mp")

    def over_groups(value):
        for level in range(groups.bit_length() - 1):
            pairs = [(source, source ^ 2**level) for source in range(groups)]
            value = value + lax.ppermute(value, "dp", pairs)
        return value

    value = lax.cond(place == model_shards - 1, over_groups, lambda value: value, value)
    result = value
    for away in range(1, model_shards):
        pairs = [(source, (source + away) % model_shards) for source in range(model_shards)]
        received = lax.ppermute(value, "mp", pairs)
        result = jnp.where(place == away - 1, received, result)
    return result


def shards(tokens_in, gate_pre, up_pre, hidden_grad, out_grad, proj_model, proj_hidden):
    model_shards = lax.axis_size("mp")
    rows_each = WIDE // model_shards
    local_examples = tokens_in.shape[0] // LEN
    place = lax.axis_index("mp").astype(jnp.int32).reshape(1)
    part = project(
        gate_pre, up_pre, hidden_grad, proj_hidden, tokens_in, out_grad, proj_model
    )
    parts = [part]
    for away in range(1, model_shards):
        pairs = [(source, (source + away) % model_shards) for source in range(model_shards)]
        parts.append(lax.ppermute(part, "mp", pairs))
    rows, gram = gram_of(place, parts, rows_each)
    gram = summed_over_groups(gram)
    factor = math.sqrt(local_examples * lax.axis_size("dp") * 2 * RANK)
    return whiten(rows, gram, rows_each, factor)


def solution(mesh):
    in_specs = (
        P("dp", "mp"),
        P("dp", "mp"),
        P("dp", "mp"),
        P("dp", "mp"),
        P("dp", "mp"),
        P("mp", None),
        P("mp", None),
    )
    out_specs = P("dp", "mp", None)
    return jax.shard_map(shards, mesh=mesh, in_specs=in_specs, out_specs=out_specs, check_vma=False)
```

```python
import functools
import math

import jax
import jax.numpy as jnp
from jax import lax
from jax.experimental import pallas as pl
from jax.experimental.pallas import tpu as pltpu
from jax.sharding import PartitionSpec as P

RANK = 64
LEN = 128
WIDE = 2 * RANK
EACH = 2048
HEAD = 512
LEAST = 256
STEP = 256
AHEAD = 6

highest = lax.Precision.HIGHEST
whole_vmem = pl.BlockSpec(memory_space=pltpu.VMEM)
left_in_hbm = pl.BlockSpec(memory_space=pl.ANY)
small = pltpu.CompilerParams(vmem_limit_bytes=8 * 2**20)


def cuts_of(width):
    full = max((width - 1) // EACH, 0)
    head = width - full * EACH
    ends = [0, min(HEAD, head)]
    while ends[-1] < head:
        ends.append(min(ends[-1] + EACH // 2, head))
    return [(begin, end - begin) for begin, end in zip(ends, ends[1:])], full


def shrinking(width):
    cuts, begin = [], 0
    while begin < width:
        size = width - begin
        if size > LEAST and size % 256 == 0:
            size //= 2
        cuts.append((begin, size))
        begin += size
    return cuts


def lanes_of(shape):
    return lax.broadcasted_iota(jnp.int32, shape, len(shape) - 1)


def paired(left, right, weights):
    low = lanes_of(weights.shape) < RANK
    none = jnp.zeros_like(weights)
    return jnp.dot(
        jnp.concatenate([left, right], axis=1),
        jnp.concatenate([jnp.where(low, weights, none), jnp.where(low, none, weights)], axis=0),
        preferred_element_type=jnp.float32,
    )


def project_kernel(gate, up, grad, proj_hidden, tokens, outer, proj_model, out, *rest):
    gate_v, up_v, grad_v, hidden_w, tokens_v, outer_v, model_w = rest[:7]
    hidden_sum, sems, model_sems = rest[7:]
    rows = gate.shape[0]
    model_cuts = shrinking(tokens.shape[1])
    head, full = cuts_of(gate.shape[1])
    head_width = gate.shape[1] - full * EACH

    def hidden_copies(slot, begin, size):
        cut = pl.ds(pl.multiple_of(begin, 128), size)
        pairs = [
            (gate.at[:, cut], gate_v.at[:, cut]),
            (grad.at[:, cut], grad_v.at[:, cut]),
            (up.at[:, cut], up_v.at[:, cut]),
            (proj_hidden.at[cut, :], hidden_w.at[cut, :]),
        ]
        return [
            pltpu.make_async_copy(source, target, sems.at[slot, which])
            for which, (source, target) in enumerate(pairs)
        ]

    def full_copies(piece):
        return hidden_copies(len(head) + piece, head_width + piece * EACH, EACH)

    def model_copies(piece):
        cut = pl.ds(*model_cuts[piece])
        pairs = [
            (tokens.at[:, cut], tokens_v.at[:, cut]),
            (outer.at[:, cut], outer_v.at[:, cut]),
            (proj_model.at[cut, :], model_w.at[cut, :]),
        ]
        return [
            pltpu.make_async_copy(source, target, model_sems.at[piece, which])
            for which, (source, target) in enumerate(pairs)
        ]

    def start(copies):
        for copy in copies:
            copy.start()

    def arrive(copies):
        for copy in copies:
            copy.wait()

    def start_models():
        for other in range(len(model_cuts)):
            start(model_copies(other))

    def advance(begin, size):
        total = None
        for first in range(0, size, STEP):
            step = min(STEP, size - first)
            cut = pl.ds(pl.multiple_of(begin + first, 128), step)
            half = (gate_v[:, cut] * 0.5).astype(jnp.float32)
            act = half + half * jnp.tanh(half)
            up_grad = (grad_v[:, cut].astype(jnp.float32) * act).astype(jnp.bfloat16)
            hidden = (act * up_v[:, cut].astype(jnp.float32)).astype(jnp.bfloat16)
            part = paired(up_grad, hidden, hidden_w[cut, :])
            total = part if total is None else total + part
        hidden_sum[...] += total

    ahead = min(AHEAD, full)
    for slot, (begin, size) in enumerate(head):
        start(hidden_copies(slot, begin, size))
    for piece in range(ahead):
        start(full_copies(piece))
    if not full:
        start_models()
    hidden_sum[...] = jnp.zeros_like(hidden_sum)
    for slot, (begin, size) in enumerate(head):
        arrive(hidden_copies(slot, begin, size))
        advance(begin, size)

    @pl.loop(0, full)
    def _(piece):
        arrive(full_copies(piece))

        @pl.when(piece + ahead < full)
        def _():
            start(full_copies(piece + ahead))

        @pl.when(piece + ahead == full)
        def _():
            start_models()

        advance(head_width + piece * EACH, EACH)

    total = None
    for piece, (begin, size) in enumerate(model_cuts):
        arrive(model_copies(piece))
        cut = slice(begin, begin + size)
        part = paired(tokens_v[:, cut], outer_v[:, cut], model_w[cut, :])
        total = part if total is None else total + part

    low = lanes_of((rows, WIDE)) < RANK
    turned = pltpu.roll(hidden_sum[...], RANK, 1)
    out[:, :WIDE] = jnp.where(low, total, turned)
    out[:, WIDE:] = jnp.where(low, turned, total)


def project(gate_pre, up_pre, hidden_grad, proj_hidden, tokens_in, out_grad, proj_model):
    rows, hidden_width = gate_pre.shape
    model_width = tokens_in.shape[1]
    head, full = cuts_of(hidden_width)
    hidden_slots = len(head) + full
    held = jnp.bfloat16
    return pl.pallas_call(
        project_kernel,
        out_shape=jax.ShapeDtypeStruct((rows, 2 * WIDE), jnp.float32),
        in_specs=[left_in_hbm] * 7,
        out_specs=whole_vmem,
        scratch_shapes=[
            pltpu.VMEM((rows, hidden_width), held),
            pltpu.VMEM((rows, hidden_width), held),
            pltpu.VMEM((rows, hidden_width), held),
            pltpu.VMEM((hidden_width, WIDE), held),
            pltpu.VMEM((rows, model_width), held),
            pltpu.VMEM((rows, model_width), held),
            pltpu.VMEM((model_width, WIDE), held),
            pltpu.VMEM((rows, WIDE), jnp.float32),
            pltpu.SemaphoreType.DMA((hidden_slots, 4)),
            pltpu.SemaphoreType.DMA((len(shrinking(model_width)), 3)),
        ],
        compiler_params=pltpu.CompilerParams(vmem_limit_bytes=56 * 10**6),
        name="project",
    )(gate_pre, up_pre, hidden_grad, proj_hidden, tokens_in, out_grad, proj_model)


def gram_kernel(rows_each, count, *refs):
    place, parts, (rows_ref, gram_ref) = refs[0], refs[1 : 1 + count], refs[1 + count :]
    total = parts[0][...]
    for part in parts[1:]:
        total += part[...]
    row = lax.broadcasted_iota(jnp.int32, (WIDE, WIDE), 0)
    lane = lanes_of((WIDE, WIDE))
    low = lanes_of((RANK, WIDE)) < RANK
    gram = jnp.zeros((RANK, WIDE), jnp.float32)
    shift = lax.rem(WIDE - place[0] * rows_each, WIDE)
    for example in range(total.shape[0] // LEN):
        mixed = []
        for at in (0, WIDE):
            sides = total[example * LEN : (example + 1) * LEN, at : at + WIDE]
            crossed = jnp.dot(
                sides.T, sides, precision=highest, preferred_element_type=jnp.float32
            )
            mixed.append(jnp.where((row < RANK) != (lane < RANK), crossed, 0.0))
        up_block, down_block = mixed[0][RANK:], mixed[1][RANK:]
        across = jnp.where(low, up_block, pltpu.roll(down_block, RANK, 1))
        rows_ref[example] = jnp.where(low, pltpu.roll(across, shift, 1), 0.0)
        gram += jnp.dot(
            jnp.concatenate([up_block, down_block], axis=1),
            jnp.concatenate(mixed, axis=0),
            precision=highest,
            preferred_element_type=jnp.float32,
        )
    top, bottom = gram[: RANK // 2], gram[RANK // 2 :]
    gram_ref[...] = jnp.where(
        lanes_of(top.shape) < RANK, pltpu.roll(top, RANK, 1), bottom
    )


def gram_of(place, parts, rows_each):
    examples = parts[0].shape[0] // LEN
    return pl.pallas_call(
        functools.partial(gram_kernel, rows_each, len(parts)),
        out_shape=[
            jax.ShapeDtypeStruct((examples, RANK, WIDE), jnp.float32),
            jax.ShapeDtypeStruct((RANK // 2, WIDE), jnp.float32),
        ],
        in_specs=[pl.BlockSpec(memory_space=pltpu.SMEM)] + [whole_vmem] * len(parts),
        out_specs=[whole_vmem] * 2,
        compiler_params=small,
        name="gram",
    )(place, *parts)


def eliminated(state, spread):
    height = 8
    blocks = len(state)
    state = list(state)
    sub = lax.broadcasted_iota(jnp.int32, state[0].shape, 0)

    def across(block, at):
        return jnp.broadcast_to(block[:, at : at + 1], block.shape)

    def down(which, at):
        return spread[which, pl.ds(at, height, stride=0), :]

    done = []
    for held in range(blocks):
        base = RANK + held * height
        own = state[held]
        first_slot = (held % 2) * (height + 1)
        for k in range(height):
            spread[first_slot + k] = across(own, base + k)
        spread[first_slot + height] = own
        corner = {
            (k, m): down(first_slot + m, k) for k in range(height) for m in range(k, height)
        }
        rows = [down(first_slot + height, k) for k in range(height)]
        ahead = None
        if held + 1 < blocks:
            ahead = [across(state[held + 1], base + k) for k in range(height)]
        factors = {}
        solved = [None] * height
        for k in range(0, height, 2):
            first, cross, second = corner[k, k], corner[k, k + 1], corner[k + 1, k + 1]
            determinant = first * second - cross * cross
            inverse = pl.reciprocal(determinant, approx=True)
            solved[k] = (second * rows[k] - cross * rows[k + 1]) * inverse
            solved[k + 1] = (first * rows[k + 1] - cross * rows[k]) * inverse
            for m in range(k + 2, height):
                left, right = corner[k, m], corner[k + 1, m]
                upper = second * left - cross * right
                lower = first * right - cross * left
                for n in range(m, height):
                    taken = upper * corner[k, n] + lower * corner[k + 1, n]
                    corner[m, n] = corner[m, n] - taken * inverse
                factors[k, m], factors[k + 1, m] = upper * inverse, lower * inverse
                for several in (rows, ahead):
                    if several is not None:
                        several[m] = several[m] - (
                            factors[k, m] * several[k] + factors[k + 1, m] * several[k + 1]
                        )
        if ahead is not None:
            taken = [ahead[k] * solved[k] for k in range(height)]
            while len(taken) > 1:
                taken = [left + right for left, right in zip(taken[::2], taken[1::2])]
            state[held + 1] = state[held + 1] - taken[0]
        if held + 2 < blocks:
            back = list(solved)
            for m in reversed(range(2, height)):
                for k in range(m - m % 2):
                    back[k] = back[k] - factors[k, m] * back[m]
            near = state[held + 2]
            taken = [across(near, base + k) * back[k] for k in range(height)]
            while len(taken) > 1:
                taken = [left + right for left, right in zip(taken[::2], taken[1::2])]
            state[held + 2] = near - taken[0]
        if held + 3 < blocks:
            packed = back[0]
            for k in range(1, height):
                packed = jnp.where(sub == k, back[k], packed)
            weights = [jnp.zeros_like(own)] * (2 * blocks)
            weights[blocks + held] = packed
            later = jnp.concatenate(state[held + 3 :], axis=0)
            later = later - jnp.dot(
                later,
                jnp.concatenate(weights, axis=0),
                precision=highest,
                preferred_element_type=jnp.float32,
            )
            for other in range(held + 3, blocks):
                at = (other - held - 3) * height
                state[other] = later[at : at + height]
        block = jnp.zeros_like(own)
        for k in range(0, height, 2):
            first, cross, second = corner[k, k], corner[k, k + 1], corner[k + 1, k + 1]
            ratio = cross * pl.reciprocal(first, approx=True)
            final = second - cross * ratio
            block = jnp.where(sub == k, rows[k] * lax.rsqrt(first), block)
            block = jnp.where(
                sub == k + 1, (rows[k + 1] - ratio * rows[k]) * lax.rsqrt(final), block
            )
        done.append(block)
    return done


def whiten_kernel(factor, rows_each, rows_ref, gram_ref, out_ref, spread):
    packed = gram_ref[...]
    gram = jnp.concatenate([pltpu.roll(packed, RANK, 1), packed], axis=0)
    low = lanes_of((RANK, WIDE)) < RANK
    for example in range(rows_ref.shape[0]):
        joined = jnp.where(low, rows_ref[example], gram)
        done = eliminated([joined[at : at + 8] for at in range(0, RANK, 8)], spread)
        solved = (jnp.concatenate(done, axis=0) * factor).T
        out_ref[example] = solved[:rows_each, :]


def whiten(rows, gram, rows_each, factor):
    return pl.pallas_call(
        functools.partial(whiten_kernel, factor, rows_each),
        out_shape=jax.ShapeDtypeStruct((rows.shape[0], rows_each, RANK), jnp.float32),
        in_specs=[whole_vmem] * 2,
        out_specs=whole_vmem,
        scratch_shapes=[pltpu.VMEM((18, 8, WIDE), jnp.float32)],
        compiler_params=small,
        name="whiten",
    )(rows, gram)


def summed_over_groups(value):
    groups, model_shards = lax.axis_size("dp"), lax.axis_size("mp")
    place = lax.axis_index("mp")

    def over_groups(value):
        for level in range(groups.bit_length() - 1):
            pairs = [(source, source ^ 2**level) for source in range(groups)]
            value = value + lax.ppermute(value, "dp", pairs)
        return value

    value = lax.cond(place == model_shards - 1, over_groups, lambda value: value, value)
    result = value
    for away in range(1, model_shards):
        pairs = [(source, (source + away) % model_shards) for source in range(model_shards)]
        received = lax.ppermute(value, "mp", pairs)
        result = jnp.where(place == away - 1, received, result)
    return result


def shards(tokens_in, gate_pre, up_pre, hidden_grad, out_grad, proj_model, proj_hidden):
    model_shards = lax.axis_size("mp")
    rows_each = WIDE // model_shards
    local_examples = tokens_in.shape[0] // LEN
    place = lax.axis_index("mp").astype(jnp.int32).reshape(1)
    part = project(
        gate_pre, up_pre, hidden_grad, proj_hidden, tokens_in, out_grad, proj_model
    )
    parts = [part]
    for away in range(1, model_shards):
        pairs = [(source, (source + away) % model_shards) for source in range(model_shards)]
        parts.append(lax.ppermute(part, "mp", pairs))
    rows, gram = gram_of(place, parts, rows_each)
    gram = summed_over_groups(gram)
    factor = math.sqrt(local_examples * lax.axis_size("dp") * 2 * RANK)
    return whiten(rows, gram, rows_each, factor)


def solution(mesh):
    in_specs = (
        P("dp", "mp"),
        P("dp", "mp"),
        P("dp", "mp"),
        P("dp", "mp"),
        P("dp", "mp"),
        P("mp", None),
        P("mp", None),
    )
    out_specs = P("dp", "mp", None)
    return jax.shard_map(shards, mesh=mesh, in_specs=in_specs, out_specs=out_specs, check_vma=False)
```

```python
import functools
import math

import jax
import jax.numpy as jnp
from jax import lax
from jax.experimental import pallas as pl
from jax.experimental.pallas import tpu as pltpu
from jax.sharding import PartitionSpec as P

RANK = 64
LEN = 128
WIDE = 2 * RANK
EACH = 2048
HEAD = 512
MODEL_EACH = 1024
STEP = 256
AHEAD = 6

highest = lax.Precision.HIGHEST
whole_vmem = pl.BlockSpec(memory_space=pltpu.VMEM)
left_in_hbm = pl.BlockSpec(memory_space=pl.ANY)
small = pltpu.CompilerParams(vmem_limit_bytes=8 * 2**20)


def cuts_of(width):
    full = max((width - 1) // EACH, 0)
    head = width - full * EACH
    ends = [0, min(HEAD, head)]
    while ends[-1] < head:
        ends.append(min(ends[-1] + EACH // 2, head))
    return [(begin, end - begin) for begin, end in zip(ends, ends[1:])], full


def lanes_of(shape):
    return lax.broadcasted_iota(jnp.int32, shape, len(shape) - 1)


def paired(left, right, weights):
    low = lanes_of(weights.shape) < RANK
    none = jnp.zeros_like(weights)
    return jnp.dot(
        jnp.concatenate([left, right], axis=1),
        jnp.concatenate([jnp.where(low, weights, none), jnp.where(low, none, weights)], axis=0),
        preferred_element_type=jnp.float32,
    )


def paired_across(left, right, weights):
    both = lax.dot_general(
        weights,
        jnp.concatenate([left, right], axis=0),
        (((0,), (1,)), ((), ())),
        preferred_element_type=jnp.float32,
    )
    rows = left.shape[0]
    return jnp.concatenate([both[:RANK, :rows], both[RANK:, rows:]], axis=0)


def project_kernel(gate, up, grad, proj_hidden, tokens, outer, proj_model, out, *rest):
    gate_v, up_v, grad_v, hidden_w, tokens_v, outer_v, model_w = rest[:7]
    hidden_sum, model_sum, hidden_turned, model_turned, sems, model_sems = rest[7:]
    rows = gate.shape[0]
    model_each = math.gcd(tokens.shape[1], MODEL_EACH)
    model_count = tokens.shape[1] // model_each
    head, full = cuts_of(gate.shape[1])
    head_width = gate.shape[1] - full * EACH

    def hidden_copies(slot, begin, size):
        cut = pl.ds(pl.multiple_of(begin, 128), size)
        pairs = [
            (gate.at[:, cut], gate_v.at[:, cut]),
            (grad.at[:, cut], grad_v.at[:, cut]),
            (up.at[:, cut], up_v.at[:, cut]),
            (proj_hidden.at[cut, :], hidden_w.at[cut, :]),
        ]
        return [
            pltpu.make_async_copy(source, target, sems.at[slot, which])
            for which, (source, target) in enumerate(pairs)
        ]

    def full_copies(piece):
        return hidden_copies(len(head) + piece, head_width + piece * EACH, EACH)

    def model_copies(piece):
        cut = pl.ds(pl.multiple_of(piece * model_each, model_each), model_each)
        pairs = [
            (tokens.at[:, cut], tokens_v.at[:, cut]),
            (outer.at[:, cut], outer_v.at[:, cut]),
            (proj_model.at[cut, :], model_w.at[cut, :]),
        ]
        return [
            pltpu.make_async_copy(source, target, model_sems.at[piece, which])
            for which, (source, target) in enumerate(pairs)
        ]

    def start(copies):
        for copy in copies:
            copy.start()

    def arrive(copies):
        for copy in copies:
            copy.wait()

    def start_models():
        for other in range(model_count):
            start(model_copies(other))

    forms = (paired, paired_across)

    def advance(begin, size):
        totals = {}
        for first in range(0, size, STEP):
            step = min(STEP, size - first)
            cut = pl.ds(pl.multiple_of(begin + first, 128), step)
            half = (gate_v[:, cut] * 0.5).astype(jnp.float32)
            act = half + half * jnp.tanh(half)
            up_grad = (grad_v[:, cut].astype(jnp.float32) * act).astype(jnp.bfloat16)
            hidden = (act * up_v[:, cut].astype(jnp.float32)).astype(jnp.bfloat16)
            form = forms[first // STEP % 2]
            part = form(up_grad, hidden, hidden_w[cut, :])
            totals[form] = totals[form] + part if form in totals else part
        for form, sums in zip(forms, (hidden_sum, hidden_turned)):
            if form in totals:
                sums[...] += totals[form]

    ahead = min(AHEAD, full)
    for slot, (begin, size) in enumerate(head):
        start(hidden_copies(slot, begin, size))
    for piece in range(ahead):
        start(full_copies(piece))
    if not full:
        start_models()
    hidden_sum[...] = jnp.zeros_like(hidden_sum)
    for sums in (model_sum, hidden_turned, model_turned):
        sums[...] = jnp.zeros_like(sums)
    for slot, (begin, size) in enumerate(head):
        arrive(hidden_copies(slot, begin, size))
        advance(begin, size)

    @pl.loop(0, full)
    def _(piece):
        arrive(full_copies(piece))

        @pl.when(piece + ahead < full)
        def _():
            start(full_copies(piece + ahead))

        @pl.when(piece + ahead == full)
        def _():
            start_models()

        advance(head_width + piece * EACH, EACH)

    @pl.loop(0, model_count)
    def _(piece):
        arrive(model_copies(piece))
        half = model_each // 2 if model_each % 256 == 0 else model_each
        begin = pl.multiple_of(piece * model_each, model_each)
        for first, form, sums in zip(
            range(0, model_each, half), forms, (model_sum, model_turned)
        ):
            cut = pl.ds(pl.multiple_of(begin + first, 128), half)
            sums[...] += form(tokens_v[:, cut], outer_v[:, cut], model_w[cut, :])

    low = lanes_of((rows, WIDE)) < RANK
    turned = pltpu.roll(hidden_sum[...] + hidden_turned[...].T, RANK, 1)
    straight = model_sum[...] + model_turned[...].T
    out[:, :WIDE] = jnp.where(low, straight, turned)
    out[:, WIDE:] = jnp.where(low, turned, straight)


def project(gate_pre, up_pre, hidden_grad, proj_hidden, tokens_in, out_grad, proj_model):
    rows, hidden_width = gate_pre.shape
    model_width = tokens_in.shape[1]
    head, full = cuts_of(hidden_width)
    hidden_slots = len(head) + full
    held = jnp.bfloat16
    return pl.pallas_call(
        project_kernel,
        out_shape=jax.ShapeDtypeStruct((rows, 2 * WIDE), jnp.float32),
        in_specs=[left_in_hbm] * 7,
        out_specs=whole_vmem,
        scratch_shapes=[
            pltpu.VMEM((rows, hidden_width), held),
            pltpu.VMEM((rows, hidden_width), held),
            pltpu.VMEM((rows, hidden_width), held),
            pltpu.VMEM((hidden_width, WIDE), held),
            pltpu.VMEM((rows, model_width), held),
            pltpu.VMEM((rows, model_width), held),
            pltpu.VMEM((model_width, WIDE), held),
            pltpu.VMEM((rows, WIDE), jnp.float32),
            pltpu.VMEM((rows, WIDE), jnp.float32),
            pltpu.VMEM((WIDE, rows), jnp.float32),
            pltpu.VMEM((WIDE, rows), jnp.float32),
            pltpu.SemaphoreType.DMA((hidden_slots, 4)),
            pltpu.SemaphoreType.DMA((model_width // math.gcd(model_width, MODEL_EACH), 3)),
        ],
        compiler_params=pltpu.CompilerParams(vmem_limit_bytes=56 * 10**6),
        name="project",
    )(gate_pre, up_pre, hidden_grad, proj_hidden, tokens_in, out_grad, proj_model)


def gram_kernel(rows_each, count, *refs):
    place, parts, (rows_ref, gram_ref) = refs[0], refs[1 : 1 + count], refs[1 + count :]
    total = parts[0][...]
    for part in parts[1:]:
        total += part[...]
    row = lax.broadcasted_iota(jnp.int32, (WIDE, WIDE), 0)
    lane = lanes_of((WIDE, WIDE))
    low = lanes_of((RANK, WIDE)) < RANK
    gram = jnp.zeros((RANK, WIDE), jnp.float32)
    shift = lax.rem(WIDE - place[0] * rows_each, WIDE)
    for example in range(total.shape[0] // LEN):
        mixed = []
        for at in (0, WIDE):
            sides = total[example * LEN : (example + 1) * LEN, at : at + WIDE]
            crossed = jnp.dot(
                sides.T, sides, precision=highest, preferred_element_type=jnp.float32
            )
            mixed.append(jnp.where((row < RANK) != (lane < RANK), crossed, 0.0))
        up_block, down_block = mixed[0][RANK:], mixed[1][RANK:]
        across = jnp.where(low, up_block, pltpu.roll(down_block, RANK, 1))
        rows_ref[example] = jnp.where(low, pltpu.roll(across, shift, 1), 0.0)
        gram += jnp.dot(
            jnp.concatenate([up_block, down_block], axis=1),
            jnp.concatenate(mixed, axis=0),
            precision=highest,
            preferred_element_type=jnp.float32,
        )
    top, bottom = gram[: RANK // 2], gram[RANK // 2 :]
    gram_ref[...] = jnp.where(
        lanes_of(top.shape) < RANK, pltpu.roll(top, RANK, 1), bottom
    )


def gram_of(place, parts, rows_each):
    examples = parts[0].shape[0] // LEN
    return pl.pallas_call(
        functools.partial(gram_kernel, rows_each, len(parts)),
        out_shape=[
            jax.ShapeDtypeStruct((examples, RANK, WIDE), jnp.float32),
            jax.ShapeDtypeStruct((RANK // 2, WIDE), jnp.float32),
        ],
        in_specs=[pl.BlockSpec(memory_space=pltpu.SMEM)] + [whole_vmem] * len(parts),
        out_specs=[whole_vmem] * 2,
        compiler_params=small,
        name="gram",
    )(place, *parts)


def eliminated(state, spread):
    height = 8
    blocks = len(state)
    state = list(state)
    sub = lax.broadcasted_iota(jnp.int32, state[0].shape, 0)

    def across(block, at):
        return jnp.broadcast_to(block[:, at : at + 1], block.shape)

    def down(which, at):
        return spread[which, pl.ds(at, height, stride=0), :]

    done = []
    for held in range(blocks):
        base = RANK + held * height
        own = state[held]
        first_slot = (held % 2) * (height + 1)
        for k in range(height):
            spread[first_slot + k] = across(own, base + k)
        spread[first_slot + height] = own
        corner = {
            (k, m): down(first_slot + m, k) for k in range(height) for m in range(k, height)
        }
        rows = [down(first_slot + height, k) for k in range(height)]
        ahead = None
        if held + 1 < blocks:
            ahead = [across(state[held + 1], base + k) for k in range(height)]
        factors = {}
        solved = [None] * height
        for k in range(0, height, 2):
            first, cross, second = corner[k, k], corner[k, k + 1], corner[k + 1, k + 1]
            determinant = first * second - cross * cross
            inverse = pl.reciprocal(determinant, approx=True)
            solved[k] = (second * rows[k] - cross * rows[k + 1]) * inverse
            solved[k + 1] = (first * rows[k + 1] - cross * rows[k]) * inverse
            for m in range(k + 2, height):
                left, right = corner[k, m], corner[k + 1, m]
                upper = second * left - cross * right
                lower = first * right - cross * left
                for n in range(m, height):
                    taken = upper * corner[k, n] + lower * corner[k + 1, n]
                    corner[m, n] = corner[m, n] - taken * inverse
                factors[k, m], factors[k + 1, m] = upper * inverse, lower * inverse
                for several in (rows, ahead):
                    if several is not None:
                        several[m] = several[m] - (
                            factors[k, m] * several[k] + factors[k + 1, m] * several[k + 1]
                        )
        if ahead is not None:
            taken = [ahead[k] * solved[k] for k in range(height)]
            while len(taken) > 1:
                taken = [left + right for left, right in zip(taken[::2], taken[1::2])]
            state[held + 1] = state[held + 1] - taken[0]
        if held + 2 < blocks:
            back = list(solved)
            for m in reversed(range(2, height)):
                for k in range(m - m % 2):
                    back[k] = back[k] - factors[k, m] * back[m]
            near = state[held + 2]
            taken = [across(near, base + k) * back[k] for k in range(height)]
            while len(taken) > 1:
                taken = [left + right for left, right in zip(taken[::2], taken[1::2])]
            state[held + 2] = near - taken[0]
        if held + 3 < blocks:
            packed = back[0]
            for k in range(1, height):
                packed = jnp.where(sub == k, back[k], packed)
            weights = [jnp.zeros_like(own)] * (2 * blocks)
            weights[blocks + held] = packed
            later = jnp.concatenate(state[held + 3 :], axis=0)
            later = later - jnp.dot(
                later,
                jnp.concatenate(weights, axis=0),
                precision=highest,
                preferred_element_type=jnp.float32,
            )
            for other in range(held + 3, blocks):
                at = (other - held - 3) * height
                state[other] = later[at : at + height]
        block = jnp.zeros_like(own)
        for k in range(0, height, 2):
            first, cross, second = corner[k, k], corner[k, k + 1], corner[k + 1, k + 1]
            ratio = cross * pl.reciprocal(first, approx=True)
            final = second - cross * ratio
            block = jnp.where(sub == k, rows[k] * lax.rsqrt(first), block)
            block = jnp.where(
                sub == k + 1, (rows[k + 1] - ratio * rows[k]) * lax.rsqrt(final), block
            )
        done.append(block)
    return done


def whiten_kernel(factor, rows_each, rows_ref, gram_ref, out_ref, spread):
    packed = gram_ref[...]
    gram = jnp.concatenate([pltpu.roll(packed, RANK, 1), packed], axis=0)
    low = lanes_of((RANK, WIDE)) < RANK
    for example in range(rows_ref.shape[0]):
        joined = jnp.where(low, rows_ref[example], gram)
        done = eliminated([joined[at : at + 8] for at in range(0, RANK, 8)], spread)
        solved = (jnp.concatenate(done, axis=0) * factor).T
        out_ref[example] = solved[:rows_each, :]


def whiten(rows, gram, rows_each, factor):
    return pl.pallas_call(
        functools.partial(whiten_kernel, factor, rows_each),
        out_shape=jax.ShapeDtypeStruct((rows.shape[0], rows_each, RANK), jnp.float32),
        in_specs=[whole_vmem] * 2,
        out_specs=whole_vmem,
        scratch_shapes=[pltpu.VMEM((18, 8, WIDE), jnp.float32)],
        compiler_params=small,
        name="whiten",
    )(rows, gram)


def summed_over_groups(value):
    groups, model_shards = lax.axis_size("dp"), lax.axis_size("mp")
    place = lax.axis_index("mp")

    def over_groups(value):
        for level in range(groups.bit_length() - 1):
            pairs = [(source, source ^ 2**level) for source in range(groups)]
            value = value + lax.ppermute(value, "dp", pairs)
        return value

    value = lax.cond(place == model_shards - 1, over_groups, lambda value: value, value)
    result = value
    for away in range(1, model_shards):
        pairs = [(source, (source + away) % model_shards) for source in range(model_shards)]
        received = lax.ppermute(value, "mp", pairs)
        result = jnp.where(place == away - 1, received, result)
    return result


def shards(tokens_in, gate_pre, up_pre, hidden_grad, out_grad, proj_model, proj_hidden):
    model_shards = lax.axis_size("mp")
    rows_each = WIDE // model_shards
    local_examples = tokens_in.shape[0] // LEN
    place = lax.axis_index("mp").astype(jnp.int32).reshape(1)
    part = project(
        gate_pre, up_pre, hidden_grad, proj_hidden, tokens_in, out_grad, proj_model
    )
    parts = [part]
    for away in range(1, model_shards):
        pairs = [(source, (source + away) % model_shards) for source in range(model_shards)]
        parts.append(lax.ppermute(part, "mp", pairs))
    rows, gram = gram_of(place, parts, rows_each)
    gram = summed_over_groups(gram)
    factor = math.sqrt(local_examples * lax.axis_size("dp") * 2 * RANK)
    return whiten(rows, gram, rows_each, factor)


def solution(mesh):
    in_specs = (
        P("dp", "mp"),
        P("dp", "mp"),
        P("dp", "mp"),
        P("dp", "mp"),
        P("dp", "mp"),
        P("mp", None),
        P("mp", None),
    )
    out_specs = P("dp", "mp", None)
    return jax.shard_map(shards, mesh=mesh, in_specs=in_specs, out_specs=out_specs, check_vma=False)
```

```python
import functools
import math

import jax
import jax.numpy as jnp
from jax import lax
from jax.experimental import pallas as pl
from jax.experimental.pallas import tpu as pltpu
from jax.sharding import PartitionSpec as P

RANK = 64
LEN = 128
WIDE = 2 * RANK
EACH = 4096
BODY = 2048
HEAD = 512
MODEL_EACH = 2048
STEP = 256
AHEAD = 4

highest = lax.Precision.HIGHEST
whole_vmem = pl.BlockSpec(memory_space=pltpu.VMEM)
left_in_hbm = pl.BlockSpec(memory_space=pl.ANY)
small = pltpu.CompilerParams(vmem_limit_bytes=8 * 2**20)


def cuts_of(width):
    full = max((width - 1) // EACH, 0)
    head = width - full * EACH
    ends = [0, min(HEAD, head)]
    while ends[-1] < head:
        ends.append(min(ends[-1] + BODY // 2, head))
    return [(begin, end - begin) for begin, end in zip(ends, ends[1:])], full


def lanes_of(shape):
    return lax.broadcasted_iota(jnp.int32, shape, len(shape) - 1)


def paired(left, right, weights):
    low = lanes_of(weights.shape) < RANK
    none = jnp.zeros_like(weights)
    return jnp.dot(
        jnp.concatenate([left, right], axis=1),
        jnp.concatenate([jnp.where(low, weights, none), jnp.where(low, none, weights)], axis=0),
        preferred_element_type=jnp.float32,
    )


def project_kernel(gate, up, grad, proj_hidden, tokens, outer, proj_model, out, *rest):
    gate_v, up_v, grad_v, hidden_w, tokens_v, outer_v, model_w = rest[:7]
    hidden_sum, model_sum, sems, model_sems = rest[7:]
    rows = gate.shape[0]
    model_each = math.gcd(tokens.shape[1], MODEL_EACH)
    model_count = tokens.shape[1] // model_each
    head, full = cuts_of(gate.shape[1])
    head_width = gate.shape[1] - full * EACH

    def hidden_copies(slot, begin, size):
        cut = pl.ds(pl.multiple_of(begin, 128), size)
        pairs = [
            (gate.at[:, cut], gate_v.at[:, cut]),
            (grad.at[:, cut], grad_v.at[:, cut]),
            (up.at[:, cut], up_v.at[:, cut]),
            (proj_hidden.at[cut, :], hidden_w.at[cut, :]),
        ]
        return [
            pltpu.make_async_copy(source, target, sems.at[slot, which])
            for which, (source, target) in enumerate(pairs)
        ]

    def full_copies(piece):
        return hidden_copies(len(head) + piece, head_width + piece * EACH, EACH)

    def model_copies(piece):
        cut = pl.ds(pl.multiple_of(piece * model_each, model_each), model_each)
        pairs = [
            (tokens.at[:, cut], tokens_v.at[:, cut]),
            (outer.at[:, cut], outer_v.at[:, cut]),
            (proj_model.at[cut, :], model_w.at[cut, :]),
        ]
        return [
            pltpu.make_async_copy(source, target, model_sems.at[piece, which])
            for which, (source, target) in enumerate(pairs)
        ]

    def start(copies):
        for copy in copies:
            copy.start()

    def arrive(copies):
        for copy in copies:
            copy.wait()

    def start_models():
        for other in range(model_count):
            start(model_copies(other))

    def advance(begin, size):
        total = None
        for first in range(0, size, STEP):
            step = min(STEP, size - first)
            cut = pl.ds(pl.multiple_of(begin + first, 128), step)
            half = (gate_v[:, cut] * 0.5).astype(jnp.float32)
            act = half + half * jnp.tanh(half)
            up_grad = (grad_v[:, cut].astype(jnp.float32) * act).astype(jnp.bfloat16)
            hidden = (act * up_v[:, cut].astype(jnp.float32)).astype(jnp.bfloat16)
            part = paired(up_grad, hidden, hidden_w[cut, :])
            total = part if total is None else total + part
        hidden_sum[...] += total

    ahead = min(AHEAD, full)
    for slot, (begin, size) in enumerate(head):
        start(hidden_copies(slot, begin, size))
    for piece in range(ahead):
        start(full_copies(piece))
    if not full:
        start_models()
    hidden_sum[...] = jnp.zeros_like(hidden_sum)
    model_sum[...] = jnp.zeros_like(model_sum)
    for slot, (begin, size) in enumerate(head):
        arrive(hidden_copies(slot, begin, size))
        advance(begin, size)

    @pl.loop(0, full)
    def _(piece):
        arrive(full_copies(piece))

        @pl.when(piece + ahead < full)
        def _():
            start(full_copies(piece + ahead))

        @pl.when(piece + ahead == full)
        def _():
            start_models()

        @pl.loop(0, EACH // BODY)
        def _(part):
            advance(head_width + piece * EACH + part * BODY, BODY)

    @pl.loop(0, model_count)
    def _(piece):
        arrive(model_copies(piece))
        cut = pl.ds(pl.multiple_of(piece * model_each, model_each), model_each)
        model_sum[...] += paired(tokens_v[:, cut], outer_v[:, cut], model_w[cut, :])

    low = lanes_of((rows, WIDE)) < RANK
    turned = pltpu.roll(hidden_sum[...], RANK, 1)
    out[:, :WIDE] = jnp.where(low, model_sum[...], turned)
    out[:, WIDE:] = jnp.where(low, turned, model_sum[...])


def project(gate_pre, up_pre, hidden_grad, proj_hidden, tokens_in, out_grad, proj_model):
    rows, hidden_width = gate_pre.shape
    model_width = tokens_in.shape[1]
    head, full = cuts_of(hidden_width)
    hidden_slots = len(head) + full
    held = jnp.bfloat16
    return pl.pallas_call(
        project_kernel,
        out_shape=jax.ShapeDtypeStruct((rows, 2 * WIDE), jnp.float32),
        in_specs=[left_in_hbm] * 7,
        out_specs=whole_vmem,
        scratch_shapes=[
            pltpu.VMEM((rows, hidden_width), held),
            pltpu.VMEM((rows, hidden_width), held),
            pltpu.VMEM((rows, hidden_width), held),
            pltpu.VMEM((hidden_width, WIDE), held),
            pltpu.VMEM((rows, model_width), held),
            pltpu.VMEM((rows, model_width), held),
            pltpu.VMEM((model_width, WIDE), held),
            pltpu.VMEM((rows, WIDE), jnp.float32),
            pltpu.VMEM((rows, WIDE), jnp.float32),
            pltpu.SemaphoreType.DMA((hidden_slots, 4)),
            pltpu.SemaphoreType.DMA((model_width // math.gcd(model_width, MODEL_EACH), 3)),
        ],
        compiler_params=pltpu.CompilerParams(vmem_limit_bytes=56 * 10**6),
        name="project",
    )(gate_pre, up_pre, hidden_grad, proj_hidden, tokens_in, out_grad, proj_model)


def gram_kernel(rows_each, count, *refs):
    place, parts, (rows_ref, gram_ref) = refs[0], refs[1 : 1 + count], refs[1 + count :]
    total = parts[0][...]
    for part in parts[1:]:
        total += part[...]
    row = lax.broadcasted_iota(jnp.int32, (WIDE, WIDE), 0)
    lane = lanes_of((WIDE, WIDE))
    low = lanes_of((RANK, WIDE)) < RANK
    gram = jnp.zeros((RANK, WIDE), jnp.float32)
    shift = lax.rem(WIDE - place[0] * rows_each, WIDE)
    for example in range(total.shape[0] // LEN):
        mixed = []
        for at in (0, WIDE):
            sides = total[example * LEN : (example + 1) * LEN, at : at + WIDE]
            crossed = jnp.dot(
                sides.T, sides, precision=highest, preferred_element_type=jnp.float32
            )
            mixed.append(jnp.where((row < RANK) != (lane < RANK), crossed, 0.0))
        up_block, down_block = mixed[0][RANK:], mixed[1][RANK:]
        across = jnp.where(low, up_block, pltpu.roll(down_block, RANK, 1))
        rows_ref[example] = jnp.where(low, pltpu.roll(across, shift, 1), 0.0)
        gram += jnp.dot(
            jnp.concatenate([up_block, down_block], axis=1),
            jnp.concatenate(mixed, axis=0),
            precision=highest,
            preferred_element_type=jnp.float32,
        )
    top, bottom = gram[: RANK // 2], gram[RANK // 2 :]
    gram_ref[...] = jnp.where(
        lanes_of(top.shape) < RANK, pltpu.roll(top, RANK, 1), bottom
    )


def gram_of(place, parts, rows_each):
    examples = parts[0].shape[0] // LEN
    return pl.pallas_call(
        functools.partial(gram_kernel, rows_each, len(parts)),
        out_shape=[
            jax.ShapeDtypeStruct((examples, RANK, WIDE), jnp.float32),
            jax.ShapeDtypeStruct((RANK // 2, WIDE), jnp.float32),
        ],
        in_specs=[pl.BlockSpec(memory_space=pltpu.SMEM)] + [whole_vmem] * len(parts),
        out_specs=[whole_vmem] * 2,
        compiler_params=small,
        name="gram",
    )(place, *parts)


def eliminated(state, spread):
    height = 8
    blocks = len(state)
    state = list(state)
    sub = lax.broadcasted_iota(jnp.int32, state[0].shape, 0)

    def across(block, at):
        return jnp.broadcast_to(block[:, at : at + 1], block.shape)

    def down(which, at):
        return spread[which, pl.ds(at, height, stride=0), :]

    done = []
    for held in range(blocks):
        base = RANK + held * height
        own = state[held]
        first_slot = (held % 2) * (height + 1)
        for k in range(height):
            spread[first_slot + k] = across(own, base + k)
        spread[first_slot + height] = own
        corner = {
            (k, m): down(first_slot + m, k) for k in range(height) for m in range(k, height)
        }
        rows = [down(first_slot + height, k) for k in range(height)]
        ahead = None
        if held + 1 < blocks:
            ahead = [across(state[held + 1], base + k) for k in range(height)]
        factors = {}
        solved = [None] * height
        for k in range(0, height, 2):
            first, cross, second = corner[k, k], corner[k, k + 1], corner[k + 1, k + 1]
            determinant = first * second - cross * cross
            inverse = pl.reciprocal(determinant, approx=True)
            solved[k] = (second * rows[k] - cross * rows[k + 1]) * inverse
            solved[k + 1] = (first * rows[k + 1] - cross * rows[k]) * inverse
            for m in range(k + 2, height):
                left, right = corner[k, m], corner[k + 1, m]
                upper = second * left - cross * right
                lower = first * right - cross * left
                for n in range(m, height):
                    taken = upper * corner[k, n] + lower * corner[k + 1, n]
                    corner[m, n] = corner[m, n] - taken * inverse
                factors[k, m], factors[k + 1, m] = upper * inverse, lower * inverse
                for several in (rows, ahead):
                    if several is not None:
                        several[m] = several[m] - (
                            factors[k, m] * several[k] + factors[k + 1, m] * several[k + 1]
                        )
        if ahead is not None:
            taken = [ahead[k] * solved[k] for k in range(height)]
            while len(taken) > 1:
                taken = [left + right for left, right in zip(taken[::2], taken[1::2])]
            state[held + 1] = state[held + 1] - taken[0]
        if held + 2 < blocks:
            back = list(solved)
            for m in reversed(range(2, height)):
                for k in range(m - m % 2):
                    back[k] = back[k] - factors[k, m] * back[m]
            near = state[held + 2]
            taken = [across(near, base + k) * back[k] for k in range(height)]
            while len(taken) > 1:
                taken = [left + right for left, right in zip(taken[::2], taken[1::2])]
            state[held + 2] = near - taken[0]
        if held + 3 < blocks:
            packed = back[0]
            for k in range(1, height):
                packed = jnp.where(sub == k, back[k], packed)
            weights = [jnp.zeros_like(own)] * (2 * blocks)
            weights[blocks + held] = packed
            later = jnp.concatenate(state[held + 3 :], axis=0)
            later = later - jnp.dot(
                later,
                jnp.concatenate(weights, axis=0),
                precision=highest,
                preferred_element_type=jnp.float32,
            )
            for other in range(held + 3, blocks):
                at = (other - held - 3) * height
                state[other] = later[at : at + height]
        block = jnp.zeros_like(own)
        for k in range(0, height, 2):
            first, cross, second = corner[k, k], corner[k, k + 1], corner[k + 1, k + 1]
            ratio = cross * pl.reciprocal(first, approx=True)
            final = second - cross * ratio
            block = jnp.where(sub == k, rows[k] * lax.rsqrt(first), block)
            block = jnp.where(
                sub == k + 1, (rows[k + 1] - ratio * rows[k]) * lax.rsqrt(final), block
            )
        done.append(block)
    return done


def whiten_kernel(factor, rows_each, rows_ref, gram_ref, out_ref, spread):
    packed = gram_ref[...]
    gram = jnp.concatenate([pltpu.roll(packed, RANK, 1), packed], axis=0)
    low = lanes_of((RANK, WIDE)) < RANK
    for example in range(rows_ref.shape[0]):
        joined = jnp.where(low, rows_ref[example], gram)
        done = eliminated([joined[at : at + 8] for at in range(0, RANK, 8)], spread)
        solved = (jnp.concatenate(done, axis=0) * factor).T
        out_ref[example] = solved[:rows_each, :]


def whiten(rows, gram, rows_each, factor):
    return pl.pallas_call(
        functools.partial(whiten_kernel, factor, rows_each),
        out_shape=jax.ShapeDtypeStruct((rows.shape[0], rows_each, RANK), jnp.float32),
        in_specs=[whole_vmem] * 2,
        out_specs=whole_vmem,
        scratch_shapes=[pltpu.VMEM((18, 8, WIDE), jnp.float32)],
        compiler_params=small,
        name="whiten",
    )(rows, gram)


def summed_over_groups(value):
    groups, model_shards = lax.axis_size("dp"), lax.axis_size("mp")
    place = lax.axis_index("mp")

    def over_groups(value):
        for level in range(groups.bit_length() - 1):
            pairs = [(source, source ^ 2**level) for source in range(groups)]
            value = value + lax.ppermute(value, "dp", pairs)
        return value

    value = lax.cond(place == model_shards - 1, over_groups, lambda value: value, value)
    result = value
    for away in range(1, model_shards):
        pairs = [(source, (source + away) % model_shards) for source in range(model_shards)]
        received = lax.ppermute(value, "mp", pairs)
        result = jnp.where(place == away - 1, received, result)
    return result


def shards(tokens_in, gate_pre, up_pre, hidden_grad, out_grad, proj_model, proj_hidden):
    model_shards = lax.axis_size("mp")
    rows_each = WIDE // model_shards
    local_examples = tokens_in.shape[0] // LEN
    place = lax.axis_index("mp").astype(jnp.int32).reshape(1)
    part = project(
        gate_pre, up_pre, hidden_grad, proj_hidden, tokens_in, out_grad, proj_model
    )
    parts = [part]
    for away in range(1, model_shards):
        pairs = [(source, (source + away) % model_shards) for source in range(model_shards)]
        parts.append(lax.ppermute(part, "mp", pairs))
    rows, gram = gram_of(place, parts, rows_each)
    gram = summed_over_groups(gram)
    factor = math.sqrt(local_examples * lax.axis_size("dp") * 2 * RANK)
    return whiten(rows, gram, rows_each, factor)


def solution(mesh):
    in_specs = (
        P("dp", "mp"),
        P("dp", "mp"),
        P("dp", "mp"),
        P("dp", "mp"),
        P("dp", "mp"),
        P("mp", None),
        P("mp", None),
    )
    out_specs = P("dp", "mp", None)
    return jax.shard_map(shards, mesh=mesh, in_specs=in_specs, out_specs=out_specs, check_vma=False)
```

```python
import functools
import math

import jax
import jax.numpy as jnp
from jax import lax
from jax.experimental import pallas as pl
from jax.experimental.pallas import tpu as pltpu
from jax.sharding import PartitionSpec as P

RANK = 64
LEN = 128
WIDE = 2 * RANK
EACH = 2048
HEAD = 512
MODEL_EACH = 1024
STEP = 256
AHEAD = 6

highest = lax.Precision.HIGHEST
whole_vmem = pl.BlockSpec(memory_space=pltpu.VMEM)
left_in_hbm = pl.BlockSpec(memory_space=pl.ANY)
small = pltpu.CompilerParams(vmem_limit_bytes=8 * 2**20)


def cuts_of(width):
    full = max((width - 1) // EACH, 0)
    head = width - full * EACH
    ends = [0, min(HEAD, head)]
    while ends[-1] < head:
        ends.append(min(ends[-1] + EACH // 2, head))
    return [(begin, end - begin) for begin, end in zip(ends, ends[1:])], full


def lanes_of(shape):
    return lax.broadcasted_iota(jnp.int32, shape, len(shape) - 1)


def paired(left, right, weights):
    low = lanes_of(weights.shape) < RANK
    none = jnp.zeros_like(weights)
    return jnp.dot(
        jnp.concatenate([left, right], axis=1),
        jnp.concatenate([jnp.where(low, weights, none), jnp.where(low, none, weights)], axis=0),
        preferred_element_type=jnp.float32,
    )


def project_kernel(gate, up, grad, proj_hidden, tokens, outer, proj_model, out, *rest):
    gate_v, up_v, grad_v, hidden_w, tokens_v, outer_v, model_w = rest[:7]
    hidden_sum, model_sum, sems, model_sems = rest[7:]
    rows = gate.shape[0]
    model_each = math.gcd(tokens.shape[1], MODEL_EACH)
    model_count = tokens.shape[1] // model_each
    head, full = cuts_of(gate.shape[1])
    head_width = gate.shape[1] - full * EACH

    def hidden_copies(slot, begin, size):
        cut = pl.ds(pl.multiple_of(begin, 128), size)
        pairs = [
            (gate.at[:, cut], gate_v.at[:, cut]),
            (grad.at[:, cut], grad_v.at[:, cut]),
            (up.at[:, cut], up_v.at[:, cut]),
            (proj_hidden.at[cut, :], hidden_w.at[cut, :]),
        ]
        return [
            pltpu.make_async_copy(source, target, sems.at[slot, which])
            for which, (source, target) in enumerate(pairs)
        ]

    def full_copies(piece):
        return hidden_copies(len(head) + piece, head_width + piece * EACH, EACH)

    def model_copies(piece):
        cut = pl.ds(pl.multiple_of(piece * model_each, model_each), model_each)
        pairs = [
            (tokens.at[:, cut], tokens_v.at[:, cut]),
            (outer.at[:, cut], outer_v.at[:, cut]),
            (proj_model.at[cut, :], model_w.at[cut, :]),
        ]
        return [
            pltpu.make_async_copy(source, target, model_sems.at[piece, which])
            for which, (source, target) in enumerate(pairs)
        ]

    def start(copies):
        for copy in copies:
            copy.start()

    def arrive(copies):
        for copy in copies:
            copy.wait()

    def start_models():
        for other in range(model_count):
            start(model_copies(other))

    def advance(begin, size):
        total = None
        for first in range(0, size, STEP):
            step = min(STEP, size - first)
            cut = pl.ds(pl.multiple_of(begin + first, 128), step)
            half = (gate_v[:, cut] * 0.5).astype(jnp.float32)
            act = half + half * jnp.tanh(half)
            up_grad = (grad_v[:, cut].astype(jnp.float32) * act).astype(jnp.bfloat16)
            hidden = (act * up_v[:, cut].astype(jnp.float32)).astype(jnp.bfloat16)
            part = paired(up_grad, hidden, hidden_w[cut, :])
            total = part if total is None else total + part
        hidden_sum[...] += total

    ahead = min(AHEAD, full)
    for slot, (begin, size) in enumerate(head):
        start(hidden_copies(slot, begin, size))
    for piece in range(ahead):
        start(full_copies(piece))
    if not full:
        start_models()
    hidden_sum[...] = jnp.zeros_like(hidden_sum)
    model_sum[...] = jnp.zeros_like(model_sum)
    for slot, (begin, size) in enumerate(head):
        arrive(hidden_copies(slot, begin, size))
        advance(begin, size)

    @pl.loop(0, full)
    def _(piece):
        arrive(full_copies(piece))

        @pl.when(piece + ahead < full)
        def _():
            start(full_copies(piece + ahead))

        @pl.when(piece + ahead == full)
        def _():
            start_models()

        advance(head_width + piece * EACH, EACH)

    @pl.loop(0, model_count)
    def _(piece):
        arrive(model_copies(piece))
        cut = pl.ds(pl.multiple_of(piece * model_each, model_each), model_each)
        model_sum[...] += paired(tokens_v[:, cut], outer_v[:, cut], model_w[cut, :])

    low = lanes_of((rows, WIDE)) < RANK
    turned = pltpu.roll(hidden_sum[...], RANK, 1)
    out[:, :WIDE] = jnp.where(low, model_sum[...], turned)
    out[:, WIDE:] = jnp.where(low, turned, model_sum[...])


def project(gate_pre, up_pre, hidden_grad, proj_hidden, tokens_in, out_grad, proj_model):
    rows, hidden_width = gate_pre.shape
    model_width = tokens_in.shape[1]
    head, full = cuts_of(hidden_width)
    hidden_slots = len(head) + full
    held = jnp.bfloat16
    return pl.pallas_call(
        project_kernel,
        out_shape=jax.ShapeDtypeStruct((rows, 2 * WIDE), jnp.float32),
        in_specs=[left_in_hbm] * 7,
        out_specs=whole_vmem,
        scratch_shapes=[
            pltpu.VMEM((rows, hidden_width), held),
            pltpu.VMEM((rows, hidden_width), held),
            pltpu.VMEM((rows, hidden_width), held),
            pltpu.VMEM((hidden_width, WIDE), held),
            pltpu.VMEM((rows, model_width), held),
            pltpu.VMEM((rows, model_width), held),
            pltpu.VMEM((model_width, WIDE), held),
            pltpu.VMEM((rows, WIDE), jnp.float32),
            pltpu.VMEM((rows, WIDE), jnp.float32),
            pltpu.SemaphoreType.DMA((hidden_slots, 4)),
            pltpu.SemaphoreType.DMA((model_width // math.gcd(model_width, MODEL_EACH), 3)),
        ],
        compiler_params=pltpu.CompilerParams(vmem_limit_bytes=56 * 10**6),
        name="project",
    )(gate_pre, up_pre, hidden_grad, proj_hidden, tokens_in, out_grad, proj_model)


def gram_kernel(rows_each, count, *refs):
    place, parts, (rows_ref, gram_ref) = refs[0], refs[1 : 1 + count], refs[1 + count :]
    total = parts[0][...]
    for part in parts[1:]:
        total += part[...]
    row = lax.broadcasted_iota(jnp.int32, (WIDE, WIDE), 0)
    lane = lanes_of((WIDE, WIDE))
    low = lanes_of((RANK, WIDE)) < RANK
    gram = jnp.zeros((RANK, WIDE), jnp.float32)
    shift = lax.rem(WIDE - place[0] * rows_each, WIDE)
    for example in range(total.shape[0] // LEN):
        mixed = []
        for at in (0, WIDE):
            sides = total[example * LEN : (example + 1) * LEN, at : at + WIDE]
            crossed = jnp.dot(
                sides.T, sides, precision=highest, preferred_element_type=jnp.float32
            )
            mixed.append(jnp.where((row < RANK) != (lane < RANK), crossed, 0.0))
        up_block, down_block = mixed[0][RANK:], mixed[1][RANK:]
        across = jnp.where(low, up_block, pltpu.roll(down_block, RANK, 1))
        rows_ref[example] = jnp.where(low, pltpu.roll(across, shift, 1), 0.0)
        gram += jnp.dot(
            jnp.concatenate([up_block, down_block], axis=1),
            jnp.concatenate(mixed, axis=0),
            precision=highest,
            preferred_element_type=jnp.float32,
        )
    top, bottom = gram[: RANK // 2], gram[RANK // 2 :]
    gram_ref[...] = jnp.where(
        lanes_of(top.shape) < RANK, pltpu.roll(top, RANK, 1), bottom
    )


def gram_of(place, parts, rows_each):
    examples = parts[0].shape[0] // LEN
    return pl.pallas_call(
        functools.partial(gram_kernel, rows_each, len(parts)),
        out_shape=[
            jax.ShapeDtypeStruct((examples, RANK, WIDE), jnp.float32),
            jax.ShapeDtypeStruct((RANK // 2, WIDE), jnp.float32),
        ],
        in_specs=[pl.BlockSpec(memory_space=pltpu.SMEM)] + [whole_vmem] * len(parts),
        out_specs=[whole_vmem] * 2,
        compiler_params=small,
        name="gram",
    )(place, *parts)


def eliminated(state, spread):
    height = 8
    blocks = len(state)
    state = list(state)
    sub = lax.broadcasted_iota(jnp.int32, state[0].shape, 0)

    def across(block, at):
        return jnp.broadcast_to(block[:, at : at + 1], block.shape)

    def down(which, at):
        return spread[which, pl.ds(at, height, stride=0), :]

    done = []
    for held in range(blocks):
        base = RANK + held * height
        own = state[held]
        first_slot = (held % 2) * (height + 1)
        for k in range(height):
            spread[first_slot + k] = across(own, base + k)
        spread[first_slot + height] = own
        corner = {
            (k, m): down(first_slot + m, k) for k in range(height) for m in range(k, height)
        }
        rows = [down(first_slot + height, k) for k in range(height)]
        nearby = range(held + 1, min(held + 3, blocks))
        moving = [rows] + [
            [across(state[other], base + k) for k in range(height)] for other in nearby
        ]
        block = jnp.zeros_like(own)
        for k in range(0, height, 2):
            first, cross, second = corner[k, k], corner[k, k + 1], corner[k + 1, k + 1]
            inverse = pl.reciprocal(first, approx=True)
            other_inverse = first * pl.reciprocal(first * second - cross * cross, approx=True)
            ratio = cross * inverse
            for several in moving:
                several[k + 1] = several[k + 1] - ratio * several[k]
            later = range(k + 2, height)
            upper = {m: corner[k, m] for m in later}
            lower = {m: corner[k + 1, m] - ratio * corner[k, m] for m in later}
            for m in later:
                for n in range(m, height):
                    corner[m, n] = (
                        corner[m, n]
                        - (upper[m] * upper[n]) * inverse
                        - (lower[m] * lower[n]) * other_inverse
                    )
                for several in moving:
                    several[m] = several[m] - (
                        (upper[m] * inverse) * several[k]
                        + (lower[m] * other_inverse) * several[k + 1]
                    )
            for which, other in enumerate(nearby):
                columns = moving[1 + which]
                state[other] = state[other] - (
                    columns[k] * (inverse * rows[k])
                    + columns[k + 1] * (other_inverse * rows[k + 1])
                )
            for m, pivot in ((k, inverse), (k + 1, other_inverse)):
                block = jnp.where(sub == m, rows[m] * (pivot * lax.rsqrt(pivot)), block)
        done.append(block)
        if held + 3 < blocks:
            far = (held + 3) * height
            update = jnp.dot(
                block.T[RANK + far :, :],
                block,
                precision=highest,
                preferred_element_type=jnp.float32,
            )
            for other in range(held + 3, blocks):
                at = other * height - far
                state[other] = state[other] - update[at : at + height]
    return done


def scaled(joined):
    lane = lanes_of(joined.shape)
    row = lax.broadcasted_iota(jnp.int32, joined.shape, 0)
    diagonal = jnp.where(lane == row + RANK, joined, 0.0)
    down = lax.rsqrt(jnp.sum(diagonal, axis=1, keepdims=True))
    along = lax.rsqrt(jnp.sum(diagonal, axis=0, keepdims=True))
    return joined * down * jnp.where(lane < RANK, 1.0, along)


def whiten_kernel(factor, rows_each, rows_ref, gram_ref, out_ref, spread):
    packed = gram_ref[...]
    gram = jnp.concatenate([pltpu.roll(packed, RANK, 1), packed], axis=0)
    low = lanes_of((RANK, WIDE)) < RANK
    for example in range(rows_ref.shape[0]):
        joined = scaled(jnp.where(low, rows_ref[example], gram))
        done = eliminated([joined[at : at + 8] for at in range(0, RANK, 8)], spread)
        solved = (jnp.concatenate(done, axis=0) * factor).T
        out_ref[example] = solved[:rows_each, :]


def whiten(rows, gram, rows_each, factor):
    return pl.pallas_call(
        functools.partial(whiten_kernel, factor, rows_each),
        out_shape=jax.ShapeDtypeStruct((rows.shape[0], rows_each, RANK), jnp.float32),
        in_specs=[whole_vmem] * 2,
        out_specs=whole_vmem,
        scratch_shapes=[pltpu.VMEM((18, 8, WIDE), jnp.float32)],
        compiler_params=small,
        name="whiten",
    )(rows, gram)


def summed_over_groups(value):
    groups, model_shards = lax.axis_size("dp"), lax.axis_size("mp")
    place = lax.axis_index("mp")

    def over_groups(value):
        for level in range(groups.bit_length() - 1):
            pairs = [(source, source ^ 2**level) for source in range(groups)]
            value = value + lax.ppermute(value, "dp", pairs)
        return value

    value = lax.cond(place == model_shards - 1, over_groups, lambda value: value, value)
    result = value
    for away in range(1, model_shards):
        pairs = [(source, (source + away) % model_shards) for source in range(model_shards)]
        received = lax.ppermute(value, "mp", pairs)
        result = jnp.where(place == away - 1, received, result)
    return result


def shards(tokens_in, gate_pre, up_pre, hidden_grad, out_grad, proj_model, proj_hidden):
    model_shards = lax.axis_size("mp")
    rows_each = WIDE // model_shards
    local_examples = tokens_in.shape[0] // LEN
    place = lax.axis_index("mp").astype(jnp.int32).reshape(1)
    part = project(
        gate_pre, up_pre, hidden_grad, proj_hidden, tokens_in, out_grad, proj_model
    )
    parts = [part]
    for away in range(1, model_shards):
        pairs = [(source, (source + away) % model_shards) for source in range(model_shards)]
        parts.append(lax.ppermute(part, "mp", pairs))
    rows, gram = gram_of(place, parts, rows_each)
    gram = summed_over_groups(gram)
    factor = math.sqrt(local_examples * lax.axis_size("dp") * 2 * RANK)
    return whiten(rows, gram, rows_each, factor)


def solution(mesh):
    in_specs = (
        P("dp", "mp"),
        P("dp", "mp"),
        P("dp", "mp"),
        P("dp", "mp"),
        P("dp", "mp"),
        P("mp", None),
        P("mp", None),
    )
    out_specs = P("dp", "mp", None)
    return jax.shard_map(shards, mesh=mesh, in_specs=in_specs, out_specs=out_specs, check_vma=False)
```

```python
import functools
import math

import jax
import jax.numpy as jnp
from jax import lax
from jax.experimental import pallas as pl
from jax.experimental.pallas import tpu as pltpu
from jax.sharding import PartitionSpec as P

RANK = 64
LEN = 128
WIDE = 2 * RANK
EACH = 2048
HEAD = 512
MODEL_EACH = 1024
STEP = 256
AHEAD = 6

highest = lax.Precision.HIGHEST
whole_vmem = pl.BlockSpec(memory_space=pltpu.VMEM)
left_in_hbm = pl.BlockSpec(memory_space=pl.ANY)
small = pltpu.CompilerParams(vmem_limit_bytes=8 * 2**20)


def cuts_of(width):
    full = max((width - 1) // EACH, 0)
    head = width - full * EACH
    ends = [0, min(HEAD, head)]
    while ends[-1] < head:
        ends.append(min(ends[-1] + EACH // 2, head))
    return [(begin, end - begin) for begin, end in zip(ends, ends[1:])], full


def lanes_of(shape):
    return lax.broadcasted_iota(jnp.int32, shape, len(shape) - 1)


def paired(left, right, weights):
    low = lanes_of(weights.shape) < RANK
    none = jnp.zeros_like(weights)
    return jnp.dot(
        jnp.concatenate([left, right], axis=1),
        jnp.concatenate([jnp.where(low, weights, none), jnp.where(low, none, weights)], axis=0),
        preferred_element_type=jnp.float32,
    )


def project_kernel(gate, up, grad, proj_hidden, tokens, outer, proj_model, out, *rest):
    gate_v, up_v, grad_v, hidden_w, tokens_v, outer_v, model_w = rest[:7]
    hidden_sum, model_sum, sems, model_sems = rest[7:]
    rows = gate.shape[0]
    model_each = math.gcd(tokens.shape[1], MODEL_EACH)
    model_count = tokens.shape[1] // model_each
    head, full = cuts_of(gate.shape[1])
    head_width = gate.shape[1] - full * EACH

    def hidden_copies(slot, begin, size):
        cut = pl.ds(pl.multiple_of(begin, 128), size)
        pairs = [
            (gate.at[:, cut], gate_v.at[:, cut]),
            (grad.at[:, cut], grad_v.at[:, cut]),
            (up.at[:, cut], up_v.at[:, cut]),
            (proj_hidden.at[cut, :], hidden_w.at[cut, :]),
        ]
        return [
            pltpu.make_async_copy(source, target, sems.at[slot, which])
            for which, (source, target) in enumerate(pairs)
        ]

    def full_copies(piece):
        return hidden_copies(len(head) + piece, head_width + piece * EACH, EACH)

    def model_copies(piece):
        cut = pl.ds(pl.multiple_of(piece * model_each, model_each), model_each)
        pairs = [
            (tokens.at[:, cut], tokens_v.at[:, cut]),
            (outer.at[:, cut], outer_v.at[:, cut]),
            (proj_model.at[cut, :], model_w.at[cut, :]),
        ]
        return [
            pltpu.make_async_copy(source, target, model_sems.at[piece, which])
            for which, (source, target) in enumerate(pairs)
        ]

    def start(copies):
        for copy in copies:
            copy.start()

    def arrive(copies):
        for copy in copies:
            copy.wait()

    def start_models():
        for other in range(model_count):
            start(model_copies(other))

    def advance(begin, size):
        total = None
        for first in range(0, size, STEP):
            step = min(STEP, size - first)
            cut = pl.ds(pl.multiple_of(begin + first, 128), step)
            half = (gate_v[:, cut] * 0.5).astype(jnp.float32)
            act = half + half * jnp.tanh(half)
            up_grad = (grad_v[:, cut].astype(jnp.float32) * act).astype(jnp.bfloat16)
            hidden = (act * up_v[:, cut].astype(jnp.float32)).astype(jnp.bfloat16)
            part = paired(up_grad, hidden, hidden_w[cut, :])
            total = part if total is None else total + part
        hidden_sum[...] += total

    ahead = min(AHEAD, full)
    for slot, (begin, size) in enumerate(head):
        start(hidden_copies(slot, begin, size))
    for piece in range(ahead):
        start(full_copies(piece))
    if not full:
        start_models()
    hidden_sum[...] = jnp.zeros_like(hidden_sum)
    model_sum[...] = jnp.zeros_like(model_sum)
    for slot, (begin, size) in enumerate(head):
        arrive(hidden_copies(slot, begin, size))
        advance(begin, size)

    @pl.loop(0, full)
    def _(piece):
        arrive(full_copies(piece))

        @pl.when(piece + ahead < full)
        def _():
            start(full_copies(piece + ahead))

        @pl.when(piece + ahead == full)
        def _():
            start_models()

        advance(head_width + piece * EACH, EACH)

    @pl.loop(0, model_count)
    def _(piece):
        arrive(model_copies(piece))
        cut = pl.ds(pl.multiple_of(piece * model_each, model_each), model_each)
        model_sum[...] += paired(tokens_v[:, cut], outer_v[:, cut], model_w[cut, :])

    low = lanes_of((rows, WIDE)) < RANK
    turned = pltpu.roll(hidden_sum[...], RANK, 1)
    out[:, :WIDE] = jnp.where(low, model_sum[...], turned)
    out[:, WIDE:] = jnp.where(low, turned, model_sum[...])


def project(gate_pre, up_pre, hidden_grad, proj_hidden, tokens_in, out_grad, proj_model):
    rows, hidden_width = gate_pre.shape
    model_width = tokens_in.shape[1]
    head, full = cuts_of(hidden_width)
    hidden_slots = len(head) + full
    held = jnp.bfloat16
    return pl.pallas_call(
        project_kernel,
        out_shape=jax.ShapeDtypeStruct((rows, 2 * WIDE), jnp.float32),
        in_specs=[left_in_hbm] * 7,
        out_specs=whole_vmem,
        scratch_shapes=[
            pltpu.VMEM((rows, hidden_width), held),
            pltpu.VMEM((rows, hidden_width), held),
            pltpu.VMEM((rows, hidden_width), held),
            pltpu.VMEM((hidden_width, WIDE), held),
            pltpu.VMEM((rows, model_width), held),
            pltpu.VMEM((rows, model_width), held),
            pltpu.VMEM((model_width, WIDE), held),
            pltpu.VMEM((rows, WIDE), jnp.float32),
            pltpu.VMEM((rows, WIDE), jnp.float32),
            pltpu.SemaphoreType.DMA((hidden_slots, 4)),
            pltpu.SemaphoreType.DMA((model_width // math.gcd(model_width, MODEL_EACH), 3)),
        ],
        compiler_params=pltpu.CompilerParams(vmem_limit_bytes=56 * 10**6),
        name="project",
    )(gate_pre, up_pre, hidden_grad, proj_hidden, tokens_in, out_grad, proj_model)


def gram_kernel(rows_each, count, *refs):
    place, parts, (rows_ref, gram_ref) = refs[0], refs[1 : 1 + count], refs[1 + count :]
    total = parts[0][...]
    for part in parts[1:]:
        total += part[...]
    row = lax.broadcasted_iota(jnp.int32, (WIDE, WIDE), 0)
    lane = lanes_of((WIDE, WIDE))
    low = lanes_of((RANK, WIDE)) < RANK
    gram = jnp.zeros((RANK, WIDE), jnp.float32)
    shift = lax.rem(WIDE - place[0] * rows_each, WIDE)
    for example in range(total.shape[0] // LEN):
        mixed = []
        for at in (0, WIDE):
            sides = total[example * LEN : (example + 1) * LEN, at : at + WIDE]
            crossed = jnp.dot(
                sides.T, sides, precision=highest, preferred_element_type=jnp.float32
            )
            mixed.append(jnp.where((row < RANK) != (lane < RANK), crossed, 0.0))
        up_block, down_block = mixed[0][RANK:], mixed[1][RANK:]
        across = jnp.where(low, up_block, pltpu.roll(down_block, RANK, 1))
        rows_ref[example] = jnp.where(low, pltpu.roll(across, shift, 1), 0.0)
        gram += jnp.dot(
            jnp.concatenate([up_block, down_block], axis=1),
            jnp.concatenate(mixed, axis=0),
            precision=highest,
            preferred_element_type=jnp.float32,
        )
    top, bottom = gram[: RANK // 2], gram[RANK // 2 :]
    gram_ref[...] = jnp.where(
        lanes_of(top.shape) < RANK, pltpu.roll(top, RANK, 1), bottom
    )


def gram_of(place, parts, rows_each):
    examples = parts[0].shape[0] // LEN
    return pl.pallas_call(
        functools.partial(gram_kernel, rows_each, len(parts)),
        out_shape=[
            jax.ShapeDtypeStruct((examples, RANK, WIDE), jnp.float32),
            jax.ShapeDtypeStruct((RANK // 2, WIDE), jnp.float32),
        ],
        in_specs=[pl.BlockSpec(memory_space=pltpu.SMEM)] + [whole_vmem] * len(parts),
        out_specs=[whole_vmem] * 2,
        compiler_params=small,
        name="gram",
    )(place, *parts)


def eliminated(state, spread):
    height = 8
    blocks = len(state)
    state = list(state)
    sub = lax.broadcasted_iota(jnp.int32, state[0].shape, 0)

    def across(block, at):
        return jnp.broadcast_to(block[:, at : at + 1], block.shape)

    def down(which, at):
        return spread[which, pl.ds(at, height, stride=0), :]

    done = []
    for held in range(blocks):
        base = RANK + held * height
        own = state[held]
        first_slot = (held % 2) * (height + 1)
        for k in range(height):
            spread[first_slot + k] = across(own, base + k)
        spread[first_slot + height] = own
        corner = {
            (k, m): down(first_slot + m, k) for k in range(height) for m in range(k, height)
        }
        rows = [down(first_slot + height, k) for k in range(height)]
        nearby = range(held + 1, min(held + 2, blocks))
        moving = [rows] + [
            [across(state[other], base + k) for k in range(height)] for other in nearby
        ]
        block = packed = divided = jnp.zeros_like(own)
        for k in range(0, height, 2):
            first, cross, second = corner[k, k], corner[k, k + 1], corner[k + 1, k + 1]
            inverse = pl.reciprocal(first, approx=True)
            other_inverse = first * pl.reciprocal(first * second - cross * cross, approx=True)
            ratio = cross * inverse
            for several in moving:
                several[k + 1] = several[k + 1] - ratio * several[k]
            later = range(k + 2, height)
            upper = {m: corner[k, m] for m in later}
            lower = {m: corner[k + 1, m] - ratio * corner[k, m] for m in later}
            for m in later:
                for n in range(m, height):
                    corner[m, n] = (
                        corner[m, n]
                        - (upper[m] * upper[n]) * inverse
                        - (lower[m] * lower[n]) * other_inverse
                    )
                for several in moving:
                    several[m] = several[m] - (
                        (upper[m] * inverse) * several[k]
                        + (lower[m] * other_inverse) * several[k + 1]
                    )
            for which, other in enumerate(nearby):
                columns = moving[1 + which]
                state[other] = state[other] - (
                    columns[k] * (inverse * rows[k])
                    + columns[k + 1] * (other_inverse * rows[k + 1])
                )
            for m, pivot in ((k, inverse), (k + 1, other_inverse)):
                block = jnp.where(sub == m, rows[m] * (pivot * lax.rsqrt(pivot)), block)
                packed = jnp.where(sub == m, rows[m], packed)
                divided = jnp.where(sub == m, rows[m] * pivot, divided)
        done.append(block)
        if held + 2 < blocks:
            far = (held + 2) * height
            update = jnp.dot(
                packed.T[RANK + far :, :],
                divided,
                precision=highest,
                preferred_element_type=jnp.float32,
            )
            for other in range(held + 2, blocks):
                at = other * height - far
                state[other] = state[other] - update[at : at + height]
    return done


def scaled(joined):
    lane = lanes_of(joined.shape)
    row = lax.broadcasted_iota(jnp.int32, joined.shape, 0)
    diagonal = jnp.where(lane == row + RANK, joined, 0.0)
    down = lax.rsqrt(jnp.sum(diagonal, axis=1, keepdims=True))
    along = lax.rsqrt(jnp.sum(diagonal, axis=0, keepdims=True))
    return joined * down * jnp.where(lane < RANK, 1.0, along)


def whiten_kernel(factor, rows_each, rows_ref, gram_ref, out_ref, spread):
    packed = gram_ref[...]
    gram = jnp.concatenate([pltpu.roll(packed, RANK, 1), packed], axis=0)
    low = lanes_of((RANK, WIDE)) < RANK
    for example in range(rows_ref.shape[0]):
        joined = scaled(jnp.where(low, rows_ref[example], gram))
        done = eliminated([joined[at : at + 8] for at in range(0, RANK, 8)], spread)
        solved = (jnp.concatenate(done, axis=0) * factor).T
        out_ref[example] = solved[:rows_each, :]


def whiten(rows, gram, rows_each, factor):
    return pl.pallas_call(
        functools.partial(whiten_kernel, factor, rows_each),
        out_shape=jax.ShapeDtypeStruct((rows.shape[0], rows_each, RANK), jnp.float32),
        in_specs=[whole_vmem] * 2,
        out_specs=whole_vmem,
        scratch_shapes=[pltpu.VMEM((18, 8, WIDE), jnp.float32)],
        compiler_params=small,
        name="whiten",
    )(rows, gram)


def summed_over_groups(value):
    groups, model_shards = lax.axis_size("dp"), lax.axis_size("mp")
    place = lax.axis_index("mp")

    def over_groups(value):
        for level in range(groups.bit_length() - 1):
            pairs = [(source, source ^ 2**level) for source in range(groups)]
            value = value + lax.ppermute(value, "dp", pairs)
        return value

    value = lax.cond(place == model_shards - 1, over_groups, lambda value: value, value)
    result = value
    for away in range(1, model_shards):
        pairs = [(source, (source + away) % model_shards) for source in range(model_shards)]
        received = lax.ppermute(value, "mp", pairs)
        result = jnp.where(place == away - 1, received, result)
    return result


def shards(tokens_in, gate_pre, up_pre, hidden_grad, out_grad, proj_model, proj_hidden):
    model_shards = lax.axis_size("mp")
    rows_each = WIDE // model_shards
    local_examples = tokens_in.shape[0] // LEN
    place = lax.axis_index("mp").astype(jnp.int32).reshape(1)
    part = project(
        gate_pre, up_pre, hidden_grad, proj_hidden, tokens_in, out_grad, proj_model
    )
    parts = [part]
    for away in range(1, model_shards):
        pairs = [(source, (source + away) % model_shards) for source in range(model_shards)]
        parts.append(lax.ppermute(part, "mp", pairs))
    rows, gram = gram_of(place, parts, rows_each)
    gram = summed_over_groups(gram)
    factor = math.sqrt(local_examples * lax.axis_size("dp") * 2 * RANK)
    return whiten(rows, gram, rows_each, factor)


def solution(mesh):
    in_specs = (
        P("dp", "mp"),
        P("dp", "mp"),
        P("dp", "mp"),
        P("dp", "mp"),
        P("dp", "mp"),
        P("mp", None),
        P("mp", None),
    )
    out_specs = P("dp", "mp", None)
    return jax.shard_map(shards, mesh=mesh, in_specs=in_specs, out_specs=out_specs, check_vma=False)
```

```python
import functools
import math

import jax
import jax.numpy as jnp
from jax import lax
from jax.experimental import pallas as pl
from jax.experimental.pallas import tpu as pltpu
from jax.sharding import PartitionSpec as P

RANK = 64
LEN = 128
WIDE = 2 * RANK
EACH = 2048
HEAD = 512
MODEL_EACH = 1024
STEP = 256
AHEAD = 6

highest = lax.Precision.HIGHEST
whole_vmem = pl.BlockSpec(memory_space=pltpu.VMEM)
left_in_hbm = pl.BlockSpec(memory_space=pl.ANY)
small = pltpu.CompilerParams(vmem_limit_bytes=8 * 2**20)


def cuts_of(width):
    full = max((width - 1) // EACH, 0)
    head = width - full * EACH
    ends = [0, min(HEAD, head)]
    while ends[-1] < head:
        ends.append(min(ends[-1] + EACH // 2, head))
    return [(begin, end - begin) for begin, end in zip(ends, ends[1:])], full


def lanes_of(shape):
    return lax.broadcasted_iota(jnp.int32, shape, len(shape) - 1)


def paired(left, right, weights):
    low = lanes_of(weights.shape) < RANK
    none = jnp.zeros_like(weights)
    return jnp.dot(
        jnp.concatenate([left, right], axis=1),
        jnp.concatenate([jnp.where(low, weights, none), jnp.where(low, none, weights)], axis=0),
        preferred_element_type=jnp.float32,
    )


def project_kernel(gate, up, grad, proj_hidden, tokens, outer, proj_model, out, *rest):
    gate_v, up_v, grad_v, hidden_w, tokens_v, outer_v, model_w = rest[:7]
    hidden_sum, model_sum, sems, model_sems = rest[7:]
    rows = gate.shape[0]
    model_each = math.gcd(tokens.shape[1], MODEL_EACH)
    model_count = tokens.shape[1] // model_each
    head, full = cuts_of(gate.shape[1])
    head_width = gate.shape[1] - full * EACH

    def hidden_copies(slot, begin, size):
        cut = pl.ds(pl.multiple_of(begin, 128), size)
        pairs = [
            (gate.at[:, cut], gate_v.at[:, cut]),
            (grad.at[:, cut], grad_v.at[:, cut]),
            (up.at[:, cut], up_v.at[:, cut]),
            (proj_hidden.at[cut, :], hidden_w.at[cut, :]),
        ]
        return [
            pltpu.make_async_copy(source, target, sems.at[slot, which])
            for which, (source, target) in enumerate(pairs)
        ]

    def full_copies(piece):
        return hidden_copies(len(head) + piece, head_width + piece * EACH, EACH)

    def model_copies(piece):
        cut = pl.ds(pl.multiple_of(piece * model_each, model_each), model_each)
        pairs = [
            (tokens.at[:, cut], tokens_v.at[:, cut]),
            (outer.at[:, cut], outer_v.at[:, cut]),
            (proj_model.at[cut, :], model_w.at[cut, :]),
        ]
        return [
            pltpu.make_async_copy(source, target, model_sems.at[piece, which])
            for which, (source, target) in enumerate(pairs)
        ]

    def start(copies):
        for copy in copies:
            copy.start()

    def arrive(copies):
        for copy in copies:
            copy.wait()

    def start_models():
        for other in range(model_count):
            start(model_copies(other))

    def advance(begin, size):
        total = None
        for first in range(0, size, STEP):
            step = min(STEP, size - first)
            cut = pl.ds(pl.multiple_of(begin + first, 128), step)
            half = (gate_v[:, cut] * 0.5).astype(jnp.float32)
            act = half + half * jnp.tanh(half)
            up_grad = (grad_v[:, cut].astype(jnp.float32) * act).astype(jnp.bfloat16)
            hidden = (act * up_v[:, cut].astype(jnp.float32)).astype(jnp.bfloat16)
            part = paired(up_grad, hidden, hidden_w[cut, :])
            total = part if total is None else total + part
        hidden_sum[...] += total

    ahead = min(AHEAD, full)
    for slot, (begin, size) in enumerate(head):
        start(hidden_copies(slot, begin, size))
    for piece in range(ahead):
        start(full_copies(piece))
    if not full:
        start_models()
    hidden_sum[...] = jnp.zeros_like(hidden_sum)
    model_sum[...] = jnp.zeros_like(model_sum)
    for slot, (begin, size) in enumerate(head):
        arrive(hidden_copies(slot, begin, size))
        advance(begin, size)

    @pl.loop(0, full)
    def _(piece):
        arrive(full_copies(piece))

        @pl.when(piece + ahead < full)
        def _():
            start(full_copies(piece + ahead))

        @pl.when(piece + ahead == full)
        def _():
            start_models()

        advance(head_width + piece * EACH, EACH)

    @pl.loop(0, model_count)
    def _(piece):
        arrive(model_copies(piece))
        cut = pl.ds(pl.multiple_of(piece * model_each, model_each), model_each)
        model_sum[...] += paired(tokens_v[:, cut], outer_v[:, cut], model_w[cut, :])

    low = lanes_of((rows, WIDE)) < RANK
    turned = pltpu.roll(hidden_sum[...], RANK, 1)
    out[:, :WIDE] = jnp.where(low, model_sum[...], turned)
    out[:, WIDE:] = jnp.where(low, turned, model_sum[...])


def project(gate_pre, up_pre, hidden_grad, proj_hidden, tokens_in, out_grad, proj_model):
    rows, hidden_width = gate_pre.shape
    model_width = tokens_in.shape[1]
    head, full = cuts_of(hidden_width)
    hidden_slots = len(head) + full
    held = jnp.bfloat16
    return pl.pallas_call(
        project_kernel,
        out_shape=jax.ShapeDtypeStruct((rows, 2 * WIDE), jnp.float32),
        in_specs=[left_in_hbm] * 7,
        out_specs=whole_vmem,
        scratch_shapes=[
            pltpu.VMEM((rows, hidden_width), held),
            pltpu.VMEM((rows, hidden_width), held),
            pltpu.VMEM((rows, hidden_width), held),
            pltpu.VMEM((hidden_width, WIDE), held),
            pltpu.VMEM((rows, model_width), held),
            pltpu.VMEM((rows, model_width), held),
            pltpu.VMEM((model_width, WIDE), held),
            pltpu.VMEM((rows, WIDE), jnp.float32),
            pltpu.VMEM((rows, WIDE), jnp.float32),
            pltpu.SemaphoreType.DMA((hidden_slots, 4)),
            pltpu.SemaphoreType.DMA((model_width // math.gcd(model_width, MODEL_EACH), 3)),
        ],
        compiler_params=pltpu.CompilerParams(vmem_limit_bytes=56 * 10**6),
        name="project",
    )(gate_pre, up_pre, hidden_grad, proj_hidden, tokens_in, out_grad, proj_model)


def gram_kernel(rows_each, count, *refs):
    place, parts, (rows_ref, gram_ref) = refs[0], refs[1 : 1 + count], refs[1 + count :]
    total = parts[0][...]
    for part in parts[1:]:
        total += part[...]
    row = lax.broadcasted_iota(jnp.int32, (WIDE, WIDE), 0)
    lane = lanes_of((WIDE, WIDE))
    low = lanes_of((RANK, WIDE)) < RANK
    gram = jnp.zeros((RANK, WIDE), jnp.float32)
    shift = lax.rem(WIDE - place[0] * rows_each, WIDE)
    for example in range(total.shape[0] // LEN):
        mixed = []
        for at in (0, WIDE):
            sides = total[example * LEN : (example + 1) * LEN, at : at + WIDE]
            crossed = jnp.dot(
                sides.T, sides, precision=highest, preferred_element_type=jnp.float32
            )
            mixed.append(jnp.where((row < RANK) != (lane < RANK), crossed, 0.0))
        up_block, down_block = mixed[0][RANK:], mixed[1][RANK:]
        across = jnp.where(low, up_block, pltpu.roll(down_block, RANK, 1))
        rows_ref[example] = jnp.where(low, pltpu.roll(across, shift, 1), 0.0)
        gram += jnp.dot(
            jnp.concatenate([up_block, down_block], axis=1),
            jnp.concatenate(mixed, axis=0),
            precision=highest,
            preferred_element_type=jnp.float32,
        )
    top, bottom = gram[: RANK // 2], gram[RANK // 2 :]
    gram_ref[...] = jnp.where(
        lanes_of(top.shape) < RANK, pltpu.roll(top, RANK, 1), bottom
    )


def gram_of(place, parts, rows_each):
    examples = parts[0].shape[0] // LEN
    return pl.pallas_call(
        functools.partial(gram_kernel, rows_each, len(parts)),
        out_shape=[
            jax.ShapeDtypeStruct((examples, RANK, WIDE), jnp.float32),
            jax.ShapeDtypeStruct((RANK // 2, WIDE), jnp.float32),
        ],
        in_specs=[pl.BlockSpec(memory_space=pltpu.SMEM)] + [whole_vmem] * len(parts),
        out_specs=[whole_vmem] * 2,
        compiler_params=small,
        name="gram",
    )(place, *parts)


def eliminated(state, spread):
    height = 8
    blocks = len(state)
    state = list(state)
    sub = lax.broadcasted_iota(jnp.int32, state[0].shape, 0)

    def across(block, at):
        return jnp.broadcast_to(block[:, at : at + 1], block.shape)

    def down(which, at):
        return spread[which, pl.ds(at, height, stride=0), :]

    done = []
    for held in range(blocks):
        base = RANK + held * height
        own = state[held]
        first_slot = (held % 2) * (height + 1)
        for k in range(height):
            spread[first_slot + k] = across(own, base + k)
        spread[first_slot + height] = own
        corner = {
            (k, m): down(first_slot + m, k) for k in range(height) for m in range(k, height)
        }
        rows = [down(first_slot + height, k) for k in range(height)]
        nearby = range(held + 1, min(held + 4, blocks))
        moving = [rows] + [
            [across(state[other], base + k) for k in range(height)] for other in nearby
        ]
        block = packed = divided = jnp.zeros_like(own)
        for k in range(0, height, 2):
            first, cross, second = corner[k, k], corner[k, k + 1], corner[k + 1, k + 1]
            inverse = pl.reciprocal(first, approx=True)
            other_inverse = first * pl.reciprocal(first * second - cross * cross, approx=True)
            ratio = cross * inverse
            for several in moving:
                several[k + 1] = several[k + 1] - ratio * several[k]
            later = range(k + 2, height)
            upper = {m: corner[k, m] for m in later}
            lower = {m: corner[k + 1, m] - ratio * corner[k, m] for m in later}
            for m in later:
                for n in range(m, height):
                    corner[m, n] = (
                        corner[m, n]
                        - (upper[m] * upper[n]) * inverse
                        - (lower[m] * lower[n]) * other_inverse
                    )
                for several in moving:
                    several[m] = several[m] - (
                        (upper[m] * inverse) * several[k]
                        + (lower[m] * other_inverse) * several[k + 1]
                    )
            for which, other in enumerate(nearby):
                columns = moving[1 + which]
                state[other] = state[other] - (
                    columns[k] * (inverse * rows[k])
                    + columns[k + 1] * (other_inverse * rows[k + 1])
                )
            for m, pivot in ((k, inverse), (k + 1, other_inverse)):
                block = jnp.where(sub == m, rows[m] * (pivot * lax.rsqrt(pivot)), block)
                packed = jnp.where(sub == m, rows[m], packed)
                divided = jnp.where(sub == m, rows[m] * pivot, divided)
        done.append(block)
        if held + 4 < blocks:
            far = (held + 4) * height
            update = jnp.dot(
                packed.T[RANK + far :, :],
                divided,
                precision=highest,
                preferred_element_type=jnp.float32,
            )
            for other in range(held + 4, blocks):
                at = other * height - far
                state[other] = state[other] - update[at : at + height]
    return done


def scaled(joined):
    lane = lanes_of(joined.shape)
    row = lax.broadcasted_iota(jnp.int32, joined.shape, 0)
    diagonal = jnp.where(lane == row + RANK, joined, 0.0)
    down = lax.rsqrt(jnp.sum(diagonal, axis=1, keepdims=True))
    along = lax.rsqrt(jnp.sum(diagonal, axis=0, keepdims=True))
    return joined * down * jnp.where(lane < RANK, 1.0, along)


def whiten_kernel(factor, rows_each, rows_ref, gram_ref, out_ref, spread):
    packed = gram_ref[...]
    gram = jnp.concatenate([pltpu.roll(packed, RANK, 1), packed], axis=0)
    low = lanes_of((RANK, WIDE)) < RANK
    for example in range(rows_ref.shape[0]):
        joined = scaled(jnp.where(low, rows_ref[example], gram))
        done = eliminated([joined[at : at + 8] for at in range(0, RANK, 8)], spread)
        solved = (jnp.concatenate(done, axis=0) * factor).T
        out_ref[example] = solved[:rows_each, :]


def whiten(rows, gram, rows_each, factor):
    return pl.pallas_call(
        functools.partial(whiten_kernel, factor, rows_each),
        out_shape=jax.ShapeDtypeStruct((rows.shape[0], rows_each, RANK), jnp.float32),
        in_specs=[whole_vmem] * 2,
        out_specs=whole_vmem,
        scratch_shapes=[pltpu.VMEM((18, 8, WIDE), jnp.float32)],
        compiler_params=small,
        name="whiten",
    )(rows, gram)


def summed_over_groups(value):
    groups, model_shards = lax.axis_size("dp"), lax.axis_size("mp")
    place = lax.axis_index("mp")

    def over_groups(value):
        for level in range(groups.bit_length() - 1):
            pairs = [(source, source ^ 2**level) for source in range(groups)]
            value = value + lax.ppermute(value, "dp", pairs)
        return value

    value = lax.cond(place == model_shards - 1, over_groups, lambda value: value, value)
    result = value
    for away in range(1, model_shards):
        pairs = [(source, (source + away) % model_shards) for source in range(model_shards)]
        received = lax.ppermute(value, "mp", pairs)
        result = jnp.where(place == away - 1, received, result)
    return result


def shards(tokens_in, gate_pre, up_pre, hidden_grad, out_grad, proj_model, proj_hidden):
    model_shards = lax.axis_size("mp")
    rows_each = WIDE // model_shards
    local_examples = tokens_in.shape[0] // LEN
    place = lax.axis_index("mp").astype(jnp.int32).reshape(1)
    part = project(
        gate_pre, up_pre, hidden_grad, proj_hidden, tokens_in, out_grad, proj_model
    )
    parts = [part]
    for away in range(1, model_shards):
        pairs = [(source, (source + away) % model_shards) for source in range(model_shards)]
        parts.append(lax.ppermute(part, "mp", pairs))
    rows, gram = gram_of(place, parts, rows_each)
    gram = summed_over_groups(gram)
    factor = math.sqrt(local_examples * lax.axis_size("dp") * 2 * RANK)
    return whiten(rows, gram, rows_each, factor)


def solution(mesh):
    in_specs = (
        P("dp", "mp"),
        P("dp", "mp"),
        P("dp", "mp"),
        P("dp", "mp"),
        P("dp", "mp"),
        P("mp", None),
        P("mp", None),
    )
    out_specs = P("dp", "mp", None)
    return jax.shard_map(shards, mesh=mesh, in_specs=in_specs, out_specs=out_specs, check_vma=False)
```

```python
import functools
import math

import jax
import jax.numpy as jnp
from jax import lax
from jax.experimental import pallas as pl
from jax.experimental.pallas import tpu as pltpu
from jax.sharding import PartitionSpec as P

RANK = 64
LEN = 128
WIDE = 2 * RANK
EACH = 2048
HEAD = 512
MODEL_EACH = 1024
STEP = 256
AHEAD = 6

highest = lax.Precision.HIGHEST
whole_vmem = pl.BlockSpec(memory_space=pltpu.VMEM)
left_in_hbm = pl.BlockSpec(memory_space=pl.ANY)
small = pltpu.CompilerParams(vmem_limit_bytes=8 * 2**20)


def cuts_of(width):
    full = max((width - 1) // EACH, 0)
    head = width - full * EACH
    ends = [0, min(HEAD, head)]
    while ends[-1] < head:
        ends.append(min(ends[-1] + EACH // 2, head))
    return [(begin, end - begin) for begin, end in zip(ends, ends[1:])], full


def lanes_of(shape):
    return lax.broadcasted_iota(jnp.int32, shape, len(shape) - 1)


def paired(left, right, weights):
    low = lanes_of(weights.shape) < RANK
    none = jnp.zeros_like(weights)
    return jnp.dot(
        jnp.concatenate([left, right], axis=1),
        jnp.concatenate([jnp.where(low, weights, none), jnp.where(low, none, weights)], axis=0),
        preferred_element_type=jnp.float32,
    )


def project_kernel(gate, up, grad, proj_hidden, tokens, outer, proj_model, out, *rest):
    gate_v, up_v, grad_v, hidden_w, tokens_v, outer_v, model_w = rest[:7]
    hidden_sum, model_sum, sems, model_sems = rest[7:]
    rows = gate.shape[0]
    model_each = math.gcd(tokens.shape[1], MODEL_EACH)
    model_count = tokens.shape[1] // model_each
    head, full = cuts_of(gate.shape[1])
    head_width = gate.shape[1] - full * EACH

    def hidden_copies(slot, begin, size):
        cut = pl.ds(pl.multiple_of(begin, 128), size)
        pairs = [
            (gate.at[:, cut], gate_v.at[:, cut]),
            (grad.at[:, cut], grad_v.at[:, cut]),
            (up.at[:, cut], up_v.at[:, cut]),
            (proj_hidden.at[cut, :], hidden_w.at[cut, :]),
        ]
        return [
            pltpu.make_async_copy(source, target, sems.at[slot, which])
            for which, (source, target) in enumerate(pairs)
        ]

    def full_copies(piece):
        return hidden_copies(len(head) + piece, head_width + piece * EACH, EACH)

    def model_copies(piece):
        cut = pl.ds(pl.multiple_of(piece * model_each, model_each), model_each)
        pairs = [
            (tokens.at[:, cut], tokens_v.at[:, cut]),
            (outer.at[:, cut], outer_v.at[:, cut]),
            (proj_model.at[cut, :], model_w.at[cut, :]),
        ]
        return [
            pltpu.make_async_copy(source, target, model_sems.at[piece, which])
            for which, (source, target) in enumerate(pairs)
        ]

    def start(copies):
        for copy in copies:
            copy.start()

    def arrive(copies):
        for copy in copies:
            copy.wait()

    def start_models():
        for other in range(model_count):
            start(model_copies(other))

    def advance(begin, size):
        total = None
        for first in range(0, size, STEP):
            step = min(STEP, size - first)
            cut = pl.ds(pl.multiple_of(begin + first, 128), step)
            half = (gate_v[:, cut] * 0.5).astype(jnp.float32)
            act = half + half * jnp.tanh(half)
            up_grad = (grad_v[:, cut].astype(jnp.float32) * act).astype(jnp.bfloat16)
            hidden = (act * up_v[:, cut].astype(jnp.float32)).astype(jnp.bfloat16)
            part = paired(up_grad, hidden, hidden_w[cut, :])
            total = part if total is None else total + part
        hidden_sum[...] += total

    ahead = min(AHEAD, full)
    for slot, (begin, size) in enumerate(head):
        start(hidden_copies(slot, begin, size))
    for piece in range(ahead):
        start(full_copies(piece))
    if not full:
        start_models()
    hidden_sum[...] = jnp.zeros_like(hidden_sum)
    model_sum[...] = jnp.zeros_like(model_sum)
    for slot, (begin, size) in enumerate(head):
        arrive(hidden_copies(slot, begin, size))
        advance(begin, size)

    @pl.loop(0, full)
    def _(piece):
        arrive(full_copies(piece))

        @pl.when(piece + ahead < full)
        def _():
            start(full_copies(piece + ahead))

        @pl.when(piece + ahead == full)
        def _():
            start_models()

        advance(head_width + piece * EACH, EACH)

    @pl.loop(0, model_count)
    def _(piece):
        arrive(model_copies(piece))
        cut = pl.ds(pl.multiple_of(piece * model_each, model_each), model_each)
        model_sum[...] += paired(tokens_v[:, cut], outer_v[:, cut], model_w[cut, :])

    low = lanes_of((rows, WIDE)) < RANK
    turned = pltpu.roll(hidden_sum[...], RANK, 1)
    out[:, :WIDE] = jnp.where(low, model_sum[...], turned)
    out[:, WIDE:] = jnp.where(low, turned, model_sum[...])


def project(gate_pre, up_pre, hidden_grad, proj_hidden, tokens_in, out_grad, proj_model):
    rows, hidden_width = gate_pre.shape
    model_width = tokens_in.shape[1]
    head, full = cuts_of(hidden_width)
    hidden_slots = len(head) + full
    held = jnp.bfloat16
    return pl.pallas_call(
        project_kernel,
        out_shape=jax.ShapeDtypeStruct((rows, 2 * WIDE), jnp.float32),
        in_specs=[left_in_hbm] * 7,
        out_specs=whole_vmem,
        scratch_shapes=[
            pltpu.VMEM((rows, hidden_width), held),
            pltpu.VMEM((rows, hidden_width), held),
            pltpu.VMEM((rows, hidden_width), held),
            pltpu.VMEM((hidden_width, WIDE), held),
            pltpu.VMEM((rows, model_width), held),
            pltpu.VMEM((rows, model_width), held),
            pltpu.VMEM((model_width, WIDE), held),
            pltpu.VMEM((rows, WIDE), jnp.float32),
            pltpu.VMEM((rows, WIDE), jnp.float32),
            pltpu.SemaphoreType.DMA((hidden_slots, 4)),
            pltpu.SemaphoreType.DMA((model_width // math.gcd(model_width, MODEL_EACH), 3)),
        ],
        compiler_params=pltpu.CompilerParams(vmem_limit_bytes=56 * 10**6),
        name="project",
    )(gate_pre, up_pre, hidden_grad, proj_hidden, tokens_in, out_grad, proj_model)


def gram_kernel(rows_each, count, *refs):
    place, parts, (rows_ref, gram_ref) = refs[0], refs[1 : 1 + count], refs[1 + count :]
    total = parts[0][...]
    for part in parts[1:]:
        total += part[...]
    row = lax.broadcasted_iota(jnp.int32, (WIDE, WIDE), 0)
    lane = lanes_of((WIDE, WIDE))
    low = lanes_of((RANK, WIDE)) < RANK
    gram = jnp.zeros((RANK, WIDE), jnp.float32)
    shift = lax.rem(WIDE - place[0] * rows_each, WIDE)
    for example in range(total.shape[0] // LEN):
        mixed = []
        for at in (0, WIDE):
            sides = total[example * LEN : (example + 1) * LEN, at : at + WIDE]
            crossed = jnp.dot(
                sides.T, sides, precision=highest, preferred_element_type=jnp.float32
            )
            mixed.append(jnp.where((row < RANK) != (lane < RANK), crossed, 0.0))
        up_block, down_block = mixed[0][RANK:], mixed[1][RANK:]
        across = jnp.where(low, up_block, pltpu.roll(down_block, RANK, 1))
        rows_ref[example] = jnp.where(low, pltpu.roll(across, shift, 1), 0.0)
        gram += jnp.dot(
            jnp.concatenate([up_block, down_block], axis=1),
            jnp.concatenate(mixed, axis=0),
            precision=highest,
            preferred_element_type=jnp.float32,
        )
    top, bottom = gram[: RANK // 2], gram[RANK // 2 :]
    gram_ref[...] = jnp.where(
        lanes_of(top.shape) < RANK, pltpu.roll(top, RANK, 1), bottom
    )


def gram_of(place, parts, rows_each):
    examples = parts[0].shape[0] // LEN
    return pl.pallas_call(
        functools.partial(gram_kernel, rows_each, len(parts)),
        out_shape=[
            jax.ShapeDtypeStruct((examples, RANK, WIDE), jnp.float32),
            jax.ShapeDtypeStruct((RANK // 2, WIDE), jnp.float32),
        ],
        in_specs=[pl.BlockSpec(memory_space=pltpu.SMEM)] + [whole_vmem] * len(parts),
        out_specs=[whole_vmem] * 2,
        compiler_params=small,
        name="gram",
    )(place, *parts)


def eliminated(state, spread):
    height = 8
    blocks = len(state)
    state = list(state)
    sub = lax.broadcasted_iota(jnp.int32, state[0].shape, 0)

    def across(block, at):
        return jnp.broadcast_to(block[:, at : at + 1], block.shape)

    def down(which, at):
        return spread[which, pl.ds(at, height, stride=0), :]

    done = []
    for held in range(blocks):
        base = RANK + held * height
        own = state[held]
        first_slot = (held % 2) * (height + 1)
        for k in range(height):
            spread[first_slot + k] = across(own, base + k)
        spread[first_slot + height] = own
        corner = {
            (k, m): down(first_slot + m, k) for k in range(height) for m in range(k, height)
        }
        rows = [down(first_slot + height, k) for k in range(height)]
        nearby = range(held + 1, min(held + 5, blocks))
        moving = [rows] + [
            [across(state[other], base + k) for k in range(height)] for other in nearby
        ]
        block = packed = divided = jnp.zeros_like(own)
        for k in range(0, height, 2):
            first, cross, second = corner[k, k], corner[k, k + 1], corner[k + 1, k + 1]
            inverse = pl.reciprocal(first, approx=True)
            other_inverse = first * pl.reciprocal(first * second - cross * cross, approx=True)
            ratio = cross * inverse
            for several in moving:
                several[k + 1] = several[k + 1] - ratio * several[k]
            later = range(k + 2, height)
            upper = {m: corner[k, m] for m in later}
            lower = {m: corner[k + 1, m] - ratio * corner[k, m] for m in later}
            for m in later:
                for n in range(m, height):
                    corner[m, n] = (
                        corner[m, n]
                        - (upper[m] * upper[n]) * inverse
                        - (lower[m] * lower[n]) * other_inverse
                    )
                for several in moving:
                    several[m] = several[m] - (
                        (upper[m] * inverse) * several[k]
                        + (lower[m] * other_inverse) * several[k + 1]
                    )
            for which, other in enumerate(nearby):
                columns = moving[1 + which]
                state[other] = state[other] - (
                    columns[k] * (inverse * rows[k])
                    + columns[k + 1] * (other_inverse * rows[k + 1])
                )
            for m, pivot in ((k, inverse), (k + 1, other_inverse)):
                block = jnp.where(sub == m, rows[m] * (pivot * lax.rsqrt(pivot)), block)
                packed = jnp.where(sub == m, rows[m], packed)
                divided = jnp.where(sub == m, rows[m] * pivot, divided)
        done.append(block)
        if held + 5 < blocks:
            far = (held + 5) * height
            update = jnp.dot(
                packed.T[RANK + far :, :],
                divided,
                precision=highest,
                preferred_element_type=jnp.float32,
            )
            for other in range(held + 5, blocks):
                at = other * height - far
                state[other] = state[other] - update[at : at + height]
    return done


def scaled(joined):
    lane = lanes_of(joined.shape)
    row = lax.broadcasted_iota(jnp.int32, joined.shape, 0)
    diagonal = jnp.where(lane == row + RANK, joined, 0.0)
    down = lax.rsqrt(jnp.sum(diagonal, axis=1, keepdims=True))
    along = lax.rsqrt(jnp.sum(diagonal, axis=0, keepdims=True))
    return joined * down * jnp.where(lane < RANK, 1.0, along)


def whiten_kernel(factor, rows_each, rows_ref, gram_ref, out_ref, spread):
    packed = gram_ref[...]
    gram = jnp.concatenate([pltpu.roll(packed, RANK, 1), packed], axis=0)
    low = lanes_of((RANK, WIDE)) < RANK
    for example in range(rows_ref.shape[0]):
        joined = scaled(jnp.where(low, rows_ref[example], gram))
        done = eliminated([joined[at : at + 8] for at in range(0, RANK, 8)], spread)
        solved = (jnp.concatenate(done, axis=0) * factor).T
        out_ref[example] = solved[:rows_each, :]


def whiten(rows, gram, rows_each, factor):
    return pl.pallas_call(
        functools.partial(whiten_kernel, factor, rows_each),
        out_shape=jax.ShapeDtypeStruct((rows.shape[0], rows_each, RANK), jnp.float32),
        in_specs=[whole_vmem] * 2,
        out_specs=whole_vmem,
        scratch_shapes=[pltpu.VMEM((18, 8, WIDE), jnp.float32)],
        compiler_params=small,
        name="whiten",
    )(rows, gram)


def summed_over_groups(value):
    groups, model_shards = lax.axis_size("dp"), lax.axis_size("mp")
    place = lax.axis_index("mp")

    def over_groups(value):
        for level in range(groups.bit_length() - 1):
            pairs = [(source, source ^ 2**level) for source in range(groups)]
            value = value + lax.ppermute(value, "dp", pairs)
        return value

    value = lax.cond(place == model_shards - 1, over_groups, lambda value: value, value)
    result = value
    for away in range(1, model_shards):
        pairs = [(source, (source + away) % model_shards) for source in range(model_shards)]
        received = lax.ppermute(value, "mp", pairs)
        result = jnp.where(place == away - 1, received, result)
    return result


def shards(tokens_in, gate_pre, up_pre, hidden_grad, out_grad, proj_model, proj_hidden):
    model_shards = lax.axis_size("mp")
    rows_each = WIDE // model_shards
    local_examples = tokens_in.shape[0] // LEN
    place = lax.axis_index("mp").astype(jnp.int32).reshape(1)
    part = project(
        gate_pre, up_pre, hidden_grad, proj_hidden, tokens_in, out_grad, proj_model
    )
    parts = [part]
    for away in range(1, model_shards):
        pairs = [(source, (source + away) % model_shards) for source in range(model_shards)]
        parts.append(lax.ppermute(part, "mp", pairs))
    rows, gram = gram_of(place, parts, rows_each)
    gram = summed_over_groups(gram)
    factor = math.sqrt(local_examples * lax.axis_size("dp") * 2 * RANK)
    return whiten(rows, gram, rows_each, factor)


def solution(mesh):
    in_specs = (
        P("dp", "mp"),
        P("dp", "mp"),
        P("dp", "mp"),
        P("dp", "mp"),
        P("dp", "mp"),
        P("mp", None),
        P("mp", None),
    )
    out_specs = P("dp", "mp", None)
    return jax.shard_map(shards, mesh=mesh, in_specs=in_specs, out_specs=out_specs, check_vma=False)
```

```python
import functools
import math

import jax
import jax.numpy as jnp
from jax import lax
from jax.experimental import pallas as pl
from jax.experimental.pallas import tpu as pltpu
from jax.sharding import PartitionSpec as P

RANK = 64
LEN = 128
WIDE = 2 * RANK
EACH = 2048
HEAD = 512
MODEL_EACH = 1024
STEP = 256
AHEAD = 6

highest = lax.Precision.HIGHEST
whole_vmem = pl.BlockSpec(memory_space=pltpu.VMEM)
left_in_hbm = pl.BlockSpec(memory_space=pl.ANY)
small = pltpu.CompilerParams(vmem_limit_bytes=8 * 2**20)


def cuts_of(width):
    full = max((width - 1) // EACH, 0)
    head = width - full * EACH
    ends = [0, min(HEAD, head)]
    while ends[-1] < head:
        ends.append(min(ends[-1] + EACH // 2, head))
    return [(begin, end - begin) for begin, end in zip(ends, ends[1:])], full


def lanes_of(shape):
    return lax.broadcasted_iota(jnp.int32, shape, len(shape) - 1)


def paired(left, right, weights):
    low = lanes_of(weights.shape) < RANK
    none = jnp.zeros_like(weights)
    return jnp.dot(
        jnp.concatenate([left, right], axis=1),
        jnp.concatenate([jnp.where(low, weights, none), jnp.where(low, none, weights)], axis=0),
        preferred_element_type=jnp.float32,
    )


def project_kernel(gate, up, grad, proj_hidden, tokens, outer, proj_model, out, *rest):
    gate_v, up_v, grad_v, hidden_w, tokens_v, outer_v, model_w = rest[:7]
    hidden_sum, model_sum, sems, model_sems = rest[7:]
    rows = gate.shape[0]
    model_each = math.gcd(tokens.shape[1], MODEL_EACH)
    model_count = tokens.shape[1] // model_each
    head, full = cuts_of(gate.shape[1])
    head_width = gate.shape[1] - full * EACH

    def hidden_copies(slot, begin, size):
        cut = pl.ds(pl.multiple_of(begin, 128), size)
        pairs = [
            (gate.at[:, cut], gate_v.at[:, cut]),
            (grad.at[:, cut], grad_v.at[:, cut]),
            (up.at[:, cut], up_v.at[:, cut]),
            (proj_hidden.at[cut, :], hidden_w.at[cut, :]),
        ]
        return [
            pltpu.make_async_copy(source, target, sems.at[slot, which])
            for which, (source, target) in enumerate(pairs)
        ]

    def full_copies(piece):
        return hidden_copies(len(head) + piece, head_width + piece * EACH, EACH)

    def model_copies(piece):
        cut = pl.ds(pl.multiple_of(piece * model_each, model_each), model_each)
        pairs = [
            (tokens.at[:, cut], tokens_v.at[:, cut]),
            (outer.at[:, cut], outer_v.at[:, cut]),
            (proj_model.at[cut, :], model_w.at[cut, :]),
        ]
        return [
            pltpu.make_async_copy(source, target, model_sems.at[piece, which])
            for which, (source, target) in enumerate(pairs)
        ]

    def start(copies):
        for copy in copies:
            copy.start()

    def arrive(copies):
        for copy in copies:
            copy.wait()

    def start_models():
        for other in range(model_count):
            start(model_copies(other))

    def advance(begin, size):
        total = None
        for first in range(0, size, STEP):
            step = min(STEP, size - first)
            cut = pl.ds(pl.multiple_of(begin + first, 128), step)
            half = (gate_v[:, cut] * 0.5).astype(jnp.float32)
            act = half + half * jnp.tanh(half)
            up_grad = (grad_v[:, cut].astype(jnp.float32) * act).astype(jnp.bfloat16)
            hidden = (act * up_v[:, cut].astype(jnp.float32)).astype(jnp.bfloat16)
            part = paired(up_grad, hidden, hidden_w[cut, :])
            total = part if total is None else total + part
        hidden_sum[...] += total

    ahead = min(AHEAD, full)
    for slot, (begin, size) in enumerate(head):
        start(hidden_copies(slot, begin, size))
    for piece in range(ahead):
        start(full_copies(piece))
    if not full:
        start_models()
    hidden_sum[...] = jnp.zeros_like(hidden_sum)
    model_sum[...] = jnp.zeros_like(model_sum)
    for slot, (begin, size) in enumerate(head):
        arrive(hidden_copies(slot, begin, size))
        advance(begin, size)

    @pl.loop(0, full)
    def _(piece):
        arrive(full_copies(piece))

        @pl.when(piece + ahead < full)
        def _():
            start(full_copies(piece + ahead))

        @pl.when(piece + ahead == full)
        def _():
            start_models()

        advance(head_width + piece * EACH, EACH)

    @pl.loop(0, model_count)
    def _(piece):
        arrive(model_copies(piece))
        cut = pl.ds(pl.multiple_of(piece * model_each, model_each), model_each)
        model_sum[...] += paired(tokens_v[:, cut], outer_v[:, cut], model_w[cut, :])

    low = lanes_of((rows, WIDE)) < RANK
    turned = pltpu.roll(hidden_sum[...], RANK, 1)
    out[:, :WIDE] = jnp.where(low, model_sum[...], turned)
    out[:, WIDE:] = jnp.where(low, turned, model_sum[...])


def project(gate_pre, up_pre, hidden_grad, proj_hidden, tokens_in, out_grad, proj_model):
    rows, hidden_width = gate_pre.shape
    model_width = tokens_in.shape[1]
    head, full = cuts_of(hidden_width)
    hidden_slots = len(head) + full
    held = jnp.bfloat16
    return pl.pallas_call(
        project_kernel,
        out_shape=jax.ShapeDtypeStruct((rows, 2 * WIDE), jnp.float32),
        in_specs=[left_in_hbm] * 7,
        out_specs=whole_vmem,
        scratch_shapes=[
            pltpu.VMEM((rows, hidden_width), held),
            pltpu.VMEM((rows, hidden_width), held),
            pltpu.VMEM((rows, hidden_width), held),
            pltpu.VMEM((hidden_width, WIDE), held),
            pltpu.VMEM((rows, model_width), held),
            pltpu.VMEM((rows, model_width), held),
            pltpu.VMEM((model_width, WIDE), held),
            pltpu.VMEM((rows, WIDE), jnp.float32),
            pltpu.VMEM((rows, WIDE), jnp.float32),
            pltpu.SemaphoreType.DMA((hidden_slots, 4)),
            pltpu.SemaphoreType.DMA((model_width // math.gcd(model_width, MODEL_EACH), 3)),
        ],
        compiler_params=pltpu.CompilerParams(vmem_limit_bytes=56 * 10**6),
        name="project",
    )(gate_pre, up_pre, hidden_grad, proj_hidden, tokens_in, out_grad, proj_model)


def gram_kernel(rows_each, count, *refs):
    place, parts, (rows_ref, gram_ref) = refs[0], refs[1 : 1 + count], refs[1 + count :]
    total = parts[0][...]
    for part in parts[1:]:
        total += part[...]
    row = lax.broadcasted_iota(jnp.int32, (WIDE, WIDE), 0)
    lane = lanes_of((WIDE, WIDE))
    low = lanes_of((RANK, WIDE)) < RANK
    gram = jnp.zeros((RANK, WIDE), jnp.float32)
    shift = lax.rem(WIDE - place[0] * rows_each, WIDE)
    for example in range(total.shape[0] // LEN):
        mixed = []
        for at in (0, WIDE):
            sides = total[example * LEN : (example + 1) * LEN, at : at + WIDE]
            crossed = jnp.dot(
                sides.T, sides, precision=highest, preferred_element_type=jnp.float32
            )
            mixed.append(jnp.where((row < RANK) != (lane < RANK), crossed, 0.0))
        up_block, down_block = mixed[0][RANK:], mixed[1][RANK:]
        across = jnp.where(low, up_block, pltpu.roll(down_block, RANK, 1))
        rows_ref[example] = jnp.where(low, pltpu.roll(across, shift, 1), 0.0)
        gram += jnp.dot(
            jnp.concatenate([up_block, down_block], axis=1),
            jnp.concatenate(mixed, axis=0),
            precision=highest,
            preferred_element_type=jnp.float32,
        )
    top, bottom = gram[: RANK // 2], gram[RANK // 2 :]
    gram_ref[...] = jnp.where(
        lanes_of(top.shape) < RANK, pltpu.roll(top, RANK, 1), bottom
    )


def gram_of(place, parts, rows_each):
    examples = parts[0].shape[0] // LEN
    return pl.pallas_call(
        functools.partial(gram_kernel, rows_each, len(parts)),
        out_shape=[
            jax.ShapeDtypeStruct((examples, RANK, WIDE), jnp.float32),
            jax.ShapeDtypeStruct((RANK // 2, WIDE), jnp.float32),
        ],
        in_specs=[pl.BlockSpec(memory_space=pltpu.SMEM)] + [whole_vmem] * len(parts),
        out_specs=[whole_vmem] * 2,
        compiler_params=small,
        name="gram",
    )(place, *parts)


def eliminated(state, spread):
    height = 8
    blocks = len(state)
    state = list(state)
    sub = lax.broadcasted_iota(jnp.int32, state[0].shape, 0)

    def across(block, at):
        return jnp.broadcast_to(block[:, at : at + 1], block.shape)

    def down(which, at):
        return spread[which, pl.ds(at, height, stride=0), :]

    done = []
    for held in range(blocks):
        base = RANK + held * height
        own = state[held]
        first_slot = (held % 2) * (height + 1)
        for k in range(height):
            spread[first_slot + k, :height] = across(own, base + k)
        spread[first_slot + height, :height] = own
        corner = {
            (k, m): down(first_slot + m, k) for k in range(height) for m in range(k, height)
        }
        rows = [down(first_slot + height, k) for k in range(height)]
        nearby = range(held + 1, min(held + 4, blocks))
        moving = [rows] + [
            [across(state[other], base + k) for k in range(height)] for other in nearby
        ]
        block = packed = divided = jnp.zeros_like(own)
        for k in range(0, height, 2):
            first, cross, second = corner[k, k], corner[k, k + 1], corner[k + 1, k + 1]
            inverse = pl.reciprocal(first, approx=True)
            other_inverse = first * pl.reciprocal(first * second - cross * cross, approx=True)
            ratio = cross * inverse
            for several in moving:
                several[k + 1] = several[k + 1] - ratio * several[k]
            later = range(k + 2, height)
            upper = {m: corner[k, m] for m in later}
            lower = {m: corner[k + 1, m] - ratio * corner[k, m] for m in later}
            for m in later:
                for n in range(m, height):
                    corner[m, n] = (
                        corner[m, n]
                        - (upper[m] * upper[n]) * inverse
                        - (lower[m] * lower[n]) * other_inverse
                    )
                for several in moving:
                    several[m] = several[m] - (
                        (upper[m] * inverse) * several[k]
                        + (lower[m] * other_inverse) * several[k + 1]
                    )
            for which, other in enumerate(nearby):
                columns = moving[1 + which]
                state[other] = state[other] - (
                    columns[k] * (inverse * rows[k])
                    + columns[k + 1] * (other_inverse * rows[k + 1])
                )
            for m, pivot in ((k, inverse), (k + 1, other_inverse)):
                block = jnp.where(sub == m, rows[m] * (pivot * lax.rsqrt(pivot)), block)
                packed = jnp.where(sub == m, rows[m], packed)
                divided = jnp.where(sub == m, rows[m] * pivot, divided)
        done.append(block)
        if held + 4 < blocks:
            far = (held + 4) * height
            update = jnp.dot(
                packed.T[RANK + far :, :],
                divided,
                precision=highest,
                preferred_element_type=jnp.float32,
            )
            for other in range(held + 4, blocks):
                at = other * height - far
                state[other] = state[other] - update[at : at + height]
    return done


def scaled(joined):
    lane = lanes_of(joined.shape)
    row = lax.broadcasted_iota(jnp.int32, joined.shape, 0)
    diagonal = jnp.where(lane == row + RANK, joined, 0.0)
    down = lax.rsqrt(jnp.sum(diagonal, axis=1, keepdims=True))
    along = lax.rsqrt(jnp.sum(diagonal, axis=0, keepdims=True))
    return joined * down * jnp.where(lane < RANK, 1.0, along)


def whiten_kernel(factor, rows_each, rows_ref, gram_ref, out_ref, spread):
    packed = gram_ref[...]
    gram = jnp.concatenate([pltpu.roll(packed, RANK, 1), packed], axis=0)
    low = lanes_of((RANK, WIDE)) < RANK
    for example in range(rows_ref.shape[0]):
        joined = scaled(jnp.where(low, rows_ref[example], gram))
        done = eliminated([joined[at : at + 8] for at in range(0, RANK, 8)], spread)
        solved = (jnp.concatenate(done, axis=0) * factor).T
        out_ref[example] = solved[:rows_each, :]


def whiten(rows, gram, rows_each, factor):
    return pl.pallas_call(
        functools.partial(whiten_kernel, factor, rows_each),
        out_shape=jax.ShapeDtypeStruct((rows.shape[0], rows_each, RANK), jnp.float32),
        in_specs=[whole_vmem] * 2,
        out_specs=whole_vmem,
        scratch_shapes=[pltpu.VMEM((18, 16, WIDE), jnp.float32)],
        compiler_params=small,
        name="whiten",
    )(rows, gram)


def summed_over_groups(value):
    groups, model_shards = lax.axis_size("dp"), lax.axis_size("mp")
    place = lax.axis_index("mp")

    def over_groups(value):
        for level in range(groups.bit_length() - 1):
            pairs = [(source, source ^ 2**level) for source in range(groups)]
            value = value + lax.ppermute(value, "dp", pairs)
        return value

    value = lax.cond(place == model_shards - 1, over_groups, lambda value: value, value)
    result = value
    for away in range(1, model_shards):
        pairs = [(source, (source + away) % model_shards) for source in range(model_shards)]
        received = lax.ppermute(value, "mp", pairs)
        result = jnp.where(place == away - 1, received, result)
    return result


def shards(tokens_in, gate_pre, up_pre, hidden_grad, out_grad, proj_model, proj_hidden):
    model_shards = lax.axis_size("mp")
    rows_each = WIDE // model_shards
    local_examples = tokens_in.shape[0] // LEN
    place = lax.axis_index("mp").astype(jnp.int32).reshape(1)
    part = project(
        gate_pre, up_pre, hidden_grad, proj_hidden, tokens_in, out_grad, proj_model
    )
    parts = [part]
    for away in range(1, model_shards):
        pairs = [(source, (source + away) % model_shards) for source in range(model_shards)]
        parts.append(lax.ppermute(part, "mp", pairs))
    rows, gram = gram_of(place, parts, rows_each)
    gram = summed_over_groups(gram)
    factor = math.sqrt(local_examples * lax.axis_size("dp") * 2 * RANK)
    return whiten(rows, gram, rows_each, factor)


def solution(mesh):
    in_specs = (
        P("dp", "mp"),
        P("dp", "mp"),
        P("dp", "mp"),
        P("dp", "mp"),
        P("dp", "mp"),
        P("mp", None),
        P("mp", None),
    )
    out_specs = P("dp", "mp", None)
    return jax.shard_map(shards, mesh=mesh, in_specs=in_specs, out_specs=out_specs, check_vma=False)
```
